32 devices in a mesh: dp: 2 (over x), head: 4 (over y, core), blk: 4 (over z).
Axes of the slice: x: 2, y: 2, z: 4, core: 2. Of those that a mesh axis runs over, the one named last changes fastest.
Arguments:
- tokens: bfloat16 [4, 2048, 768], P('dp', ('blk', 'head')), may hold values from -6 to 6
- segments: int32 [4, 2048], P('dp', ('blk', 'head')), may hold values from 0 to 255, as said below
- qkv_weight: bfloat16 [768, 2304], P(('dp', 'head', 'blk')), may hold values from -0.21875 to 0.21875
- qv_bias: bfloat16 [1536], P(('dp', 'head', 'blk')), may hold values from -3 to 3
- out_weight: bfloat16 [768, 768], P(('dp', 'head', 'blk')), may hold values from -9 to 9
- out_bias: bfloat16 [768], P(('dp', 'head', 'blk')), may hold values from -3 to 3
- attn_gain: bfloat16 [768], P(('dp', 'head', 'blk')), may hold values from 0.5 to 1.5
- attn_shift: bfloat16 [768], P(('dp', 'head', 'blk')), may hold values from -3 to 3
- up_weight: bfloat16 [768, 3072], P(('dp', 'head', 'blk')), may hold values from -0.21875 to 0.21875
- up_bias: bfloat16 [3072], P(('dp', 'head', 'blk')), may hold values from -3 to 3
- down_weight: bfloat16 [3072, 768], P(('dp', 'head', 'blk')), may hold values from -0.109375 to 0.109375
- down_bias: bfloat16 [768], P(('dp', 'head', 'blk')), may hold values from -3 to 3
- ffn_gain: bfloat16 [768], P(('dp', 'head', 'blk')), may hold values from 0.5 to 1.5
- ffn_shift: bfloat16 [768], P(('dp', 'head', 'blk')), may hold values from -3 to 3
- cotangent: bfloat16 [4, 2048, 768], P('dp', ('blk', 'head')), may hold values from -6 to 6
Outputs:
- layer_out: bfloat16 [4, 2048, 768], P('dp', ('blk', 'head'))
- grad_tokens: float32 [4, 2048, 768], P('dp', ('blk', 'head'))
- grad_qkv_weight: float32 [768, 2304], P(('dp', 'head', 'blk'))
- grad_qv_bias: float32 [1536], P(('dp', 'head', 'blk'))
- grad_out_weight: float32 [768, 768], P(('dp', 'head', 'blk'))
- grad_out_bias: float32 [768], P(('dp', 'head', 'blk'))
- grad_attn_gain: float32 [768], P(('dp', 'head', 'blk'))
- grad_attn_shift: float32 [768], P(('dp', 'head', 'blk'))
- grad_up_weight: float32 [768, 3072], P(('dp', 'head', 'blk'))
- grad_up_bias: float32 [3072], P(('dp', 'head', 'blk'))
- grad_down_weight: float32 [3072, 768], P(('dp', 'head', 'blk'))
- grad_down_bias: float32 [768], P(('dp', 'head', 'blk'))
- grad_ffn_gain: float32 [768], P(('dp', 'head', 'blk'))
- grad_ffn_shift: float32 [768], P(('dp', 'head', 'blk'))
The draws below stay inside these ranges and needn't reach their ends.
Inputs may be any that keep to these rules, and one draw needn't show every extreme that they name: `segments`: along each row segment numbers never fall; each row ends in one or more padding tokens with segment number 256 - 1. Of the 2 rows of each index of dp, one holds a document that begins within its first 512 positions and ends within its last 512, with documents of under 512 tokens before and after it; the others hold documents of 200 to 2000 tokens, the last one before the padding possibly shorter.
All inputs are finite; a program needn't handle non-finite values.
Results may differ from the reference program's by a relative error of at most 0.017.
Values may be sent and summed in bfloat16 or wider, within the bound.
A program may use at most 192 MiB of HBM per device.

```python
import math
import jax
import jax.numpy as jnp
from jax import lax

D = 768
FF = 3072
HEADS = 12
HDIM = 64
SEQS = 2
NSEG = 256
DOC_MIN = 200
DOC_MAX = 2000
BLOCK = 512
LEN = 2048
ROWS = 4


def draw_segments(key, part):
    pick_key = jax.random.fold_in(key, 7919)
    spanning = jax.random.randint(pick_key, (ROWS // SEQS,), 0, SEQS)
    count_docs = LEN // DOC_MIN + 1
    places = jnp.arange(LEN)

    def one_row(row_index):
        row_key = jax.random.fold_in(key, row_index)
        split_keys = jax.random.split(row_key, 5)
        padding = 1 + jax.random.randint(split_keys[2], (), 0, BLOCK // 4)
        head_cuts = jax.random.randint(split_keys[0], (3,), 1, BLOCK)
        finish = LEN - BLOCK + jax.random.randint(split_keys[1], (), 1, BLOCK // 2)
        tail_cuts = jax.random.randint(split_keys[3], (2,), finish, LEN - padding)
        long_number = jnp.sum((places[:, None] >= head_cuts[None, :]).astype(jnp.int32), axis=1)
        long_number = long_number + (places >= finish).astype(jnp.int32)
        long_number = long_number + jnp.sum((places[:, None] >= tail_cuts[None, :]).astype(jnp.int32), axis=1)
        lengths = jax.random.randint(split_keys[4], (count_docs,), DOC_MIN, DOC_MAX + 1)
        ends = jnp.cumsum(lengths)
        short_number = jnp.sum((places[:, None] >= ends[None, :]).astype(jnp.int32), axis=1)
        is_spanning = spanning[row_index // SEQS] == row_index % SEQS
        number = jnp.where(is_spanning, long_number, short_number)
        return jnp.where(places >= LEN - padding, NSEG - 1, number).astype(jnp.int32)
    return jax.vmap(one_row)(jnp.arange(ROWS))


def shard_levels(rng, extent, cuts, least, top_value):
    level = 1.0
    for axis_at, shards_of in cuts:
        heights = jax.random.uniform(jax.random.fold_in(jax.random.fold_in(rng, 6), axis_at), (shards_of,), jnp.float32, least / len(cuts), top_value / len(cuts))
        level = level * jnp.repeat(jnp.exp(heights), extent[axis_at] // shards_of).reshape((-1,) + (1,) * (len(extent) - 1 - axis_at))
    return level


def normal_values(rng, shape, scale, reach, pieces=(), kind=jnp.bfloat16):
    level = shard_levels(rng, shape, pieces, -0.22, 0.18) if pieces else 1.0
    array = jax.random.normal(rng, shape, jnp.float32) * scale * level
    return jnp.minimum(jnp.maximum(array, -reach), reach).astype(kind)


def setup_inputs(seed: int = 0) -> dict:
    arg_keys = jax.random.split(jax.random.key(seed), 16)
    tokens = normal_values(arg_keys[0], (ROWS, LEN, D), 1.0, 6.0, ((0, 2), (1, 16)))
    segments = draw_segments(jax.random.fold_in(arg_keys[15], 71), 0)
    qkv_weight = normal_values(arg_keys[2], (D, 3 * D), D ** -0.5, 0.21875, ((0, 32),))
    qv_bias = normal_values(arg_keys[3], (2 * D,), 0.5, 3.0, ((0, 32),))
    out_weight = normal_values(arg_keys[4], (D, D), 1.5, 9.0, ((0, 32),))
    out_bias = normal_values(arg_keys[5], (D,), 0.5, 3.0, ((0, 32),))
    attn_gain = jnp.clip(1.0 + 0.1 * jax.random.normal(arg_keys[6], (D,), jnp.float32), 0.5, 1.5).astype(jnp.bfloat16)
    attn_shift = normal_values(arg_keys[7], (D,), 0.5, 3.0, ((0, 32),))
    up_weight = normal_values(arg_keys[8], (D, FF), D ** -0.5, 0.21875, ((0, 32),))
    up_bias = normal_values(arg_keys[9], (FF,), 0.5, 3.0, ((0, 32),))
    down_weight = normal_values(arg_keys[10], (FF, D), FF ** -0.5, 0.109375, ((0, 32),))
    down_bias = normal_values(arg_keys[11], (D,), 0.5, 3.0, ((0, 32),))
    ffn_gain = jnp.clip(1.0 + 0.1 * jax.random.normal(arg_keys[12], (D,), jnp.float32), 0.5, 1.5).astype(jnp.bfloat16)
    ffn_shift = normal_values(arg_keys[13], (D,), 0.5, 3.0, ((0, 32),))
    cotangent = normal_values(arg_keys[14], (ROWS, LEN, D), 1.0, 6.0, ((0, 2), (1, 16)))
    return {"tokens": tokens, "segments": segments, "qkv_weight": qkv_weight, "qv_bias": qv_bias, "out_weight": out_weight, "out_bias": out_bias, "attn_gain": attn_gain, "attn_shift": attn_shift, "up_weight": up_weight, "up_bias": up_bias, "down_weight": down_weight, "down_bias": down_bias, "ffn_gain": ffn_gain, "ffn_shift": ffn_shift, "cotangent": cotangent}


EPS = 1e-12
MASKED = -1e+30
SCALE = 0.125
HIGH = lax.Precision.HIGHEST

@jax.custom_vjp
def low(v):
    return lax.optimization_barrier(v.astype(jnp.bfloat16)).astype(jnp.float32)

@jax.custom_vjp
def low_back(v):
    return v

def low_keep(v):
    return (low(v), None)

def low_pass(kept, grad):
    return (grad,)

def back_keep(v):
    return (v, None)

def back_low(kept, grad):
    return (low(grad),)
low.defvjp(low_keep, low_pass)
low_back.defvjp(back_keep, back_low)

def layer_norm(values_in, gain, shift):
    mean_val = lax.optimization_barrier(jnp.mean(values_in, axis=-1, keepdims=True))
    centred = values_in - mean_val
    spread = lax.optimization_barrier(jnp.mean(centred * centred, axis=-1, keepdims=True))
    return centred * lax.rsqrt(spread + EPS) * gain + shift

def attend_row(row_inputs):
    queries, keys_row, values_row, segment = row_inputs
    total_len = segment.shape[0]
    step_rows = math.gcd(total_len, 512)
    places = jnp.arange(total_len)

    def one_block(block_inputs):
        query_block, seg_block, place_block = block_inputs
        scores = low_back(jnp.einsum('qhd,khd->hqk', query_block, keys_row, precision=HIGH) * SCALE)
        same_doc = seg_block[:, None] == segment[None, :]
        usable = (seg_block[:, None] != NSEG - 1) | (place_block[:, None] == places[None, :])
        allowed = same_doc & usable
        masked = jnp.where(allowed[None], scores, MASKED)
        top_score = lax.optimization_barrier(jnp.max(masked, axis=-1, keepdims=True))
        weights = jnp.where(allowed[None], jnp.exp(masked - top_score), 0.0)
        probs = low(weights / lax.optimization_barrier(jnp.sum(weights, axis=-1, keepdims=True)))
        return jnp.einsum('hqk,khd->qhd', probs, values_row, precision=HIGH)
    count_blocks = total_len // step_rows
    result = lax.map(jax.checkpoint(one_block), (queries.reshape(count_blocks, step_rows, HEADS, HDIM), segment.reshape(count_blocks, step_rows), places.reshape(count_blocks, step_rows)))
    return result.reshape(total_len, HEADS * HDIM)

def layer(tokens, segments, qkv_weight, qv_bias, out_weight, out_bias, attn_gain, attn_shift, up_weight, up_bias, down_weight, down_bias, ffn_gain, ffn_shift):
    row_count = tokens.shape[0]
    mixed = jnp.einsum('rld,de->rle', tokens, qkv_weight, precision=HIGH)
    queries = low_back(low(mixed[..., :D] + qv_bias[:D]))
    keys_all = low_back(low(mixed[..., D:2 * D]))
    values_all = low_back(low(mixed[..., 2 * D:] + qv_bias[D:]))
    head_shape = (row_count, LEN, HEADS, HDIM)
    context = lax.map(attend_row, (queries.reshape(head_shape), keys_all.reshape(head_shape), values_all.reshape(head_shape), segments))
    context = low_back(low(context))
    attended = low_back(jnp.einsum('rld,de->rle', context, out_weight, precision=HIGH) + out_bias)
    hidden = layer_norm(tokens + attended, attn_gain, attn_shift)
    inner = low_back(jnp.einsum('rld,df->rlf', low(hidden), up_weight, precision=HIGH) + up_bias)
    active = low(jax.nn.gelu(inner, approximate=False))
    branch = low_back(jnp.einsum('rlf,fd->rld', active, down_weight, precision=HIGH) + down_bias)
    return layer_norm(hidden + branch, ffn_gain, ffn_shift)

def reference(tokens, segments, qkv_weight, qv_bias, out_weight, out_bias, attn_gain, attn_shift, up_weight, up_bias, down_weight, down_bias, ffn_gain, ffn_shift, cotangent):
    inputs = tuple((item.astype(jnp.float32) for item in (tokens, qkv_weight, qv_bias, out_weight, out_bias, attn_gain, attn_shift, up_weight, up_bias, down_weight, down_bias, ffn_gain, ffn_shift)))

    def closed(tokens_in, *params):
        return layer(tokens_in, segments, *params)
    output, pull_back = jax.vjp(closed, *inputs)
    grads = pull_back(cotangent.astype(jnp.float32))
    return (output.astype(jnp.bfloat16), grads[0], grads[1], grads[2], grads[3], grads[4], grads[5], grads[6], grads[7], grads[8], grads[9], grads[10], grads[11], grads[12])
```

```python
import math

import jax
import jax.numpy as jnp
from jax import lax
from jax.experimental import pallas as pl
from jax.experimental.pallas import tpu as pltpu
from jax.sharding import PartitionSpec as P

HEADS = 12
HDIM = 64
NSEG = 256


EPS = 1e-12
MASKED = -1e30
SCALE = 0.125


def norm_forward(values_in, gain, shift):
    mean_val = jnp.mean(values_in, axis=-1, keepdims=True)
    centred = values_in - mean_val
    inv_std = lax.rsqrt(jnp.mean(centred * centred, axis=-1, keepdims=True) + EPS)
    normed = centred * inv_std
    return (normed * gain + shift, normed, inv_std)


def norm_backward(grad_in, normed, inv_std, gain):
    scaled = grad_in * gain
    inner_term = (
        scaled
        - jnp.mean(scaled, axis=-1, keepdims=True)
        - normed * jnp.mean(scaled * normed, axis=-1, keepdims=True)
    )
    return (inner_term * inv_std, jnp.sum(grad_in * normed, axis=0), jnp.sum(grad_in, axis=0))


def exact_gelu(values_in):
    return jax.nn.gelu(values_in, approximate=False)


def stretch_scores(queries, key_part, query_seg, key_seg, query_place, key_place):
    scores = (
        jnp.einsum("sqhd,skhd->shqk", queries, key_part, preferred_element_type=jnp.float32) * SCALE
    )
    same_doc = query_seg[:, None, :, None] == key_seg[:, None, None, :]
    own_place = query_place[:, None] == key_place[None, :]
    usable = (query_seg[:, None, :, None] != NSEG - 1) | own_place[None, None]
    return (scores, same_doc & usable)


def slice_keys(key_piece, value_piece, seg_piece, offset, step_rows):
    key_part = lax.dynamic_slice_in_dim(key_piece, offset, step_rows, 1)
    value_part = lax.dynamic_slice_in_dim(value_piece, offset, step_rows, 1)
    seg_part = lax.dynamic_slice_in_dim(seg_piece, offset, step_rows, 1)
    return (key_part, value_part, seg_part)


def part_grads(
    queries,
    grad_ctx,
    log_total,
    row_delta,
    query_seg,
    query_place,
    key_part,
    value_part,
    key_seg,
    key_place,
):
    scores, allowed = stretch_scores(queries, key_part, query_seg, key_seg, query_place, key_place)
    probs = jnp.where(allowed, jnp.exp(scores - log_total[..., None]), 0.0)
    grad_probs = jnp.einsum(
        "sqhd,skhd->shqk", grad_ctx, value_part, preferred_element_type=jnp.float32
    )
    grad_scores = (probs * (grad_probs - row_delta[..., None])).astype(jnp.bfloat16)
    grad_query = (
        jnp.einsum("shqk,skhd->sqhd", grad_scores, key_part, preferred_element_type=jnp.float32)
        * SCALE
    )
    grad_key = (
        jnp.einsum("shqk,sqhd->skhd", grad_scores, queries, preferred_element_type=jnp.float32)
        * SCALE
    )
    grad_value = jnp.einsum(
        "shqk,sqhd->skhd", probs.astype(jnp.bfloat16), grad_ctx, preferred_element_type=jnp.float32
    )
    return (grad_query, grad_key, grad_value)


def general_body(
    tokens,
    segments,
    qkv_weight,
    qv_bias,
    out_weight,
    out_bias,
    attn_gain,
    attn_shift,
    up_weight,
    up_bias,
    down_weight,
    down_bias,
    ffn_gain,
    ffn_shift,
    cotangent,
):
    seq_count, local_rows, model_width = tokens.shape
    group_count = lax.axis_size("head")
    group_width = model_width // group_count
    heads_here = HEADS // group_count
    block_rows = local_rows * group_count
    key_rows = block_rows * lax.axis_size("blk")
    token_count = seq_count * local_rows
    gathered = (
        lax.all_gather(qkv_weight, ("dp", "head", "blk"), axis=0, tiled=True),
        lax.all_gather(qv_bias, ("dp", "head", "blk"), axis=0, tiled=True),
        lax.all_gather(out_weight, ("dp", "head", "blk"), axis=0, tiled=True),
        lax.all_gather(out_bias, ("dp", "head", "blk"), axis=0, tiled=True),
        lax.all_gather(attn_gain, ("dp", "head", "blk"), axis=0, tiled=True),
        lax.all_gather(attn_shift, ("dp", "head", "blk"), axis=0, tiled=True),
        lax.all_gather(up_weight, ("dp", "head", "blk"), axis=0, tiled=True),
        lax.all_gather(up_bias, ("dp", "head", "blk"), axis=0, tiled=True),
        lax.all_gather(down_weight, ("dp", "head", "blk"), axis=0, tiled=True),
        lax.all_gather(down_bias, ("dp", "head", "blk"), axis=0, tiled=True),
        lax.all_gather(ffn_gain, ("dp", "head", "blk"), axis=0, tiled=True),
        lax.all_gather(ffn_shift, ("dp", "head", "blk"), axis=0, tiled=True),
    )
    (
        whole_qkv,
        whole_qv,
        whole_out,
        whole_out_bias,
        whole_attn_gain,
        whole_attn_shift,
        whole_up,
        whole_up_bias,
        whole_down,
        whole_down_bias,
        whole_ffn_gain,
        whole_ffn_shift,
    ) = gathered
    attn_scale = whole_attn_gain.astype(jnp.float32)
    ffn_scale = whole_ffn_gain.astype(jnp.float32)
    flat_tokens = tokens.reshape(token_count, model_width)
    mixed = jnp.dot(flat_tokens, whole_qkv, preferred_element_type=jnp.float32)
    bias_row = jnp.concatenate(
        [whole_qv[:model_width], jnp.zeros((model_width,), jnp.bfloat16), whole_qv[model_width:]]
    ).astype(jnp.float32)
    mixed_low = (mixed + bias_row).astype(jnp.bfloat16)
    grouped = (
        mixed_low.reshape(seq_count, local_rows, 3, group_count, group_width)
        .transpose(0, 1, 3, 2, 4)
        .reshape(seq_count, local_rows, group_count, 3 * group_width)
    )
    seg_copies = jnp.broadcast_to(
        segments.astype(jnp.bfloat16)[:, :, None, None], (seq_count, local_rows, group_count, 1)
    )
    arrived, seg_arrived = (
        lax.all_to_all(grouped, "head", split_axis=2, concat_axis=1, tiled=True),
        lax.all_to_all(seg_copies, "head", split_axis=2, concat_axis=1, tiled=True),
    )
    arrived = arrived.reshape(seq_count, block_rows, 3, heads_here, HDIM)
    queries = arrived[:, :, 0]
    keys_here = arrived[:, :, 1]
    values_here = arrived[:, :, 2]
    query_seg = seg_arrived.reshape(seq_count, block_rows)
    query_place = lax.axis_index("blk") * block_rows + jnp.arange(block_rows)
    row_shape = (seq_count, heads_here, block_rows)
    start_state = (
        jnp.full(row_shape, MASKED, jnp.float32),
        jnp.zeros(row_shape, jnp.float32),
        jnp.zeros(row_shape + (HDIM,), jnp.float32),
    )
    key_piece = lax.all_gather(keys_here, "blk", axis=1, tiled=True)
    value_piece = lax.all_gather(values_here, "blk", axis=1, tiled=True)
    seg_piece = lax.all_gather(query_seg, "blk", axis=1, tiled=True)
    piece_rows = key_piece.shape[1]
    step_rows = math.gcd(piece_rows, 512)

    def attend_one_step(state_in, step_index):
        offset = step_index * step_rows
        key_part, value_part, key_seg = slice_keys(
            key_piece, value_piece, seg_piece, offset, step_rows
        )
        key_place = offset + jnp.arange(step_rows)
        best, total, accum = state_in
        scores, allowed = stretch_scores(
            queries, key_part, query_seg, key_seg, query_place, key_place
        )
        new_best = jnp.maximum(best, jnp.max(jnp.where(allowed, scores, MASKED), axis=-1))
        weights = jnp.where(allowed, jnp.exp(scores - new_best[..., None]), 0.0)
        factor = jnp.exp(best - new_best)
        total = total * factor + jnp.sum(weights, axis=-1)
        accum = accum * factor[..., None] + jnp.einsum(
            "shqk,skhd->shqd",
            weights.astype(jnp.bfloat16),
            value_part,
            preferred_element_type=jnp.float32,
        )
        return ((new_best, total, accum), None)

    result, unused = lax.scan(attend_one_step, start_state, jnp.arange(piece_rows // step_rows))
    best, total, accum = result
    context = accum / total[..., None]
    log_total = best + jnp.log(total)
    context_low = (
        context.astype(jnp.bfloat16)
        .transpose(0, 2, 1, 3)
        .reshape(seq_count, block_rows, 1, group_width)
    )
    returned_ctx = lax.all_to_all(context_low, "head", split_axis=1, concat_axis=2, tiled=True)
    ctx_tokens = returned_ctx.reshape(token_count, model_width)
    attended = jnp.dot(
        ctx_tokens, whole_out, preferred_element_type=jnp.float32
    ) + whole_out_bias.astype(jnp.float32)
    first_sum = flat_tokens.astype(jnp.float32) + attended
    hidden, normed_one, inv_one = norm_forward(
        first_sum, attn_scale, whole_attn_shift.astype(jnp.float32)
    )
    hidden_low = hidden.astype(jnp.bfloat16)
    inner = jnp.dot(
        hidden_low, whole_up, preferred_element_type=jnp.float32
    ) + whole_up_bias.astype(jnp.float32)
    active, gelu_pull = jax.vjp(exact_gelu, inner)
    active_low = active.astype(jnp.bfloat16)
    branch = jnp.dot(
        active_low, whole_down, preferred_element_type=jnp.float32
    ) + whole_down_bias.astype(jnp.float32)
    final, normed_two, inv_two = norm_forward(
        hidden + branch, ffn_scale, whole_ffn_shift.astype(jnp.float32)
    )
    layer_out = final.astype(jnp.bfloat16).reshape(seq_count, local_rows, model_width)
    grad_final = cotangent.reshape(token_count, model_width).astype(jnp.float32)
    grad_second, grad_ffn_gain, grad_ffn_shift = norm_backward(
        grad_final, normed_two, inv_two, ffn_scale
    )
    grad_branch = grad_second.astype(jnp.bfloat16)
    grad_down = jnp.dot(active_low.T, grad_branch, preferred_element_type=jnp.float32)
    grad_down_bias = jnp.sum(grad_branch.astype(jnp.float32), axis=0)
    grad_active = jnp.dot(grad_branch, whole_down.T, preferred_element_type=jnp.float32)
    grad_inner = gelu_pull(grad_active)[0].astype(jnp.bfloat16)
    grad_up = jnp.dot(hidden_low.T, grad_inner, preferred_element_type=jnp.float32)
    grad_up_bias = jnp.sum(grad_inner.astype(jnp.float32), axis=0)
    grad_hidden = grad_second + jnp.dot(grad_inner, whole_up.T, preferred_element_type=jnp.float32)
    grad_first, grad_attn_gain, grad_attn_shift = norm_backward(
        grad_hidden, normed_one, inv_one, attn_scale
    )
    grad_attended = grad_first.astype(jnp.bfloat16)
    grad_out = jnp.dot(ctx_tokens.T, grad_attended, preferred_element_type=jnp.float32)
    grad_out_bias = jnp.sum(grad_attended.astype(jnp.float32), axis=0)
    grad_context = jnp.dot(grad_attended, whole_out.T, preferred_element_type=jnp.float32).astype(
        jnp.bfloat16
    )
    grad_sent = lax.all_to_all(
        grad_context.reshape(seq_count, local_rows, group_count, group_width),
        "head",
        split_axis=2,
        concat_axis=1,
        tiled=True,
    )
    grad_ctx = grad_sent.reshape(seq_count, block_rows, heads_here, HDIM)
    row_delta = jnp.einsum("sqhd,shqd->shq", grad_ctx.astype(jnp.float32), context)
    query_zero = jnp.zeros((seq_count, block_rows, heads_here, HDIM), jnp.float32)
    zero_keys = jnp.zeros((seq_count, key_rows, heads_here, HDIM), jnp.float32)
    gather_key_piece = lax.all_gather(keys_here, "blk", axis=1, tiled=True)
    gather_value_piece = lax.all_gather(values_here, "blk", axis=1, tiled=True)
    gather_seg_piece = lax.all_gather(query_seg, "blk", axis=1, tiled=True)
    piece_rows = gather_key_piece.shape[1]
    gather_step_rows = math.gcd(piece_rows, 512)

    def gather_one_step(state_in, step_index):
        offset = step_index * gather_step_rows
        key_part, value_part, key_seg = slice_keys(
            gather_key_piece, gather_value_piece, gather_seg_piece, offset, gather_step_rows
        )
        key_place = offset + jnp.arange(gather_step_rows)
        grad_q, grad_k, grad_v = state_in
        part_q, part_k, part_v = part_grads(
            queries,
            grad_ctx,
            log_total,
            row_delta,
            query_seg,
            query_place,
            key_part,
            value_part,
            key_seg,
            key_place,
        )
        grad_k = lax.dynamic_update_slice_in_dim(
            grad_k,
            lax.dynamic_slice_in_dim(grad_k, offset, gather_step_rows, 1) + part_k,
            offset,
            1,
        )
        grad_v = lax.dynamic_update_slice_in_dim(
            grad_v,
            lax.dynamic_slice_in_dim(grad_v, offset, gather_step_rows, 1) + part_v,
            offset,
            1,
        )
        return ((grad_q + part_q, grad_k, grad_v), None)

    result, unused = lax.scan(
        gather_one_step,
        (query_zero, zero_keys, zero_keys),
        jnp.arange(piece_rows // gather_step_rows),
    )
    grad_q, all_keys, all_values = result
    grad_k, grad_v = (
        lax.psum_scatter(
            all_keys.astype(jnp.bfloat16), "blk", scatter_dimension=1, tiled=True
        ).astype(jnp.float32),
        lax.psum_scatter(
            all_values.astype(jnp.bfloat16), "blk", scatter_dimension=1, tiled=True
        ).astype(jnp.float32),
    )
    grad_low = jnp.concatenate(
        [
            grad_q.astype(jnp.bfloat16).reshape(seq_count, block_rows, 1, group_width),
            grad_k.astype(jnp.bfloat16).reshape(seq_count, block_rows, 1, group_width),
            grad_v.astype(jnp.bfloat16).reshape(seq_count, block_rows, 1, group_width),
        ],
        axis=3,
    )
    back_tokens = lax.all_to_all(grad_low, "head", split_axis=1, concat_axis=2, tiled=True)
    grad_mixed = (
        back_tokens.reshape(seq_count, local_rows, group_count, 3, group_width)
        .transpose(0, 1, 3, 2, 4)
        .reshape(token_count, 3 * model_width)
    )
    grad_qkv = jnp.dot(flat_tokens.T, grad_mixed, preferred_element_type=jnp.float32)
    column_sums = jnp.sum(grad_mixed.astype(jnp.float32), axis=0)
    grad_qv = jnp.concatenate([column_sums[:model_width], column_sums[2 * model_width :]])
    grad_tokens = grad_first + jnp.dot(grad_mixed, whole_qkv.T, preferred_element_type=jnp.float32)
    summed = (
        lax.psum_scatter(grad_qkv, ("dp", "head", "blk"), scatter_dimension=0, tiled=True),
        lax.psum_scatter(grad_qv, ("dp", "head", "blk"), scatter_dimension=0, tiled=True),
        lax.psum_scatter(grad_out, ("dp", "head", "blk"), scatter_dimension=0, tiled=True),
        lax.psum_scatter(grad_out_bias, ("dp", "head", "blk"), scatter_dimension=0, tiled=True),
        lax.psum_scatter(grad_attn_gain, ("dp", "head", "blk"), scatter_dimension=0, tiled=True),
        lax.psum_scatter(grad_attn_shift, ("dp", "head", "blk"), scatter_dimension=0, tiled=True),
        lax.psum_scatter(grad_up, ("dp", "head", "blk"), scatter_dimension=0, tiled=True),
        lax.psum_scatter(grad_up_bias, ("dp", "head", "blk"), scatter_dimension=0, tiled=True),
        lax.psum_scatter(grad_down, ("dp", "head", "blk"), scatter_dimension=0, tiled=True),
        lax.psum_scatter(grad_down_bias, ("dp", "head", "blk"), scatter_dimension=0, tiled=True),
        lax.psum_scatter(grad_ffn_gain, ("dp", "head", "blk"), scatter_dimension=0, tiled=True),
        lax.psum_scatter(grad_ffn_shift, ("dp", "head", "blk"), scatter_dimension=0, tiled=True),
    )
    return (
        layer_out,
        grad_tokens.reshape(seq_count, local_rows, model_width),
        summed[0],
        summed[1],
        summed[2],
        summed[3],
        summed[4],
        summed[5],
        summed[6],
        summed[7],
        summed[8],
        summed[9],
        summed[10],
        summed[11],
    )


MESH = pl.DeviceIdType.MESH
ANY = pl.ANY
VMEM_LIMIT = 60 * 1024 * 1024


def remote(src, dst, send_sem, recv_sem, device):
    return pltpu.make_async_remote_copy(
        src_ref=src,
        dst_ref=dst,
        send_sem=send_sem,
        recv_sem=recv_sem,
        device_id=device,
        device_id_type=MESH,
    )


def wait_for(ref, sem):
    pltpu.make_async_copy(ref, ref, sem).wait()


def place():
    x, h, z = lax.axis_index("dp"), lax.axis_index("head"), lax.axis_index("blk")
    return x, lax.div(h, 2), lax.rem(h, 2), h, z


def greet(peers):
    barrier = pltpu.get_barrier_semaphore()
    for peer in peers:
        pl.semaphore_signal(barrier, inc=1, device_id=peer, device_id_type=MESH)
    pl.semaphore_wait(barrier, len(peers))


def peers_of(x, h, c, z):
    around = [(x, h, lax.rem(z + k, 4)) for k in (1, 2, 3)]
    other = lax.rem(h + 2, 4)
    beside = z + 1 - 2 * lax.rem(z, 2)
    return around + [(1 - x, h, z), (x, other, z), (x, other, beside), (x, h + 1 - 2 * c, z)]


def nt(left, right):
    return lax.dot_general(left, right, (((1,), (1,)), ((), ())), preferred_element_type=jnp.float32)


def tn(left, right):
    return lax.dot_general(left, right, (((0,), (0,)), ((), ())), preferred_element_type=jnp.float32)


def nn(left, right):
    return jnp.dot(left, right, preferred_element_type=jnp.float32)


def add_norm(values_in):
    mean_val = jnp.mean(values_in, axis=-1, keepdims=True)
    centred = values_in - mean_val
    inv_std = lax.rsqrt(jnp.mean(centred * centred, axis=-1, keepdims=True) + EPS)
    return centred * inv_std, inv_std


def norm_pull(scaled, normed, inv_std):
    return inv_std * (
        scaled
        - jnp.mean(scaled, axis=-1, keepdims=True)
        - normed * jnp.mean(scaled * normed, axis=-1, keepdims=True)
    )


def column_sum(values_in):
    return jnp.sum(values_in, axis=0, keepdims=True)


CUT = 1
EARLY = 1
AHEAD = 2
BESIDE_TOKENS = {
    15: ((0, 0),),
    16: ((0, 1),),
    18: ((1, 0),),
    99: ((1, 1),),
    100: ((1, 2),),
    101: ((1, 3), (1, 4)),
    102: ((1, 5),),
    103: ((1, 6),),
    104: ((1, 7),),
    105: ((1, 8),),
    111: ((1, 9),),
    112: ((1, 10),),
}
SUB = 4
ROWS_SUB = 32
PIECES = (
    ("out", (24, 768), 0, 0),
    ("vec", (16, 128), 0, 0),
    ("up", (24, 768), 0, 0),
    ("up", (24, 768), 0, 768),
    ("up", (24, 768), 0, 1536),
    ("up", (24, 768), 0, 2304),
    ("down", (32, 768), 0, 0),
    ("down", (32, 768), 32, 0),
    ("down", (32, 768), 64, 0),
)


def forward_kernel(
    tokens,
    cot,
    segments,
    wqkv,
    wout,
    wup,
    wdown,
    rows24,
    up_bias,
    qv_bias,
    lo,
    dr1,
    dctx,
    gvec,
    gout_h,
    gup_h,
    gdown_h,
    tok_all,
    q_all,
    k_all,
    v_all,
    o_all,
    lse_all,
    wq_all,
    idrow_all,
    idcol_all,
    tok,
    idp,
    land,
    wqs,
    qs,
    ks,
    vs,
    os_,
    lses,
    idrow,
    idcol,
    ctx,
    wout_g,
    wup_g,
    wdown_g,
    vec_g,
    ctx_in,
    cot_in,
    wout_v,
    wup_v,
    active,
    slope,
    go,
    gu,
    gd,
    ro,
    ru,
    rd,
    tok_rs,
    id_rs,
    tz_ss,
    tx_ss,
    ty_ss,
    tc_ss,
    iz_ss,
    ix_ss,
    iy_ss,
    ic_ss,
    cot_ss,
    cot_rs,
    wq_ss,
    wq_rs,
    wz_ss,
    wz_rs,
    wp_ss,
    wp_rs,
    ctx_ss,
    ctx_rs,
    out_sem,
    c_ss,
    c_rs,
    o_sem,
    ids,
    wq,
    vec,
):
    f32, bf = jnp.float32, jnp.bfloat16
    x, y, c, h, z = place()
    zl, pi = lax.rem(z, 2), lax.div(z, 2)
    g = 2 * zl + y
    me = x * 16 + h * 4 + z
    hy = lax.rem(h + 2, 4)
    hc = h + 1 - 2 * c
    to_x, to_y, to_c = (1 - x, h, z), (x, hy, z), (x, hc, z)
    pz, zc = z + 1 - 2 * zl, lax.rem(z + 2, 4)
    to_n, to_d, to_z = (x, h, pz), (x, hy, pz), (x, h, zc)
    mid = jnp.where(z < 2, 2, 1)
    inner = jnp.logical_or(z == 1, z == 2)
    outer = jnp.logical_not(inner)
    spot = z * 512 + h * 128 + lax.broadcasted_iota(jnp.int32, (2, 128), 1)
    ident = jnp.where(segments[...] == NSEG - 1, 1000 + spot, segments[...]).astype(f32)
    for i in range(2):
        ids[i] = jnp.broadcast_to(ident[i : i + 1], (8, 128))
    def moved(values, width, steps, index):
        out = None
        for k, start in enumerate(steps):
            ends = []
            if start:
                ends.append(jnp.zeros((values.shape[0], start), f32))
            ends.append(values)
            if width - start - values.shape[1]:
                ends.append(jnp.zeros((values.shape[0], width - start - values.shape[1]), f32))
            row = jnp.concatenate(ends, axis=1)
            out = row if out is None else jnp.where(index == k, row, out)
        return out

    row8 = lax.broadcasted_iota(jnp.int32, (8, 576), 0)
    starts = [48 * k for k in range(4)] + [384 + 48 * k for k in range(4)]
    bias_row = moved(qv_bias[...].astype(f32), 576, starts, 4 * x + z)
    whole = wqkv[...].astype(f32)
    for q in range(4):
        cols = [whole[:, 768 * p + 192 * q : 768 * p + 192 * q + 192] for p in range(3)]
        bias_rows = jnp.where((h == q) & (row8 == 0), bias_row, 0.0)
        wq[q] = jnp.concatenate([jnp.concatenate(cols, axis=1), bias_rows], axis=0).astype(bf)
    rows16 = jnp.concatenate(
        [
            moved(rows24[...].astype(f32), 128, [24 * k for k in range(4)], z),
            jnp.zeros((10, 128), f32),
        ],
        axis=0,
    )
    up_row = jnp.concatenate([up_bias[...].astype(f32), jnp.zeros((1, 32), f32)], axis=1)
    row16 = lax.broadcasted_iota(jnp.int32, (16, 128), 0)
    vec[...] = jnp.where(row16 == 6 + z, up_row, rows16).astype(bf)
    greet(peers_of(x, h, c, z))

    mine = z * 4 + h
    weights = {"out": (wout, wout_g), "up": (wup, wup_g), "down": (wdown, wdown_g), "vec": (vec, vec_g)}
    count = len(PIECES)
    base = x * 16 + h * 4
    bx, by = (1 - x) * 16 + h * 4, x * 16 + hy * 4

    def side(start, ab):
        return pl.ds(start, CUT) if ab == 0 else pl.ds(start + CUT, 4 - CUT)

    pa, pb, sa, sb = side(base, 0), side(base, 1), side(bx, 0), side(by, 1)
    sent = []

    def shard(n):
        name, shape, row, col = PIECES[n]
        return weights[name][0].at[pl.ds(row, shape[0]), pl.ds(col, shape[1])]

    def at(n, where):
        name, shape, row, col = PIECES[n]
        return weights[name][1].at[where, pl.ds(row, shape[0]), pl.ds(col, shape[1])]

    def two(n):
        return at(n, pl.ds(0, 2))

    def some(n, ab):
        return at(n, side(0, ab))

    def pass_on(n, where, k, sem, dev):
        remote(at(n, where), at(n, where), wp_ss.at[n, k], wp_rs.at[(n,) + sem], dev).start()
        sent.append((n, k, sem[2]))

    def along_z(n):
        pltpu.make_async_copy(shard(n), at(n, me), wz_rs.at[n, z]).start()
        for k, zz in enumerate((pz, mid)):
            remote(shard(n), at(n, me), wz_ss.at[n, k], wz_rs.at[n, z], (x, h, zz)).start()

    def relay(n):
        @pl.when(inner)
        def _():
            there = pl.ds(base + jnp.where(z < 2, 2, 0), 2)
            for k in range(2):
                wait_for(at(n, 0), wz_rs.at[n, jnp.where(z < 2, 2, 0) + k])
            remote(at(n, there), at(n, there), wz_ss.at[n, 2], wz_rs.at[n, 4], (x, h, pz)).start()

    def first_hop(n):
        for k in range(2):
            wait_for(at(n, 0), wz_rs.at[n, jnp.where(z < 2, 0, 2) + k])

        @pl.when(outer)
        def _():
            wait_for(two(n), wz_rs.at[n, 4])

        pass_on(n, pa, 0, (x, h, 0), to_x)
        pass_on(n, pb, 1, (x, h, 1), to_y)
        pass_on(n, pa, 2, (x, h, 0), to_y)
        pass_on(n, pb, 3, (x, h, 1), to_x)
        pass_on(n, pa, 4, (x, h, 0), to_c)
        pass_on(n, pb, 5, (x, h, 1), to_c)

    def second_hop(n):
        wait_for(some(n, 0), wp_rs.at[n, 1 - x, h, 0])
        wait_for(some(n, 1), wp_rs.at[n, x, hy, 1])
        pass_on(n, sa, 6, (1 - x, h, 0), to_y)
        pass_on(n, sb, 7, (x, hy, 1), to_x)
        pass_on(n, sa, 8, (1 - x, h, 0), to_c)
        pass_on(n, sb, 9, (x, hy, 1), to_c)

    def third_hop(n):
        for k, (xs, hs, ab) in enumerate(((x, hy, 0), (1 - x, h, 1), (1 - x, hy, 0), (1 - x, hy, 1))):
            wait_for(some(n, ab), wp_rs.at[n, xs, hs, ab])
            pass_on(n, side(xs * 16 + hs * 4, ab), 10 + k, (xs, hs, ab), to_c)

    def advance(t):
        if t < count:
            first_hop(t)
        if t + AHEAD < count:
            relay(t + AHEAD)
        if 0 <= t - 1 < count:
            second_hop(t - 1)
        if 0 <= t - 2 < count:
            third_hop(t - 2)

    for n in range(EARLY):
        along_z(n)

    cuts = [pl.ds(ROWS_SUB * q, ROWS_SUB) for q in range(SUB)]

    def send_row(i, to):
        for q in range(SUB):
            remote(
                tokens.at[i, cuts[q]], tok.at[mine, cuts[q]], tz_ss.at[i, q], tok_rs.at[mine, q], to
            ).start()
        remote(ids.at[i], idp.at[mine], iz_ss.at[i], id_rs.at[mine], to).start()

    for i in range(2):

        @pl.when(pi == i)
        def _():
            send_row(i, to_n)
            for q in range(SUB):
                pltpu.make_async_copy(
                    tokens.at[i, cuts[q]], tok.at[mine, cuts[q]], tok_rs.at[mine, q]
                ).start()
            pltpu.make_async_copy(ids.at[i], idp.at[mine], id_rs.at[mine]).start()

        @pl.when(pi != i)
        def _():
            send_row(i, (x, h, 1 + i))

    def run_beside(t):
        for kind, n in BESIDE_TOKENS.get(t, ()):
            relay(n) if kind == 0 else advance(n)

    pltpu.make_async_copy(wq.at[g], land.at[c, x, pi, g], wq_rs.at[c, x, pi, g]).start()
    for k, (dev, target) in enumerate(
        ((to_n, 2 * (1 - zl) + y), (to_y, 2 * zl + 1 - y), (to_d, 2 * (1 - zl) + 1 - y))
    ):
        remote(wq.at[target], land.at[c, x, pi, g], wq_ss.at[k], wq_rs.at[c, x, pi, g], dev).start()

    def give_slices(xs, pp, k, dev):
        block = land.at[c, xs, pp]
        remote(block, block, wq_ss.at[k], wq_rs.at[c, xs, pp, 0], dev).start()

    for q in range(4):
        wait_for(land.at[c, x, pi, q], wq_rs.at[c, x, pi, q])
    give_slices(x, pi, 3, to_z)
    give_slices(x, pi, 4, to_x)
    give_slices(x, pi, 5, to_c)
    for n in range(EARLY, count):
        along_z(n)
    for i in range(2):

        @pl.when(pi == i)
        def _():
            pltpu.make_async_copy(cot.at[i], cot_in.at[pi], cot_rs.at[pi]).start()

        @pl.when(pi != i)
        def _():
            remote(cot.at[i], cot_in.at[pi], cot_ss, cot_rs.at[pi], to_z).start()

    turns = (z, pz, zc, lax.rem(pz + 2, 4))

    def hand_on(p, q, sends):
        wait_for(tok.at[p, cuts[q]], tok_rs.at[p, q])
        if q == 0:
            wait_for(idp.at[p], id_rs.at[p])
        for sem, id_sem, dev in sends:
            remote(tok.at[p, cuts[q]], tok.at[p, cuts[q]], sem.at[q], tok_rs.at[p, q], dev).start()
            if q == 0:
                remote(idp.at[p], idp.at[p], id_sem, id_rs.at[p], dev).start()

    def own_piece(k, q):
        p = turns[k] * 4 + h
        hand_on(
            p, q, [(ty_ss.at[k], iy_ss.at[k], to_y), (tc_ss.at[k], ic_ss.at[k], to_c)]
        )

        if k >= 2:

            @pl.when(inner)
            def _():
                cut = cuts[q]
                remote(
                    tok.at[p, cut], tok.at[p, cut], tx_ss.at[k, q], tok_rs.at[p, q], to_n
                ).start()
                if q == 0:
                    remote(idp.at[p], idp.at[p], ix_ss.at[k], id_rs.at[p], to_n).start()

    def side_piece(k, q):
        hand_on(
            turns[k] * 4 + hy, q, [(tc_ss.at[4 + k], ic_ss.at[4 + k], to_c)]
        )

    order = [(0, q) for q in range(SUB)] + [(k, q) for q in range(SUB) for k in range(1, 4)]
    lag = 4
    for t in range(len(order) + lag):
        if t < len(order):
            own_piece(*order[t])
        if t >= lag:
            side_piece(*order[t - lag])
        run_beside(t)

    wait_for(land.at[c, x, 1 - pi], wq_rs.at[c, x, 1 - pi, 0])
    give_slices(x, 1 - pi, 6, to_x)
    give_slices(x, 1 - pi, 7, to_c)
    for k in range(2):
        wait_for(land.at[c, 1 - x, k], wq_rs.at[c, 1 - x, k, 0])
        give_slices(1 - x, k, 8 + k, to_c)
    run_beside(99)
    for k in range(4):
        zz = lax.rem(z + k, 4)
        for hh in (hc, lax.rem(hc + 2, 4)):
            p = zz * 4 + hh
            for q in range(SUB):
                wait_for(tok.at[p, cuts[q]], tok_rs.at[p, q])
            wait_for(idp.at[p], id_rs.at[p])
    for k in range(4):
        wait_for(land.at[1 - c, k // 2, k % 2], wq_rs.at[1 - c, k // 2, k % 2, 0])

    run_beside(100)
    bias8 = jnp.zeros((8, 576), jnp.float32)
    for xs in range(2):
        for hs in range(4):
            part = []
            for zz in range(4):
                block = land[hs % 2, xs, zz // 2, 2 * (zz % 2) + hs // 2].astype(jnp.float32)
                part.append(block[:24])
                bias8 = bias8 + block[24:]
            start = (xs * 16 + hs * 4) * 24
            wqs[start : start + 96, :] = jnp.concatenate(part, axis=0).astype(jnp.bfloat16)
    bias = bias8[0:1, :]

    for p in range(16):
        idrow[:, 128 * p : 128 * p + 128] = idp[p]

    def project(j, carry):
        zz, yy = lax.div(j, 2), lax.rem(j, 2)
        p = zz * 4 + yy * 2 + c
        rows = pl.ds(pl.multiple_of(j * 128, 128), 128)
        mixed = nn(tok[p], wqs[:, 0:192]) + bias[:, 0:192]
        low = mixed.astype(jnp.bfloat16) * jnp.bfloat16(SCALE)
        for hh in range(3):
            qs[hh, rows, :] = low[:, 64 * hh : 64 * hh + 64]
        for q in range(2):
            line = jnp.broadcast_to(idp[2 * j + q][0:1, :], (128, 128))
            at = pl.ds(pl.multiple_of((2 * j + q) * 128, 128), 128)
            idcol[at, :] = jnp.transpose(line)
        both = tok[pl.ds(2 * j, 2)].reshape(256, 768)
        wide = nn(both, wqs[:, 192:576]) + bias[:, 192:576]
        wide = wide.astype(jnp.bfloat16)
        key_rows = pl.ds(pl.multiple_of(j * 256, 256), 256)
        for hh in range(3):
            ks[hh, key_rows, :] = wide[:, 64 * hh : 64 * hh + 64]
            vs[hh, key_rows, :] = wide[:, 192 + 64 * hh : 256 + 64 * hh]
        return carry

    lax.fori_loop(0, 8, project, 0)
    run_beside(101)

    def attend(zz):
        rows = slice(zz * 256, zz * 256 + 256)
        upper = pl.ds(pl.multiple_of((zz * 4 + c) * 128, 128), 128)
        lower = pl.ds(pl.multiple_of((zz * 4 + 2 + c) * 128, 128), 128)
        idq = jnp.concatenate([idcol[upper, :], idcol[lower, :]], axis=0)
        mask = idq[:, 0:1] == idrow[0:1, :]
        def one_head(hh, carry):
            scores = nt(qs[hh, rows, :], ks[hh])
            scores = jnp.where(mask, scores, MASKED)
            top = jnp.max(scores, axis=-1, keepdims=True)
            weights_ = jnp.exp(scores - top)
            total = jnp.sum(weights_, axis=-1, keepdims=True)
            o = nn(weights_.astype(jnp.bfloat16), vs[hh]) / total
            os_[hh, rows, :] = o
            lse = jnp.broadcast_to(top + jnp.log(total), (256, 128))
            lses[hh, :, rows] = jnp.transpose(lse)[0:8, :]
            return carry

        lax.fori_loop(0, 3, one_head, 0)
        out = jnp.concatenate([os_[k, rows, :] for k in range(3)], axis=1).astype(jnp.bfloat16)
        slot = zz // 2
        for yy in range(2):
            j = zz * 2 + yy
            ctx[j] = out[128 * yy : 128 * yy + 128]
            stay = jnp.logical_and(zl == zz % 2, y == yy)

            @pl.when(stay)
            def _():
                pltpu.make_async_copy(ctx.at[j], ctx_in.at[g, slot], ctx_rs.at[g, slot]).start()

            @pl.when(jnp.logical_not(stay))
            def _():
                remote(
                    ctx.at[j],
                    ctx_in.at[g, slot],
                    ctx_ss.at[j],
                    ctx_rs.at[g, slot],
                    (x, yy * 2 + c, 2 * pi + zz % 2),
                ).start()

    for t in range(4):
        attend(t)
        run_beside(102 + t)

    kept = (
        (tok, tok_all),
        (qs, q_all),
        (ks, k_all),
        (vs, v_all),
        (os_, o_all),
        (lses, lse_all),
        (wqs, wq_all),
        (idrow, idrow_all),
        (idcol, idcol_all),
    )
    for k, (src, dst) in enumerate(kept):
        pltpu.make_async_copy(src, dst, out_sem.at[k]).start()
    def arrive(n):
        for xs in range(2):
            for yy in range(2):
                for ab in range(2):
                    wait_for(some(n, ab), wp_rs.at[n, xs, yy * 2 + 1 - c, ab])

    def flatten(src, dst, cols):
        for k in range(8):
            part = [src[4 * k + q, :, cols].astype(f32) for q in range(4)]
            dst[96 * k : 96 * k + 96, cols] = jnp.concatenate(part, axis=0).astype(bf)

    run_beside(110)
    for s in range(2):
        wait_for(cot_in.at[s], cot_rs.at[s])
        for q in range(4):
            wait_for(ctx_in.at[q, s], ctx_rs.at[q, s])
    arrive(0)
    arrive(1)
    windows = []
    for i in range(8):
        window = vec_g[4 * i].astype(f32)
        for k in range(1, 4):
            window = window + vec_g[4 * i + k].astype(f32)
        windows.append(window)

    def row(i):
        if i < 6:
            return jnp.concatenate([w[i : i + 1, :96] for w in windows], axis=1)
        pair = windows[2 * (i - 6) : 2 * (i - 6) + 2]
        return jnp.concatenate([w[k : k + 1, :96] for w in pair for k in range(6, 10)], axis=1)

    full_ctx = jnp.concatenate([ctx_in[q].reshape(256, 192) for q in range(4)], axis=1)
    flatten(wout_g, wout_v, slice(0, 768))
    own = jnp.concatenate([tok[zl * 4 + h], tok[(2 + zl) * 4 + h]], axis=0).astype(f32)
    normed_one, inv_one = add_norm(own + nn(full_ctx, wout_v[...]) + row(0))
    hidden = normed_one * row(1) + row(2)
    hidden_low = hidden.astype(bf)
    run_beside(111)
    for k in range(4):
        cols = slice(768 * k, 768 * k + 768)
        arrive(2 + k)
        flatten(wup_g, wup_v, cols)
        raised = nn(hidden_low, wup_v[:, cols]) + row(6 + k)
        normal = 0.5 + 0.5 * lax.erf(raised * (0.5**0.5))
        active[:, cols] = (raised * normal).astype(bf)
        slope[:, cols] = normal + raised * jnp.exp(-0.5 * raised * raised) * (0.5 / math.pi) ** 0.5
    run_beside(112)
    for n in (6, 7, 8):
        arrive(n)
    branch = nn(active[...], wdown_g[...].reshape(3072, 768)) + row(3)
    normed_two, inv_two = add_norm(hidden + branch)
    lo[...] = (normed_two * row(4) + row(5)).astype(bf).reshape(2, 128, 768)
    grad = cot_in[...].reshape(256, 768).astype(f32)
    gvec[4:5, :] = column_sum(grad * normed_two)
    gvec[5:6, :] = column_sum(grad)
    grad_second = norm_pull(grad * row(4), normed_two, inv_two)
    grad_branch = grad_second.astype(bf)
    gvec[3:4, :] = column_sum(grad_branch.astype(f32))

    def halves(n, full, back, rows, part):
        def at(xs, ys, core):
            start = (xs * 16 + (ys * 2 + core) * 4) * (rows // 4)
            return pl.ds(pl.multiple_of(start, rows // 4 * 4), rows)

        for xs in range(2):
            for ys in range(2):
                remote(
                    full.at[at(xs, ys, 1 - c), part],
                    back.at[xs, ys, :, part],
                    c_ss.at[n, xs, ys],
                    c_rs.at[n, xs, ys],
                    to_c,
                ).start()

    for k in range(4):
        rows = slice(768 * k, 768 * k + 768)
        gd[rows, :] = tn(active[:, rows], grad_branch).astype(bf)
    halves(0, gd, rd, 384, pl.ds(0, 768))
    for k in range(4):
        cols = slice(768 * k, 768 * k + 768)
        pulled = (nt(grad_branch, wdown_g[8 * k : 8 * k + 8].reshape(768, 768)) * slope[:, cols]).astype(bf)
        active[:, cols] = pulled
        gvec[6 + k : 7 + k, :] = column_sum(pulled.astype(f32))
        gu[:, cols] = tn(hidden_low, pulled).astype(bf)
        halves(1 + k, gu, ru, 96, pl.ds(768 * k, 768))
    grad_hidden = grad_second + nt(active[...], wup_v[...])
    gvec[1:2, :] = column_sum(grad_hidden * normed_one)
    gvec[2:3, :] = column_sum(grad_hidden)
    grad_first = norm_pull(grad_hidden * row(1), normed_one, inv_one)
    dr1[...] = grad_first.reshape(2, 128, 768)
    grad_attended = grad_first.astype(bf)
    gvec[0:1, :] = column_sum(grad_attended.astype(f32))
    gvec[10:16, :] = jnp.zeros((6, 768), f32)
    go[...] = tn(full_ctx, grad_attended).astype(bf)
    halves(5, go, ro, 96, pl.ds(0, 768))
    back = nt(grad_attended, wout_v[...]).astype(bf)
    for q in range(4):
        dctx[q] = back[:, 192 * q : 192 * q + 192].reshape(2, 128, 192)

    def settle(full, back, rows, out, sems, base, parts):
        for xs in range(2):
            for ys in range(2):
                for n, part in parts:
                    wait_for(back.at[xs, ys, :, part], c_rs.at[n, xs, ys])

                def body(t, carry):
                    rel = pl.multiple_of(t * 16, 16)
                    start = (xs * 16 + (ys * 2 + c) * 4) * (rows // 4)
                    mine = full[pl.ds(pl.multiple_of(start + rel, 16), 16), :].astype(f32)
                    there = pl.ds(rel, 16)
                    back[xs, ys, there, :] = (
                        mine + back[xs, ys, there, :].astype(f32)
                    ).astype(bf)
                    return carry

                lax.fori_loop(0, rows // 16, body, 0)
                k = base + xs * 2 + ys
                pltpu.make_async_copy(back.at[xs, ys], out.at[xs, ys], sems.at[k]).start()

    settle(gd, rd, 384, gdown_h, o_sem, 0, [(0, pl.ds(0, 768))])
    settle(gu, ru, 96, gup_h, o_sem, 4, [(1 + k, pl.ds(768 * k, 768)) for k in range(4)])
    settle(go, ro, 96, gout_h, o_sem, 8, [(5, pl.ds(0, 768))])
    for n in range(6):
        for xs in range(2):
            for ys in range(2):
                gone = gd.at[pl.ds(0, 384)] if n == 0 else gu.at[pl.ds(0, 96), pl.ds(0, 768)]
                wait_for(gone, c_ss.at[n, xs, ys])
    for first, out in ((0, gdown_h), (4, gup_h), (8, gout_h)):
        for k in range(4):
            wait_for(out.at[k // 2, k % 2], o_sem.at[first + k])

    wait_for(cot.at[0], cot_ss)
    for i in range(2):
        for q in range(SUB):
            wait_for(tok.at[0, cuts[q]], tz_ss.at[i, q])
        wait_for(ids.at[i], iz_ss.at[i])
    for k in range(2, 4):

        @pl.when(inner)
        def _():
            for q in range(SUB):
                wait_for(tok.at[0, cuts[q]], tx_ss.at[k, q])
            wait_for(idp.at[0], ix_ss.at[k])

    for k in range(4):
        for q in range(SUB):
            wait_for(tok.at[0, cuts[q]], ty_ss.at[k, q])
        wait_for(idp.at[0], iy_ss.at[k])
    for k in range(8):
        for q in range(SUB):
            wait_for(tok.at[0, cuts[q]], tc_ss.at[k, q])
        wait_for(idp.at[0], ic_ss.at[k])
    for k in range(3):
        wait_for(wq.at[0], wq_ss.at[k])
    for k in range(3, 10):
        wait_for(land.at[0, 0, 0], wq_ss.at[k])
    for n in range(count):
        for k in range(2):
            wait_for(shard(n), wz_ss.at[n, k])

        @pl.when(inner)
        def _():
            wait_for(two(n), wz_ss.at[n, 2])

    for n, k, ab in sent:
        wait_for(some(n, ab), wp_ss.at[n, k])
    for j in range(8):
        zz, yy = j // 2, j % 2
        stay = jnp.logical_and(zl == zz % 2, y == yy)

        @pl.when(jnp.logical_not(stay))
        def _():
            wait_for(ctx.at[j], ctx_ss.at[j])

    for k, (src, dst) in enumerate(kept):
        wait_for(dst, out_sem.at[k])


def forward_call(tokens, cot, segments, wqkv, wout, wup, wdown, rows24, up_bias, qv_bias):
    bf, f32 = jnp.bfloat16, jnp.float32
    sds = jax.ShapeDtypeStruct
    dma = pltpu.SemaphoreType.DMA
    outs = [
        sds((2, 128, 768), bf),
        sds((2, 128, 768), f32),
        sds((4, 2, 128, 192), bf),
        sds((16, 768), f32),
        sds((2, 2, 96, 768), bf),
        sds((2, 2, 96, 3072), bf),
        sds((2, 2, 384, 768), bf),
        sds((16, 128, 768), bf),
        sds((3, 1024, 64), bf),
        sds((3, 2048, 64), bf),
        sds((3, 2048, 64), bf),
        sds((3, 1024, 64), f32),
        sds((3, 8, 1024), f32),
        sds((768, 576), bf),
        sds((8, 2048), f32),
        sds((2048, 128), f32),
    ]
    scratch = [
        pltpu.VMEM((16, 128, 768), bf),
        pltpu.VMEM((16, 8, 128), f32),
        pltpu.VMEM((2, 2, 2, 4, 32, 576), bf),
        pltpu.VMEM((768, 576), bf),
        pltpu.VMEM((3, 1024, 64), bf),
        pltpu.VMEM((3, 2048, 64), bf),
        pltpu.VMEM((3, 2048, 64), bf),
        pltpu.VMEM((3, 1024, 64), f32),
        pltpu.VMEM((3, 8, 1024), f32),
        pltpu.VMEM((8, 2048), f32),
        pltpu.VMEM((2048, 128), f32),
        pltpu.VMEM((8, 128, 192), bf),
        pltpu.VMEM((32, 24, 768), bf),
        pltpu.VMEM((32, 24, 3072), bf),
        pltpu.VMEM((32, 96, 768), bf),
        pltpu.VMEM((32, 16, 128), bf),
        pltpu.VMEM((4, 2, 128, 192), bf),
        pltpu.VMEM((2, 128, 768), bf),
        pltpu.VMEM((768, 768), bf),
        pltpu.VMEM((768, 3072), bf),
        pltpu.VMEM((256, 3072), bf),
        pltpu.VMEM((256, 3072), f32),
        pltpu.VMEM((768, 768), bf),
        pltpu.VMEM((768, 3072), bf),
        pltpu.VMEM((3072, 768), bf),
        pltpu.VMEM((2, 2, 96, 768), bf),
        pltpu.VMEM((2, 2, 96, 3072), bf),
        pltpu.VMEM((2, 2, 384, 768), bf),
        dma((16, SUB)),
        dma((16,)),
        dma((2, SUB)),
        dma((4, SUB)),
        dma((4, SUB)),
        dma((8, SUB)),
        dma((2,)),
        dma((4,)),
        dma((4,)),
        dma((8,)),
        dma(()),
        dma((2,)),
        dma((10,)),
        dma((2, 2, 2, 4)),
        dma((len(PIECES), 3)),
        dma((len(PIECES), 5)),
        dma((len(PIECES), 14)),
        dma((len(PIECES), 2, 4, 2)),
        dma((8,)),
        dma((4, 2)),
        dma((9,)),
        dma((6, 2, 2)),
        dma((6, 2, 2)),
        dma((12,)),
        pltpu.VMEM((2, 8, 128), f32),
        pltpu.VMEM((4, 32, 576), bf),
        pltpu.VMEM((16, 128), bf),
    ]
    here, far = pl.BlockSpec(memory_space=pltpu.VMEM), pl.BlockSpec(memory_space=ANY)
    return pl.pallas_call(
        forward_kernel,
        out_shape=outs,
        in_specs=[far, far, here, here, far, far, far, here, here, here],
        out_specs=[here] * 4 + [far] * (len(outs) - 4),
        scratch_shapes=scratch,
        compiler_params=pltpu.CompilerParams(
            collective_id=0, has_side_effects=True, vmem_limit_bytes=VMEM_LIMIT
        ),
        name="forward",
    )(tokens, cot, segments, wqkv, wout, wup, wdown, rows24, up_bias, qv_bias)


RCUT = 2
JOBS = (
    ("down", (48, 768), 0, 0),
    ("down", (48, 768), 48, 0),
    ("up", (24, 1536), 0, 0),
    ("up", (24, 1536), 0, 1536),
    ("out", (24, 768), 0, 0),
)


def add_block(dst, src):
    dst[...] = (dst[...].astype(jnp.float32) + src[...].astype(jnp.float32)).astype(jnp.bfloat16)


def backward_kernel(
    dctx,
    lo,
    dr1,
    gout,
    gup,
    gdown,
    gvec,
    tok_h,
    q_h,
    k_h,
    v_h,
    o_h,
    lse_h,
    wq_h,
    idrow_h,
    idcol_h,
    lo_out,
    gt_out,
    gout_o,
    gup_o,
    gdown_o,
    gq_o,
    small_o,
    *rest,
):
    count = len(JOBS)
    accs, rest = rest[:count], rest[count:]
    r2as, rest = rest[:count], rest[count:]
    r2bs, rest = rest[:count], rest[count:]
    r1as, rest = rest[:count], rest[count:]
    r1bs, rest = rest[:count], rest[count:]
    rzs, rest = rest[:count], rest[count:]
    (
        tok,
        qs,
        ks,
        vs,
        os_,
        lses,
        wqs,
        idrow,
        idcol,
        dc,
        dks,
        dvs,
        dqs,
        douts,
        kv_send,
        kv_recv,
        dmix,
        dx,
        rx,
        dr,
        gt_send,
        gt_in,
        gq,
        gqc,
        gqx,
        gqz,
        gqin,
        gva,
        gvr,
        qb,
        qbr,
        qb_o,
        in_sem,
        own_ss,
        dc_ss,
        dc_rs,
        lo_ss,
        lo_rs,
        s2_ss,
        s2_rs,
        s1_ss,
        s1_rs,
        z_ss,
        z_rs,
        kv_ss,
        kv_rs,
        dx_ss,
        dx_rs,
        gt_ss,
        gt_rs,
        gq_ss,
        gq_rs,
        gv_ss,
        gv_rs,
        qb_ss,
        qb_rs,
    ) = rest
    x, y, c, h, z = place()
    zl, pi = lax.rem(z, 2), lax.div(z, 2)
    pz, zc = z + 1 - 2 * zl, lax.rem(z + 2, 4)
    g = 2 * zl + y
    hy = lax.rem(h + 2, 4)
    hc = h + 1 - 2 * c
    to_x, to_y, to_c = (1 - x, h, z), (x, hy, z), (x, hc, z)
    to_n, to_d, to_z = (x, h, pz), (x, hy, pz), (x, h, zc)
    sources = {"out": gout, "up": gup, "down": gdown}
    greet(peers_of(x, h, c, z))

    def loaded():
        return (
            (tok_h, tok),
            (q_h, qs),
            (k_h, ks),
            (v_h, vs),
            (o_h, os_),
            (lse_h, lses),
            (wq_h, wqs),
            (idrow_h, idrow),
            (idcol_h, idcol),
            (dr1, dr),
            (gvec, gva),
        )

    for s in range(2):
        j = (2 * s + zl) * 2 + y
        for k, (dev, target) in enumerate(
            ((to_n, 2 * (1 - zl) + y), (to_y, 2 * zl + 1 - y), (to_d, 2 * (1 - zl) + 1 - y))
        ):
            remote(dctx.at[target, s], dc.at[j], dc_ss.at[s, k], dc_rs.at[j], dev).start()
        pltpu.make_async_copy(dctx.at[g, s], dc.at[j], dc_rs.at[j]).start()
    for k, (src, dst) in enumerate(loaded()):
        pltpu.make_async_copy(src, dst, in_sem.at[k]).start()
    def part_of(n):
        name, shape, row, col = JOBS[n]
        return sources[name], (pl.ds(row, shape[0]), pl.ds(col, shape[1]))

    def stage1(n):
        src, part = part_of(n)
        acc = accs[n]
        for k in range(2):
            remote(
                src.at[(k, 1 - y, pl.ds(0, RCUT)) + part],
                r2as[n].at[k],
                s2_ss.at[n, k],
                s2_rs.at[n, k],
                to_y,
            ).start()
            remote(
                src.at[(1 - x, k, pl.ds(RCUT, 4 - RCUT)) + part],
                r2bs[n].at[k],
                s2_ss.at[n, 2 + k],
                s2_rs.at[n, 2 + k],
                to_x,
            ).start()
        for k in range(2):
            pltpu.make_async_copy(
                src.at[(k, y, pl.ds(0, RCUT)) + part], acc.at[k, y, pl.ds(0, RCUT)], own_ss.at[n, k]
            ).start()
            pltpu.make_async_copy(
                src.at[(x, k, pl.ds(RCUT, 4 - RCUT)) + part],
                acc.at[x, k, pl.ds(RCUT, 4 - RCUT)],
                own_ss.at[n, 2 + k],
            ).start()

    for n in range(count):
        stage1(n)
    for s in range(2):
        zz = 2 * s + zl
        row = pi
        stay = pi == s

        @pl.when(stay)
        def _():
            pltpu.make_async_copy(lo.at[s], lo_out.at[row], lo_rs.at[row]).start()

        @pl.when(jnp.logical_not(stay))
        def _():
            remote(lo.at[s], lo_out.at[row], lo_ss.at[s], lo_rs.at[row], to_z).start()

    def stage2(n):
        acc = accs[n]
        for k in range(2):
            wait_for(r2as[n].at[k], s2_rs.at[n, k])
            wait_for(r2bs[n].at[k], s2_rs.at[n, 2 + k])
            wait_for(r2as[n].at[k], own_ss.at[n, k])
            wait_for(r2bs[n].at[k], own_ss.at[n, 2 + k])
        for k in range(2):
            for q in range(RCUT):
                add_block(acc.at[k, y, q], r2as[n].at[k, q])
            for q in range(4 - RCUT):
                add_block(acc.at[x, k, RCUT + q], r2bs[n].at[k, q])
        remote(
            acc.at[1 - x, y, pl.ds(0, RCUT)], r1as[n], s1_ss.at[n, 0], s1_rs.at[n, 0], to_x
        ).start()
        remote(
            acc.at[x, 1 - y, pl.ds(RCUT, 4 - RCUT)], r1bs[n], s1_ss.at[n, 1], s1_rs.at[n, 1], to_y
        ).start()

    def stage3(n):
        acc = accs[n]
        wait_for(r1as[n], s1_rs.at[n, 0])
        wait_for(r1bs[n], s1_rs.at[n, 1])
        for q in range(RCUT):
            add_block(acc.at[x, y, q], r1as[n].at[q])
        for q in range(4 - RCUT):
            add_block(acc.at[x, y, RCUT + q], r1bs[n].at[q])
        for k in range(1, 4):
            zz = lax.rem(z + k, 4)
            remote(
                acc.at[x, y, zz], rzs[n].at[z], z_ss.at[n, k - 1], z_rs.at[n, z], (x, h, zz)
            ).start()

    def stage4(n):
        acc = accs[n]
        name, shape, row, col = JOBS[n]
        total = acc[x, y, z].astype(jnp.float32)
        for k in range(1, 4):
            zz = lax.rem(z + k, 4)
            wait_for(rzs[n].at[zz], z_rs.at[n, zz])
            total = total + rzs[n][zz].astype(jnp.float32)
        out = {"out": gout_o, "up": gup_o, "down": gdown_o}[name]
        out[row : row + shape[0], col : col + shape[1]] = total

    for k, (src, dst) in enumerate(loaded()):
        wait_for(dst, in_sem.at[k])
    for j in range(8):
        wait_for(dc.at[j], dc_rs.at[j])

    def attend(zz):
        rows = slice(zz * 256, zz * 256 + 256)
        first = pl.ds(pl.multiple_of((zz * 4 + c) * 128, 128), 128)
        second = pl.ds(pl.multiple_of((zz * 4 + 2 + c) * 128, 128), 128)
        idq = jnp.concatenate([idrow[0:1, first], idrow[0:1, second]], axis=1)
        mask = idcol[:, 0:1] == idq
        both = jnp.concatenate([dc[2 * zz], dc[2 * zz + 1]], axis=0)
        for hh in range(3):
            douts[hh] = both[:, 64 * hh : 64 * hh + 64]

        def one_head(hh, carry):
            dout = douts[hh]
            q = qs[hh, rows, :]
            delta = jnp.sum(dout.astype(jnp.float32) * os_[hh, rows, :], axis=-1, keepdims=True)
            delta = jnp.transpose(jnp.broadcast_to(delta, (256, 128)))[0:1, :]
            scores = jnp.where(mask, nt(ks[hh], q), MASKED)
            probs = jnp.exp(scores - lses[hh, 0:1, rows])
            dprobs = nt(vs[hh], dout)
            ds = (probs * (dprobs - delta)).astype(jnp.bfloat16)
            dk = nn(ds, q)
            dv = nn(probs.astype(jnp.bfloat16), dout)
            if zz == 0:
                dks[hh] = dk
                dvs[hh] = dv
            else:
                dks[hh] += dk
                dvs[hh] += dv
            dqs[hh, rows, :] = (tn(ds, ks[hh]) * SCALE).astype(jnp.bfloat16)
            return carry

        lax.fori_loop(0, 3, one_head, 0)

    def add_gv(k):
        wait_for(gva, gv_rs.at[k])
        wait_for(gva, gv_ss.at[k])
        gva[...] = gva[...] + gvr[k]

    def gv_stage(n):
        if n < 3:
            if n > 0:
                add_gv(n - 1)
            remote(gva, gvr.at[n], gv_ss.at[n], gv_rs.at[n], (to_c, to_x, to_y)[n]).start()
        elif n == 3:
            add_gv(2)
            for k in range(1, 4):
                remote(
                    gva,
                    gvr.at[3 + z],
                    gv_ss.at[2 + k],
                    gv_rs.at[3 + z],
                    (x, h, lax.rem(z + k, 4)),
                ).start()
        else:
            gv = gva[...]
            for k in range(1, 4):
                zz = lax.rem(z + k, 4)
                wait_for(gvr.at[3 + zz], gv_rs.at[3 + zz])
                gv = gv + gvr[3 + zz]
            gvr[3 + z] = gv

    gv_stage(0)
    beside = {
        0: ((stage2, 0),),
        1: ((stage2, 1), (stage3, 0)),
        2: ((stage2, 2), (stage3, 1)),
    }
    for t in range(4):
        attend(t)
        gv_stage(t + 1)
        for stage, n in beside.get(t, ()):
            stage(n)

    for j in range(8):
        p = (j // 2) * 4 + (j % 2) * 2 + 1 - c
        rows = pl.ds(pl.multiple_of(p * 128, 128), 128)
        kv_send[j] = jnp.concatenate(
            [dks[hh, rows, :] for hh in range(3)] + [dvs[hh, rows, :] for hh in range(3)], axis=1
        ).astype(jnp.bfloat16)
    remote(kv_send, kv_recv, kv_ss, kv_rs, to_c).start()
    stage2(3)
    stage3(2)
    wait_for(kv_recv, kv_rs)

    qsum = jnp.zeros((1, 192), jnp.float32)
    vsum = jnp.zeros((1, 192), jnp.float32)
    for j in range(8):
        p = (j // 2) * 4 + (j % 2) * 2 + c
        rows = pl.ds(pl.multiple_of(p * 128, 128), 128)
        wide = jnp.concatenate(
            [dks[hh, rows, :] for hh in range(3)] + [dvs[hh, rows, :] for hh in range(3)], axis=1
        )
        wide = (wide + kv_recv[j].astype(jnp.float32)).astype(jnp.bfloat16)
        part = jnp.concatenate([dqs[hh, 128 * j : 128 * j + 128, :] for hh in range(3)], axis=1)
        dmix[128 * j : 128 * j + 128, :] = jnp.concatenate([part, wide], axis=1)
        qsum = qsum + jnp.sum(part.astype(jnp.float32), axis=0, keepdims=True)
        vsum = vsum + jnp.sum(wide[:, 192:].astype(jnp.float32), axis=0, keepdims=True)
    none = jnp.zeros((1, 192), jnp.float32)
    qb[...] = jnp.broadcast_to(
        jnp.concatenate([qsum, none, vsum, none[:, :64]], axis=1), (8, 640)
    )
    remote(qb, qbr.at[0], qb_ss.at[0], qb_rs.at[0], to_c).start()

    for j in range(8):
        zz, yy = j // 2, j % 2
        dx[j] = nt(dmix[128 * j : 128 * j + 128, :], wqs[...]).astype(jnp.bfloat16)
        slot = zz // 2
        stay = jnp.logical_and(zl == zz % 2, y == yy)

        @pl.when(jnp.logical_not(stay))
        def _():
            remote(
                dx.at[j],
                rx.at[g, slot],
                dx_ss.at[j],
                dx_rs.at[g, slot],
                (x, yy * 2 + c, 2 * pi + zz % 2),
            ).start()

        @pl.when(stay)
        def _():
            pltpu.make_async_copy(dx.at[j], rx.at[g, slot], dx_rs.at[g, slot]).start()

    total = jnp.zeros((768, 576), jnp.float32)
    for zz in range(4):
        left = jnp.concatenate([tok[zz * 4 + c], tok[zz * 4 + 2 + c]], axis=0)
        total = total + tn(left, dmix[256 * zz : 256 * zz + 256, :])
    for xs in range(2):
        for hs in range(4):
            for zz in range(4):
                base = (xs * 16 + hs * 4 + zz) * 24
                gq[hs % 2, xs, zz // 2, 2 * (zz % 2) + hs // 2] = total[base : base + 24].astype(jnp.bfloat16)
    remote(gq.at[1 - c], gqc, gq_ss.at[0], gq_rs.at[0], to_c).start()
    stage2(4)
    stage3(3)
    stage4(0)

    def add_qb(k):
        wait_for(qb, qb_rs.at[k])
        wait_for(qb, qb_ss.at[k])
        qb[...] = qb[...] + qbr[k]

    wait_for(gqc, gq_rs.at[0])

    def addq(t, carry):
        i, q = lax.div(t, 4), lax.rem(t, 4)
        xs, pp = lax.div(i, 2), lax.rem(i, 2)
        add_block(gq.at[c, xs, pp, q], gqc.at[xs, pp, q])
        return carry

    lax.fori_loop(0, 16, addq, 0)
    remote(gq.at[c, 1 - x], gqx, gq_ss.at[1], gq_rs.at[1], to_x).start()
    add_qb(0)
    remote(qb, qbr.at[1], qb_ss.at[1], qb_rs.at[1], to_x).start()
    stage3(4)
    stage4(1)
    wait_for(gqx, gq_rs.at[1])

    def addx(t, carry):
        pp, q = lax.div(t, 4), lax.rem(t, 4)
        add_block(gq.at[c, x, pp, q], gqx.at[pp, q])
        return carry

    lax.fori_loop(0, 8, addx, 0)
    remote(gq.at[c, x, 1 - pi], gqz, gq_ss.at[2], gq_rs.at[2], to_z).start()
    add_qb(1)
    remote(qb, qbr.at[2], qb_ss.at[2], qb_rs.at[2], to_z).start()
    stage4(2)

    for s in range(2):
        acc = dr[s]
        for q in range(4):
            wait_for(rx.at[q, s], dx_rs.at[q, s])
            acc = acc + rx[q, s].astype(jnp.float32)
        gt_send[s] = acc.astype(jnp.bfloat16)
        zz = 2 * s + zl
        row = pi
        stay = pi == s

        @pl.when(stay)
        def _():
            pltpu.make_async_copy(gt_send.at[s], gt_in.at[row], gt_rs.at[row]).start()

        @pl.when(jnp.logical_not(stay))
        def _():
            remote(gt_send.at[s], gt_in.at[row], gt_ss.at[s], gt_rs.at[row], to_z).start()

    wait_for(gqz, gq_rs.at[2])
    for q in range(4):
        add_block(gq.at[c, x, pi, q], gqz.at[q])
    add_qb(2)
    gqzs = gq.at[c, x, pi]
    for k, (dev, target) in enumerate(
        ((to_n, 2 * (1 - zl) + y), (to_y, 2 * zl + 1 - y), (to_d, 2 * (1 - zl) + 1 - y))
    ):
        remote(gqzs.at[target], gqin.at[g], gq_ss.at[3 + k], gq_rs.at[3 + g], dev).start()
        remote(qb, qb_o.at[g], qb_ss.at[3 + k], qb_rs.at[3 + g], dev).start()
    pltpu.make_async_copy(gqzs.at[g], gqin.at[g], gq_rs.at[3 + g]).start()
    pltpu.make_async_copy(qb, qb_o.at[g], qb_rs.at[3 + g]).start()
    stage4(3)
    for q in range(4):
        wait_for(gqin.at[q], gq_rs.at[3 + q])
        wait_for(qb_o.at[q], qb_rs.at[3 + q])
        gq_o[q] = gqin[q].astype(jnp.float32)
    me = x * 16 + h * 4 + z
    vectors = gvr[3 + z]
    own_rows = pltpu.roll(vectors[0:8, :], lax.rem(768 - 24 * me, 768), 1)[:, 0:128]
    up_row = jnp.zeros((1, 768), jnp.float32)
    for i in range(4):
        up_row = up_row + jnp.where(lax.div(me, 8) == i, vectors[6 + i : 7 + i, :], 0.0)
    up_rows = jnp.broadcast_to(up_row, (8, 768))
    up_rows = pltpu.roll(up_rows, lax.rem(768 - 96 * lax.rem(me, 8), 768), 1)[:, 0:128]
    qv_rows = pltpu.roll(qb_o[h], lax.rem(640 - 48 * z - 384 * x, 640), 1)[:, 0:128]
    line = lax.broadcasted_iota(jnp.int32, (8, 128), 0)
    small_o[...] = jnp.where(line < 6, own_rows, jnp.where(line == 6, up_rows, qv_rows))
    stage4(4)
    for i in range(2):
        wait_for(gt_in.at[i], gt_rs.at[i])
        gt_out[i] = gt_in[i].astype(jnp.float32)
        wait_for(lo_out.at[i], lo_rs.at[i])

    for s in range(2):
        for k in range(3):
            wait_for(dctx.at[0, 0], dc_ss.at[s, k])

        @pl.when(pi != s)
        def _():
            wait_for(lo.at[s], lo_ss.at[s])
            wait_for(gt_send.at[s], gt_ss.at[s])

    for n in range(count):
        for k in range(2):
            wait_for(r1as[n], s2_ss.at[n, k])
            wait_for(r1bs[n], s2_ss.at[n, 2 + k])
        wait_for(r1as[n], s1_ss.at[n, 0])
        wait_for(r1bs[n], s1_ss.at[n, 1])
        for k in range(3):
            wait_for(rzs[n].at[0], z_ss.at[n, k])
    wait_for(kv_send, kv_ss)
    for j in range(8):
        stay = jnp.logical_and(zl == (j // 2) % 2, y == j % 2)

        @pl.when(jnp.logical_not(stay))
        def _():
            wait_for(dx.at[j], dx_ss.at[j])

    wait_for(gqc, gq_ss.at[0])
    wait_for(gqx, gq_ss.at[1])
    wait_for(gqz, gq_ss.at[2])
    for k in range(3):
        wait_for(gqin.at[0], gq_ss.at[3 + k])
        wait_for(qb, qb_ss.at[3 + k])
        wait_for(gva, gv_ss.at[3 + k])


def backward_call(*args):
    bf, f32 = jnp.bfloat16, jnp.float32
    sds = jax.ShapeDtypeStruct
    dma = pltpu.SemaphoreType.DMA
    vm = pltpu.VMEM
    outs = [
        sds((2, 128, 768), bf),
        sds((2, 128, 768), f32),
        sds((24, 768), f32),
        sds((24, 3072), f32),
        sds((96, 768), f32),
        sds((4, 24, 576), f32),
        sds((8, 128), f32),
    ]
    shapes = [job[1] for job in JOBS]
    count = len(JOBS)
    scratch = (
        [vm((2, 2, 4) + s, bf) for s in shapes]
        + [vm((2, RCUT) + s, bf) for s in shapes]
        + [vm((2, 4 - RCUT) + s, bf) for s in shapes]
        + [vm((RCUT,) + s, bf) for s in shapes]
        + [vm((4 - RCUT,) + s, bf) for s in shapes]
        + [vm((4,) + s, bf) for s in shapes]
        + [
            vm((16, 128, 768), bf),
            vm((3, 1024, 64), bf),
            vm((3, 2048, 64), bf),
            vm((3, 2048, 64), bf),
            vm((3, 1024, 64), f32),
            vm((3, 8, 1024), f32),
            vm((768, 576), bf),
            vm((8, 2048), f32),
            vm((2048, 128), f32),
            vm((8, 128, 192), bf),
            vm((3, 2048, 64), f32),
            vm((3, 2048, 64), f32),
            vm((3, 1024, 64), bf),
            vm((3, 256, 64), bf),
            vm((8, 128, 384), bf),
            vm((8, 128, 384), bf),
            vm((1024, 576), bf),
            vm((8, 128, 768), bf),
            vm((4, 2, 128, 768), bf),
            vm((2, 128, 768), f32),
            vm((2, 128, 768), bf),
            vm((2, 128, 768), bf),
            vm((2, 2, 2, 4, 24, 576), bf),
            vm((2, 2, 4, 24, 576), bf),
            vm((2, 4, 24, 576), bf),
            vm((4, 24, 576), bf),
            vm((4, 24, 576), bf),
            vm((16, 768), f32),
            vm((7, 16, 768), f32),
            vm((8, 640), f32),
            vm((3, 8, 640), f32),
            vm((4, 8, 640), f32),
            dma((11,)),
            dma((count, 4)),
            dma((2, 3)),
            dma((8,)),
            dma((2,)),
            dma((2,)),
            dma((count, 4)),
            dma((count, 4)),
            dma((count, 2)),
            dma((count, 2)),
            dma((count, 3)),
            dma((count, 4)),
            dma(()),
            dma(()),
            dma((8,)),
            dma((4, 2)),
            dma((2,)),
            dma((2,)),
            dma((6,)),
            dma((7,)),
            dma((6,)),
            dma((7,)),
            dma((6,)),
            dma((7,)),
        ]
    )
    here = pl.BlockSpec(memory_space=pltpu.VMEM)
    far = pl.BlockSpec(memory_space=ANY)
    return pl.pallas_call(
        backward_kernel,
        out_shape=outs,
        in_specs=[far] * 16,
        out_specs=[far] + [here] * 6,
        scratch_shapes=scratch,
        compiler_params=pltpu.CompilerParams(
            collective_id=1, has_side_effects=True, vmem_limit_bytes=VMEM_LIMIT
        ),
        name="backward",
    )(*args)


def finish_kernel(lo, gt, gq, gout, gup, gdown, small, lo_o, gt_o, gqkv_o, gout_o, gup_o, gdown_o, *vectors):
    for src, dst in ((lo, lo_o), (gt, gt_o), (gout, gout_o), (gup, gup_o), (gdown, gdown_o)):
        dst[...] = src[...]
    for part in range(3):
        gqkv_o[:, 768 * part : 768 * part + 768] = jnp.concatenate(
            [gq[q, :, 192 * part : 192 * part + 192] for q in range(4)], axis=1
        )
    for k, dst in enumerate(vectors):
        dst[...] = small[k : k + 1, : dst.shape[1]]


def finish_call(lo, gt, gq, gout, gup, gdown, small):
    f32 = jnp.float32
    here = pl.BlockSpec(memory_space=pltpu.VMEM)
    like = lambda a: jax.ShapeDtypeStruct(a.shape, a.dtype)
    wide = jax.ShapeDtypeStruct((24, 2304), f32)
    outs = [like(lo), like(gt), wide, like(gout), like(gup), like(gdown)]
    outs += [jax.ShapeDtypeStruct((1, width), f32) for width in (24,) * 6 + (96, 48)]
    return pl.pallas_call(
        finish_kernel,
        out_shape=outs,
        in_specs=[here] * 7,
        out_specs=[here] * len(outs),
        compiler_params=pltpu.CompilerParams(vmem_limit_bytes=VMEM_LIMIT),
        name="finish",
    )(lo, gt, gq, gout, gup, gdown, small)


def slab_body(
    tokens,
    segments,
    qkv_weight,
    qv_bias,
    out_weight,
    out_bias,
    attn_gain,
    attn_shift,
    up_weight,
    up_bias,
    down_weight,
    down_bias,
    ffn_gain,
    ffn_shift,
    cotangent,
):
    rows24 = jnp.stack([out_bias, attn_gain, attn_shift, down_bias, ffn_gain, ffn_shift])
    (
        layer_out,
        grad_first,
        dctx,
        gvec,
        grad_out,
        grad_up,
        grad_down,
        tok_all,
        q_all,
        k_all,
        v_all,
        o_all,
        lse_all,
        wq_all,
        idrow_all,
        idcol_all,
    ) = forward_call(
        tokens,
        cotangent,
        segments,
        qkv_weight,
        out_weight,
        up_weight,
        down_weight,
        rows24,
        up_bias.reshape(1, 96),
        qv_bias.reshape(1, 48),
    )
    lo_out, gt_out, gout_o, gup_o, gdown_o, gq_o, small = backward_call(
        dctx,
        layer_out,
        grad_first,
        grad_out.reshape(2, 2, 4, 24, 768),
        grad_up.reshape(2, 2, 4, 24, 3072),
        grad_down.reshape(2, 2, 4, 96, 768),
        gvec,
        tok_all,
        q_all,
        k_all,
        v_all,
        o_all,
        lse_all,
        wq_all,
        idrow_all,
        idcol_all,
    )
    lo_out, gt_out, gqkv, gout_o, gup_o, gdown_o, *vectors = finish_call(
        lo_out, gt_out, gq_o, gout_o, gup_o, gdown_o, small
    )
    rows = [vector.reshape(vector.shape[1]) for vector in vectors]
    return (
        lo_out,
        gt_out,
        gqkv,
        rows[7],
        gout_o,
        rows[0],
        rows[1],
        rows[2],
        gup_o,
        rows[6],
        gdown_o,
        rows[3],
        rows[4],
        rows[5],
    )


def solution(mesh):
    sizes = tuple(mesh.shape[name] for name in ("dp", "head", "blk"))
    body = slab_body if sizes == (2, 4, 4) else general_body
    placed = (
        P("dp", ("blk", "head"), None),
        P("dp", ("blk", "head")),
        P(("dp", "head", "blk"), None),
        P(("dp", "head", "blk")),
        P(("dp", "head", "blk"), None),
        P(("dp", "head", "blk")),
        P(("dp", "head", "blk")),
        P(("dp", "head", "blk")),
        P(("dp", "head", "blk"), None),
        P(("dp", "head", "blk")),
        P(("dp", "head", "blk"), None),
        P(("dp", "head", "blk")),
        P(("dp", "head", "blk")),
        P(("dp", "head", "blk")),
        P("dp", ("blk", "head"), None),
    )
    return jax.shard_map(
        body,
        mesh=mesh,
        in_specs=placed,
        out_specs=(
            P("dp", ("blk", "head"), None),
            P("dp", ("blk", "head"), None),
            P(("dp", "head", "blk"), None),
            P(("dp", "head", "blk")),
            P(("dp", "head", "blk"), None),
            P(("dp", "head", "blk")),
            P(("dp", "head", "blk")),
            P(("dp", "head", "blk")),
            P(("dp", "head", "blk"), None),
            P(("dp", "head", "blk")),
            P(("dp", "head", "blk"), None),
            P(("dp", "head", "blk")),
            P(("dp", "head", "blk")),
            P(("dp", "head", "blk")),
        ),
        check_vma=False,
    )
```

```python
import math

import jax
import jax.numpy as jnp
from jax import lax
from jax.experimental import pallas as pl
from jax.experimental.pallas import tpu as pltpu
from jax.sharding import PartitionSpec as P

HEADS = 12
HDIM = 64
NSEG = 256


EPS = 1e-12
MASKED = -1e30
SCALE = 0.125


def norm_forward(values_in, gain, shift):
    mean_val = jnp.mean(values_in, axis=-1, keepdims=True)
    centred = values_in - mean_val
    inv_std = lax.rsqrt(jnp.mean(centred * centred, axis=-1, keepdims=True) + EPS)
    normed = centred * inv_std
    return (normed * gain + shift, normed, inv_std)


def norm_backward(grad_in, normed, inv_std, gain):
    scaled = grad_in * gain
    inner_term = (
        scaled
        - jnp.mean(scaled, axis=-1, keepdims=True)
        - normed * jnp.mean(scaled * normed, axis=-1, keepdims=True)
    )
    return (inner_term * inv_std, jnp.sum(grad_in * normed, axis=0), jnp.sum(grad_in, axis=0))


def exact_gelu(values_in):
    return jax.nn.gelu(values_in, approximate=False)


def stretch_scores(queries, key_part, query_seg, key_seg, query_place, key_place):
    scores = (
        jnp.einsum("sqhd,skhd->shqk", queries, key_part, preferred_element_type=jnp.float32) * SCALE
    )
    same_doc = query_seg[:, None, :, None] == key_seg[:, None, None, :]
    own_place = query_place[:, None] == key_place[None, :]
    usable = (query_seg[:, None, :, None] != NSEG - 1) | own_place[None, None]
    return (scores, same_doc & usable)


def slice_keys(key_piece, value_piece, seg_piece, offset, step_rows):
    key_part = lax.dynamic_slice_in_dim(key_piece, offset, step_rows, 1)
    value_part = lax.dynamic_slice_in_dim(value_piece, offset, step_rows, 1)
    seg_part = lax.dynamic_slice_in_dim(seg_piece, offset, step_rows, 1)
    return (key_part, value_part, seg_part)


def part_grads(
    queries,
    grad_ctx,
    log_total,
    row_delta,
    query_seg,
    query_place,
    key_part,
    value_part,
    key_seg,
    key_place,
):
    scores, allowed = stretch_scores(queries, key_part, query_seg, key_seg, query_place, key_place)
    probs = jnp.where(allowed, jnp.exp(scores - log_total[..., None]), 0.0)
    grad_probs = jnp.einsum(
        "sqhd,skhd->shqk", grad_ctx, value_part, preferred_element_type=jnp.float32
    )
    grad_scores = (probs * (grad_probs - row_delta[..., None])).astype(jnp.bfloat16)
    grad_query = (
        jnp.einsum("shqk,skhd->sqhd", grad_scores, key_part, preferred_element_type=jnp.float32)
        * SCALE
    )
    grad_key = (
        jnp.einsum("shqk,sqhd->skhd", grad_scores, queries, preferred_element_type=jnp.float32)
        * SCALE
    )
    grad_value = jnp.einsum(
        "shqk,sqhd->skhd", probs.astype(jnp.bfloat16), grad_ctx, preferred_element_type=jnp.float32
    )
    return (grad_query, grad_key, grad_value)


def general_body(
    tokens,
    segments,
    qkv_weight,
    qv_bias,
    out_weight,
    out_bias,
    attn_gain,
    attn_shift,
    up_weight,
    up_bias,
    down_weight,
    down_bias,
    ffn_gain,
    ffn_shift,
    cotangent,
):
    seq_count, local_rows, model_width = tokens.shape
    group_count = lax.axis_size("head")
    group_width = model_width // group_count
    heads_here = HEADS // group_count
    block_rows = local_rows * group_count
    key_rows = block_rows * lax.axis_size("blk")
    token_count = seq_count * local_rows
    gathered = (
        lax.all_gather(qkv_weight, ("dp", "head", "blk"), axis=0, tiled=True),
        lax.all_gather(qv_bias, ("dp", "head", "blk"), axis=0, tiled=True),
        lax.all_gather(out_weight, ("dp", "head", "blk"), axis=0, tiled=True),
        lax.all_gather(out_bias, ("dp", "head", "blk"), axis=0, tiled=True),
        lax.all_gather(attn_gain, ("dp", "head", "blk"), axis=0, tiled=True),
        lax.all_gather(attn_shift, ("dp", "head", "blk"), axis=0, tiled=True),
        lax.all_gather(up_weight, ("dp", "head", "blk"), axis=0, tiled=True),
        lax.all_gather(up_bias, ("dp", "head", "blk"), axis=0, tiled=True),
        lax.all_gather(down_weight, ("dp", "head", "blk"), axis=0, tiled=True),
        lax.all_gather(down_bias, ("dp", "head", "blk"), axis=0, tiled=True),
        lax.all_gather(ffn_gain, ("dp", "head", "blk"), axis=0, tiled=True),
        lax.all_gather(ffn_shift, ("dp", "head", "blk"), axis=0, tiled=True),
    )
    (
        whole_qkv,
        whole_qv,
        whole_out,
        whole_out_bias,
        whole_attn_gain,
        whole_attn_shift,
        whole_up,
        whole_up_bias,
        whole_down,
        whole_down_bias,
        whole_ffn_gain,
        whole_ffn_shift,
    ) = gathered
    attn_scale = whole_attn_gain.astype(jnp.float32)
    ffn_scale = whole_ffn_gain.astype(jnp.float32)
    flat_tokens = tokens.reshape(token_count, model_width)
    mixed = jnp.dot(flat_tokens, whole_qkv, preferred_element_type=jnp.float32)
    bias_row = jnp.concatenate(
        [whole_qv[:model_width], jnp.zeros((model_width,), jnp.bfloat16), whole_qv[model_width:]]
    ).astype(jnp.float32)
    mixed_low = (mixed + bias_row).astype(jnp.bfloat16)
    grouped = (
        mixed_low.reshape(seq_count, local_rows, 3, group_count, group_width)
        .transpose(0, 1, 3, 2, 4)
        .reshape(seq_count, local_rows, group_count, 3 * group_width)
    )
    seg_copies = jnp.broadcast_to(
        segments.astype(jnp.bfloat16)[:, :, None, None], (seq_count, local_rows, group_count, 1)
    )
    arrived, seg_arrived = (
        lax.all_to_all(grouped, "head", split_axis=2, concat_axis=1, tiled=True),
        lax.all_to_all(seg_copies, "head", split_axis=2, concat_axis=1, tiled=True),
    )
    arrived = arrived.reshape(seq_count, block_rows, 3, heads_here, HDIM)
    queries = arrived[:, :, 0]
    keys_here = arrived[:, :, 1]
    values_here = arrived[:, :, 2]
    query_seg = seg_arrived.reshape(seq_count, block_rows)
    query_place = lax.axis_index("blk") * block_rows + jnp.arange(block_rows)
    row_shape = (seq_count, heads_here, block_rows)
    start_state = (
        jnp.full(row_shape, MASKED, jnp.float32),
        jnp.zeros(row_shape, jnp.float32),
        jnp.zeros(row_shape + (HDIM,), jnp.float32),
    )
    key_piece = lax.all_gather(keys_here, "blk", axis=1, tiled=True)
    value_piece = lax.all_gather(values_here, "blk", axis=1, tiled=True)
    seg_piece = lax.all_gather(query_seg, "blk", axis=1, tiled=True)
    piece_rows = key_piece.shape[1]
    step_rows = math.gcd(piece_rows, 512)

    def attend_one_step(state_in, step_index):
        offset = step_index * step_rows
        key_part, value_part, key_seg = slice_keys(
            key_piece, value_piece, seg_piece, offset, step_rows
        )
        key_place = offset + jnp.arange(step_rows)
        best, total, accum = state_in
        scores, allowed = stretch_scores(
            queries, key_part, query_seg, key_seg, query_place, key_place
        )
        new_best = jnp.maximum(best, jnp.max(jnp.where(allowed, scores, MASKED), axis=-1))
        weights = jnp.where(allowed, jnp.exp(scores - new_best[..., None]), 0.0)
        factor = jnp.exp(best - new_best)
        total = total * factor + jnp.sum(weights, axis=-1)
        accum = accum * factor[..., None] + jnp.einsum(
            "shqk,skhd->shqd",
            weights.astype(jnp.bfloat16),
            value_part,
            preferred_element_type=jnp.float32,
        )
        return ((new_best, total, accum), None)

    result, unused = lax.scan(attend_one_step, start_state, jnp.arange(piece_rows // step_rows))
    best, total, accum = result
    context = accum / total[..., None]
    log_total = best + jnp.log(total)
    context_low = (
        context.astype(jnp.bfloat16)
        .transpose(0, 2, 1, 3)
        .reshape(seq_count, block_rows, 1, group_width)
    )
    returned_ctx = lax.all_to_all(context_low, "head", split_axis=1, concat_axis=2, tiled=True)
    ctx_tokens = returned_ctx.reshape(token_count, model_width)
    attended = jnp.dot(
        ctx_tokens, whole_out, preferred_element_type=jnp.float32
    ) + whole_out_bias.astype(jnp.float32)
    first_sum = flat_tokens.astype(jnp.float32) + attended
    hidden, normed_one, inv_one = norm_forward(
        first_sum, attn_scale, whole_attn_shift.astype(jnp.float32)
    )
    hidden_low = hidden.astype(jnp.bfloat16)
    inner = jnp.dot(
        hidden_low, whole_up, preferred_element_type=jnp.float32
    ) + whole_up_bias.astype(jnp.float32)
    active, gelu_pull = jax.vjp(exact_gelu, inner)
    active_low = active.astype(jnp.bfloat16)
    branch = jnp.dot(
        active_low, whole_down, preferred_element_type=jnp.float32
    ) + whole_down_bias.astype(jnp.float32)
    final, normed_two, inv_two = norm_forward(
        hidden + branch, ffn_scale, whole_ffn_shift.astype(jnp.float32)
    )
    layer_out = final.astype(jnp.bfloat16).reshape(seq_count, local_rows, model_width)
    grad_final = cotangent.reshape(token_count, model_width).astype(jnp.float32)
    grad_second, grad_ffn_gain, grad_ffn_shift = norm_backward(
        grad_final, normed_two, inv_two, ffn_scale
    )
    grad_branch = grad_second.astype(jnp.bfloat16)
    grad_down = jnp.dot(active_low.T, grad_branch, preferred_element_type=jnp.float32)
    grad_down_bias = jnp.sum(grad_branch.astype(jnp.float32), axis=0)
    grad_active = jnp.dot(grad_branch, whole_down.T, preferred_element_type=jnp.float32)
    grad_inner = gelu_pull(grad_active)[0].astype(jnp.bfloat16)
    grad_up = jnp.dot(hidden_low.T, grad_inner, preferred_element_type=jnp.float32)
    grad_up_bias = jnp.sum(grad_inner.astype(jnp.float32), axis=0)
    grad_hidden = grad_second + jnp.dot(grad_inner, whole_up.T, preferred_element_type=jnp.float32)
    grad_first, grad_attn_gain, grad_attn_shift = norm_backward(
        grad_hidden, normed_one, inv_one, attn_scale
    )
    grad_attended = grad_first.astype(jnp.bfloat16)
    grad_out = jnp.dot(ctx_tokens.T, grad_attended, preferred_element_type=jnp.float32)
    grad_out_bias = jnp.sum(grad_attended.astype(jnp.float32), axis=0)
    grad_context = jnp.dot(grad_attended, whole_out.T, preferred_element_type=jnp.float32).astype(
        jnp.bfloat16
    )
    grad_sent = lax.all_to_all(
        grad_context.reshape(seq_count, local_rows, group_count, group_width),
        "head",
        split_axis=2,
        concat_axis=1,
        tiled=True,
    )
    grad_ctx = grad_sent.reshape(seq_count, block_rows, heads_here, HDIM)
    row_delta = jnp.einsum("sqhd,shqd->shq", grad_ctx.astype(jnp.float32), context)
    query_zero = jnp.zeros((seq_count, block_rows, heads_here, HDIM), jnp.float32)
    zero_keys = jnp.zeros((seq_count, key_rows, heads_here, HDIM), jnp.float32)
    gather_key_piece = lax.all_gather(keys_here, "blk", axis=1, tiled=True)
    gather_value_piece = lax.all_gather(values_here, "blk", axis=1, tiled=True)
    gather_seg_piece = lax.all_gather(query_seg, "blk", axis=1, tiled=True)
    piece_rows = gather_key_piece.shape[1]
    gather_step_rows = math.gcd(piece_rows, 512)

    def gather_one_step(state_in, step_index):
        offset = step_index * gather_step_rows
        key_part, value_part, key_seg = slice_keys(
            gather_key_piece, gather_value_piece, gather_seg_piece, offset, gather_step_rows
        )
        key_place = offset + jnp.arange(gather_step_rows)
        grad_q, grad_k, grad_v = state_in
        part_q, part_k, part_v = part_grads(
            queries,
            grad_ctx,
            log_total,
            row_delta,
            query_seg,
            query_place,
            key_part,
            value_part,
            key_seg,
            key_place,
        )
        grad_k = lax.dynamic_update_slice_in_dim(
            grad_k,
            lax.dynamic_slice_in_dim(grad_k, offset, gather_step_rows, 1) + part_k,
            offset,
            1,
        )
        grad_v = lax.dynamic_update_slice_in_dim(
            grad_v,
            lax.dynamic_slice_in_dim(grad_v, offset, gather_step_rows, 1) + part_v,
            offset,
            1,
        )
        return ((grad_q + part_q, grad_k, grad_v), None)

    result, unused = lax.scan(
        gather_one_step,
        (query_zero, zero_keys, zero_keys),
        jnp.arange(piece_rows // gather_step_rows),
    )
    grad_q, all_keys, all_values = result
    grad_k, grad_v = (
        lax.psum_scatter(
            all_keys.astype(jnp.bfloat16), "blk", scatter_dimension=1, tiled=True
        ).astype(jnp.float32),
        lax.psum_scatter(
            all_values.astype(jnp.bfloat16), "blk", scatter_dimension=1, tiled=True
        ).astype(jnp.float32),
    )
    grad_low = jnp.concatenate(
        [
            grad_q.astype(jnp.bfloat16).reshape(seq_count, block_rows, 1, group_width),
            grad_k.astype(jnp.bfloat16).reshape(seq_count, block_rows, 1, group_width),
            grad_v.astype(jnp.bfloat16).reshape(seq_count, block_rows, 1, group_width),
        ],
        axis=3,
    )
    back_tokens = lax.all_to_all(grad_low, "head", split_axis=1, concat_axis=2, tiled=True)
    grad_mixed = (
        back_tokens.reshape(seq_count, local_rows, group_count, 3, group_width)
        .transpose(0, 1, 3, 2, 4)
        .reshape(token_count, 3 * model_width)
    )
    grad_qkv = jnp.dot(flat_tokens.T, grad_mixed, preferred_element_type=jnp.float32)
    column_sums = jnp.sum(grad_mixed.astype(jnp.float32), axis=0)
    grad_qv = jnp.concatenate([column_sums[:model_width], column_sums[2 * model_width :]])
    grad_tokens = grad_first + jnp.dot(grad_mixed, whole_qkv.T, preferred_element_type=jnp.float32)
    summed = (
        lax.psum_scatter(grad_qkv, ("dp", "head", "blk"), scatter_dimension=0, tiled=True),
        lax.psum_scatter(grad_qv, ("dp", "head", "blk"), scatter_dimension=0, tiled=True),
        lax.psum_scatter(grad_out, ("dp", "head", "blk"), scatter_dimension=0, tiled=True),
        lax.psum_scatter(grad_out_bias, ("dp", "head", "blk"), scatter_dimension=0, tiled=True),
        lax.psum_scatter(grad_attn_gain, ("dp", "head", "blk"), scatter_dimension=0, tiled=True),
        lax.psum_scatter(grad_attn_shift, ("dp", "head", "blk"), scatter_dimension=0, tiled=True),
        lax.psum_scatter(grad_up, ("dp", "head", "blk"), scatter_dimension=0, tiled=True),
        lax.psum_scatter(grad_up_bias, ("dp", "head", "blk"), scatter_dimension=0, tiled=True),
        lax.psum_scatter(grad_down, ("dp", "head", "blk"), scatter_dimension=0, tiled=True),
        lax.psum_scatter(grad_down_bias, ("dp", "head", "blk"), scatter_dimension=0, tiled=True),
        lax.psum_scatter(grad_ffn_gain, ("dp", "head", "blk"), scatter_dimension=0, tiled=True),
        lax.psum_scatter(grad_ffn_shift, ("dp", "head", "blk"), scatter_dimension=0, tiled=True),
    )
    return (
        layer_out,
        grad_tokens.reshape(seq_count, local_rows, model_width),
        summed[0],
        summed[1],
        summed[2],
        summed[3],
        summed[4],
        summed[5],
        summed[6],
        summed[7],
        summed[8],
        summed[9],
        summed[10],
        summed[11],
    )


MESH = pl.DeviceIdType.MESH
ANY = pl.ANY
VMEM_LIMIT = 60 * 1024 * 1024


def remote(src, dst, send_sem, recv_sem, device):
    return pltpu.make_async_remote_copy(
        src_ref=src,
        dst_ref=dst,
        send_sem=send_sem,
        recv_sem=recv_sem,
        device_id=device,
        device_id_type=MESH,
    )


def wait_for(ref, sem):
    pltpu.make_async_copy(ref, ref, sem).wait()


def place():
    x, h, z = lax.axis_index("dp"), lax.axis_index("head"), lax.axis_index("blk")
    return x, lax.div(h, 2), lax.rem(h, 2), h, z


def greet(peers):
    barrier = pltpu.get_barrier_semaphore()
    for peer in peers:
        pl.semaphore_signal(barrier, inc=1, device_id=peer, device_id_type=MESH)
    pl.semaphore_wait(barrier, len(peers))


def peers_of(x, h, c, z):
    around = [(x, h, lax.rem(z + k, 4)) for k in (1, 2, 3)]
    other = lax.rem(h + 2, 4)
    beside = z + 1 - 2 * lax.rem(z, 2)
    return around + [(1 - x, h, z), (x, other, z), (x, other, beside), (x, h + 1 - 2 * c, z)]


def nt(left, right):
    return lax.dot_general(left, right, (((1,), (1,)), ((), ())), preferred_element_type=jnp.float32)


def tn(left, right):
    return lax.dot_general(left, right, (((0,), (0,)), ((), ())), preferred_element_type=jnp.float32)


def nn(left, right):
    return jnp.dot(left, right, preferred_element_type=jnp.float32)


def add_norm(values_in):
    mean_val = jnp.mean(values_in, axis=-1, keepdims=True)
    centred = values_in - mean_val
    inv_std = lax.rsqrt(jnp.mean(centred * centred, axis=-1, keepdims=True) + EPS)
    return centred * inv_std, inv_std


def norm_pull(scaled, normed, inv_std):
    return inv_std * (
        scaled
        - jnp.mean(scaled, axis=-1, keepdims=True)
        - normed * jnp.mean(scaled * normed, axis=-1, keepdims=True)
    )


def column_sum(values_in):
    return jnp.sum(values_in, axis=0, keepdims=True)


CUT = 1
EARLY = 0
AHEAD = 2
BESIDE_TOKENS = {
    99: ((0, 0), (0, 1)),
    100: ((1, 0),),
    101: ((1, 1), (1, 2)),
    102: ((1, 3),),
    104: ((1, 4),),
    111: ((1, 5),),
    112: ((1, 6),),
}
WQ_STEPS = (4, 5, 8)
SUB = 2
ROWS_SUB = 64
PIECES = (
    ("out", (24, 768), 0, 0),
    ("up", (24, 1536), 0, 0),
    ("up", (24, 1536), 0, 1536),
    ("down", (48, 768), 0, 0),
    ("down", (48, 768), 48, 0),
)


def forward_kernel(
    tokens,
    cot,
    segments,
    wqkv,
    wout,
    wup,
    wdown,
    rows24,
    up_bias,
    qv_bias,
    dr1,
    gvec,
    lo_out,
    dc_all,
    gout_h,
    gup_h,
    gdown_h,
    tok_all,
    q_all,
    k_all,
    v_all,
    o_all,
    lse_all,
    wq_all,
    idrow_all,
    idcol_all,
    tok,
    land,
    wqs,
    qs,
    ks,
    vs,
    os_,
    lses,
    idrow,
    idcol,
    ctx,
    wout_g,
    wup_g,
    wdown_g,
    win,
    ctx_in,
    cot_in,
    wout_v,
    wup_v,
    active,
    slope,
    go,
    gu,
    gd,
    ro,
    ru,
    rd,
    tok_rs,
    tz_ss,
    tx_ss,
    ty_ss,
    tc_ss,
    cot_ss,
    cot_rs,
    wq_ss,
    wq_rs,
    wz_ss,
    wz_rs,
    wp_ss,
    wp_rs,
    ctx_ss,
    ctx_rs,
    out_sem,
    c_ss,
    c_rs,
    o_sem,
    wq,
    lo,
    dctx,
    r2a,
    r2b,
    lo_ss,
    lo_rs,
    dc_ss,
    dc_rs,
    s2_ss,
    s2_rs,
):
    f32, bf = jnp.float32, jnp.bfloat16
    x, y, c, h, z = place()
    zl, pi = lax.rem(z, 2), lax.div(z, 2)
    g = 2 * zl + y
    me = x * 16 + h * 4 + z
    hy = lax.rem(h + 2, 4)
    hc = h + 1 - 2 * c
    to_x, to_y, to_c = (1 - x, h, z), (x, hy, z), (x, hc, z)
    pz, zc = z + 1 - 2 * zl, lax.rem(z + 2, 4)
    to_n, to_d, to_z = (x, h, pz), (x, hy, pz), (x, h, zc)
    mid = jnp.where(z < 2, 2, 1)
    inner = jnp.logical_or(z == 1, z == 2)
    outer = jnp.logical_not(inner)
    def moved(values, width, steps, index):
        out = None
        for k, start in enumerate(steps):
            ends = []
            if start:
                ends.append(jnp.zeros((values.shape[0], start), f32))
            ends.append(values)
            if width - start - values.shape[1]:
                ends.append(jnp.zeros((values.shape[0], width - start - values.shape[1]), f32))
            row = jnp.concatenate(ends, axis=1)
            out = row if out is None else jnp.where(index == k, row, out)
        return out

    starts = [48 * k for k in range(4)] + [384 + 48 * k for k in range(4)]
    bias_row = moved(qv_bias[...].astype(f32), 576, starts, 4 * x + z)
    six = moved(rows24[...].astype(f32), 128, [24 * k for k in range(4)], z)
    up_row = jnp.concatenate([up_bias[...].astype(f32), jnp.zeros((1, 32), f32)], axis=1)
    ten = [six[k : k + 1] for k in range(6)] + [jnp.where(z == k, up_row, 0.0) for k in range(4)]
    gap = jnp.zeros((1, 64), f32)
    none = jnp.zeros((1, 128), f32)
    slots = [
        jnp.concatenate(ten[0:4] + [gap], axis=1),
        jnp.concatenate(ten[4:8] + [gap], axis=1),
        jnp.concatenate(ten[8:10] + [none, none, gap], axis=1),
    ]
    seg_rows = segments[...].astype(f32)
    seg_rows = [jnp.concatenate([seg_rows[k : k + 1], jnp.zeros((1, 448), f32)], axis=1) for k in range(2)]
    last_rows = jnp.concatenate(slots + seg_rows + [jnp.zeros((2, 576), f32)], axis=0)
    whole = wqkv[...].astype(f32)
    for q in range(4):
        cols = [whole[:, 768 * p + 192 * q : 768 * p + 192 * q + 192] for p in range(3)]
        first_row = jnp.where(h == q, bias_row, 0.0)
        rows = [jnp.concatenate(cols, axis=1), first_row, last_rows]
        wq[q] = jnp.concatenate(rows, axis=0).astype(bf)
    greet(peers_of(x, h, c, z))

    mine = z * 4 + h
    weights = {"out": (wout, wout_g), "up": (wup, wup_g), "down": (wdown, wdown_g)}
    count = len(PIECES)
    base = x * 16 + h * 4
    bx, by = (1 - x) * 16 + h * 4, x * 16 + hy * 4

    def side(start, ab):
        return pl.ds(start, CUT) if ab == 0 else pl.ds(start + CUT, 4 - CUT)

    sa, sb = side(bx, 0), side(by, 1)

    def quad(xs, hs):
        return pl.ds(xs * 16 + hs * 4, 4)

    sent = []

    def shard(n):
        name, shape, row, col = PIECES[n]
        return weights[name][0].at[pl.ds(row, shape[0]), pl.ds(col, shape[1])]

    def at(n, where):
        name, shape, row, col = PIECES[n]
        return weights[name][1].at[where, pl.ds(row, shape[0]), pl.ds(col, shape[1])]

    def two(n):
        return at(n, pl.ds(0, 2))

    def some(n, ab):
        return at(n, side(0, ab))

    def pass_on(n, where, k, sem, dev):
        remote(at(n, where), at(n, where), wp_ss.at[n, k], wp_rs.at[(n,) + sem], dev).start()
        sent.append((n, k))

    def along_z(n):
        pltpu.make_async_copy(shard(n), at(n, me), wz_rs.at[n, z]).start()
        for k, zz in enumerate((pz, mid)):
            remote(shard(n), at(n, me), wz_ss.at[n, k], wz_rs.at[n, z], (x, h, zz)).start()

    def relay(n):
        @pl.when(inner)
        def _():
            there = pl.ds(base + jnp.where(z < 2, 2, 0), 2)
            for k in range(2):
                wait_for(at(n, 0), wz_rs.at[n, jnp.where(z < 2, 2, 0) + k])
            remote(at(n, there), at(n, there), wz_ss.at[n, 2], wz_rs.at[n, 4], (x, h, pz)).start()

    def first_hop(n):
        for k in range(2):
            wait_for(at(n, 0), wz_rs.at[n, jnp.where(z < 2, 0, 2) + k])

        @pl.when(outer)
        def _():
            wait_for(two(n), wz_rs.at[n, 4])

        for k, dev in enumerate((to_x, to_y, to_c)):
            pass_on(n, quad(x, h), k, (x, h, 0), dev)

    def second_hop(n):
        wait_for(at(n, quad(0, 0)), wp_rs.at[n, 1 - x, h, 0])
        wait_for(at(n, quad(0, 0)), wp_rs.at[n, x, hy, 0])
        pass_on(n, sa, 3, (1 - x, h, 0), to_y)
        pass_on(n, sb, 4, (x, hy, 1), to_x)
        pass_on(n, quad(1 - x, h), 5, (1 - x, h, 0), to_c)
        pass_on(n, quad(x, hy), 6, (x, hy, 0), to_c)

    def third_hop(n):
        for ab in range(2):
            wait_for(some(n, ab), wp_rs.at[n, 1 - x, hy, ab])
        pass_on(n, quad(1 - x, hy), 7, (1 - x, hy, 0), to_c)

    def advance(t):
        if t < count:
            first_hop(t)
        if t + AHEAD < count:
            relay(t + AHEAD)
        if 0 <= t - 1 < count:
            second_hop(t - 1)
        if 0 <= t - 2 < count:
            third_hop(t - 2)

    for n in range(EARLY):
        along_z(n)

    cuts = [pl.ds(ROWS_SUB * q, ROWS_SUB) for q in range(SUB)]

    def send_row(i, to):
        for q in range(SUB):
            remote(
                tokens.at[i, cuts[q]], tok.at[mine, cuts[q]], tz_ss.at[i, q], tok_rs.at[mine, q], to
            ).start()

    for i in range(2):

        @pl.when(pi == i)
        def _():
            send_row(i, to_n)
            for q in range(SUB):
                pltpu.make_async_copy(
                    tokens.at[i, cuts[q]], tok.at[mine, cuts[q]], tok_rs.at[mine, q]
                ).start()

        @pl.when(pi != i)
        def _():
            send_row(i, (x, h, 1 + i))

    def run_beside(t):
        for kind, n in BESIDE_TOKENS.get(t, ()):
            relay(n) if kind == 0 else advance(n)

    pltpu.make_async_copy(wq.at[g], land.at[c, x, pi, g], wq_rs.at[c, x, pi, g]).start()
    for k, (dev, target) in enumerate(
        ((to_n, 2 * (1 - zl) + y), (to_y, 2 * zl + 1 - y), (to_d, 2 * (1 - zl) + 1 - y))
    ):
        remote(wq.at[target], land.at[c, x, pi, g], wq_ss.at[k], wq_rs.at[c, x, pi, g], dev).start()

    def give_slices(xs, pp, k, dev):
        block = land.at[c, xs, pp]
        remote(block, block, wq_ss.at[k], wq_rs.at[c, xs, pp, 0], dev).start()

    for q in range(4):
        wait_for(land.at[c, x, pi, q], wq_rs.at[c, x, pi, q])
    give_slices(x, pi, 3, to_z)
    give_slices(x, pi, 4, to_x)
    give_slices(x, pi, 5, to_c)
    for n in range(EARLY, count):
        along_z(n)
    for i in range(2):

        @pl.when(pi == i)
        def _():
            pltpu.make_async_copy(cot.at[i], cot_in.at[pi], cot_rs.at[pi]).start()

        @pl.when(pi != i)
        def _():
            remote(cot.at[i], cot_in.at[pi], cot_ss, cot_rs.at[pi], to_z).start()

    turns = (z, pz, zc, lax.rem(pz + 2, 4))

    def hand_on(p, q, sends, keep_sem):
        wait_for(tok.at[p, cuts[q]], tok_rs.at[p, q])
        for sem, dev in sends:
            remote(tok.at[p, cuts[q]], tok.at[p, cuts[q]], sem.at[q], tok_rs.at[p, q], dev).start()
        if q == SUB - 1:
            remote(tok.at[p], tok.at[p], keep_sem, tok_rs.at[p, 0], to_c).start()

    def own_piece(k, q):
        p = turns[k] * 4 + h
        hand_on(p, q, [(ty_ss.at[k], to_y)], tc_ss.at[k])
        if k >= 2:

            @pl.when(inner)
            def _():
                cut = cuts[q]
                remote(
                    tok.at[p, cut], tok.at[p, cut], tx_ss.at[k, q], tok_rs.at[p, q], to_n
                ).start()

    def side_piece(k, q):
        hand_on(turns[k] * 4 + hy, q, [], tc_ss.at[4 + k])

    def slices_step(t):
        if t == WQ_STEPS[0]:
            wait_for(land.at[c, x, 1 - pi], wq_rs.at[c, x, 1 - pi, 0])
            give_slices(x, 1 - pi, 6, to_x)
            give_slices(x, 1 - pi, 7, to_c)
        for k in range(2):
            if t == WQ_STEPS[1 + k]:
                there = (pi, 1 - pi)[k]
                wait_for(land.at[c, 1 - x, there], wq_rs.at[c, 1 - x, there, 0])
                give_slices(1 - x, there, 8 + k, to_c)

    order = [(0, q) for q in range(SUB)] + [(k, q) for q in range(SUB) for k in range(1, 4)]
    lag = 3
    for t in range(len(order) + lag):
        if t < len(order):
            own_piece(*order[t])
        if t >= lag:
            side_piece(*order[t - lag])
        slices_step(t)
        run_beside(t)

    run_beside(99)
    for k in range(4):
        zz = lax.rem(z + k, 4)
        for hh in (hc, lax.rem(hc + 2, 4)):
            p = zz * 4 + hh
            wait_for(tok.at[p], tok_rs.at[p, 0])
    for k in range(4):
        wait_for(land.at[1 - c, k // 2, k % 2], wq_rs.at[1 - c, k // 2, k % 2, 0])

    run_beside(100)
    bias8 = jnp.zeros((8, 576), jnp.float32)
    for xs in range(2):
        for hs in range(4):
            part = []
            window = jnp.zeros((8, 576), jnp.float32)
            for zz in range(4):
                block = land[hs % 2, xs, zz // 2, 2 * (zz % 2) + hs // 2].astype(jnp.float32)
                part.append(block[:24])
                window = window + block[24:]
            start = (xs * 16 + hs * 4) * 24
            bias8 = bias8 + window
            win[xs * 4 + hs] = window
            wqs[start : start + 96, :] = jnp.concatenate(part, axis=0).astype(jnp.bfloat16)
    bias = bias8[0:1, :]

    lane = lax.broadcasted_iota(jnp.int32, (1, 128), 1)
    for p in range(16):
        zz, hs = p // 4, p % 4
        block = land[hs % 2, x, zz // 2, 2 * (zz % 2) + hs // 2].astype(jnp.float32)
        seg = jnp.where(pi == 0, block[28:29, :128], block[29:30, :128])
        ident = jnp.where(seg == NSEG - 1.0, (1000.0 + 128 * p) + lane.astype(f32), seg)
        idrow[:, 128 * p : 128 * p + 128] = jnp.broadcast_to(ident, (8, 128))
        idcol[128 * p : 128 * p + 128, :] = jnp.transpose(jnp.broadcast_to(ident, (128, 128)))

    def project(j, carry):
        zz, yy = lax.div(j, 2), lax.rem(j, 2)
        p = zz * 4 + yy * 2 + c
        rows = pl.ds(pl.multiple_of(j * 128, 128), 128)
        mixed = nn(tok[p], wqs[:, 0:192]) + bias[:, 0:192]
        low = mixed.astype(jnp.bfloat16) * jnp.bfloat16(SCALE)
        for hh in range(3):
            qs[hh, rows, :] = low[:, 64 * hh : 64 * hh + 64]
        both = tok[pl.ds(2 * j, 2)].reshape(256, 768)
        wide = nn(both, wqs[:, 192:576]) + bias[:, 192:576]
        wide = wide.astype(jnp.bfloat16)
        key_rows = pl.ds(pl.multiple_of(j * 256, 256), 256)
        for hh in range(3):
            ks[hh, key_rows, :] = wide[:, 64 * hh : 64 * hh + 64]
            vs[hh, key_rows, :] = wide[:, 192 + 64 * hh : 256 + 64 * hh]
        return carry

    lax.fori_loop(0, 8, project, 0)
    run_beside(101)

    def attend(zz):
        rows = slice(zz * 256, zz * 256 + 256)
        upper = pl.ds(pl.multiple_of((zz * 4 + c) * 128, 128), 128)
        lower = pl.ds(pl.multiple_of((zz * 4 + 2 + c) * 128, 128), 128)
        idq = jnp.concatenate([idcol[upper, :], idcol[lower, :]], axis=0)
        mask = idq[:, 0:1] == idrow[0:1, :]
        def one_head(hh, carry):
            scores = nt(qs[hh, rows, :], ks[hh])
            scores = jnp.where(mask, scores, MASKED)
            top = jnp.max(scores, axis=-1, keepdims=True)
            weights_ = jnp.exp(scores - top)
            total = jnp.sum(weights_, axis=-1, keepdims=True)
            o = nn(weights_.astype(jnp.bfloat16), vs[hh]) / total
            os_[hh, rows, :] = o
            lse = jnp.broadcast_to(top + jnp.log(total), (256, 128))
            lses[hh, :, rows] = jnp.transpose(lse)[0:8, :]
            return carry

        lax.fori_loop(0, 3, one_head, 0)
        out = jnp.concatenate([os_[k, rows, :] for k in range(3)], axis=1).astype(jnp.bfloat16)
        slot = zz // 2
        for yy in range(2):
            j = zz * 2 + yy
            ctx[j] = out[128 * yy : 128 * yy + 128]
            stay = jnp.logical_and(zl == zz % 2, y == yy)

            @pl.when(stay)
            def _():
                pltpu.make_async_copy(ctx.at[j], ctx_in.at[g, slot], ctx_rs.at[g, slot]).start()

            @pl.when(jnp.logical_not(stay))
            def _():
                remote(
                    ctx.at[j],
                    ctx_in.at[g, slot],
                    ctx_ss.at[j],
                    ctx_rs.at[g, slot],
                    (x, yy * 2 + c, 2 * pi + zz % 2),
                ).start()

    for t in range(4):
        attend(t)
        run_beside(102 + t)

    kept = (
        (tok, tok_all),
        (qs, q_all),
        (ks, k_all),
        (vs, v_all),
        (os_, o_all),
        (lses, lse_all),
        (wqs, wq_all),
        (idrow, idrow_all),
        (idcol, idcol_all),
    )
    for k, (src, dst) in enumerate(kept):
        pltpu.make_async_copy(src, dst, out_sem.at[k]).start()
    def arrive(n):
        for xs in range(2):
            for yy in range(2):
                wait_for(at(n, quad(0, 0)), wp_rs.at[n, xs, yy * 2 + 1 - c, 0])

    def flatten(src, dst, cols):
        for k in range(8):
            part = [src[4 * k + q, :, cols].astype(f32) for q in range(4)]
            dst[96 * k : 96 * k + 96, cols] = jnp.concatenate(part, axis=0).astype(bf)

    run_beside(110)
    for s in range(2):
        wait_for(cot_in.at[s], cot_rs.at[s])
        for q in range(4):
            wait_for(ctx_in.at[q, s], ctx_rs.at[q, s])
    arrive(0)
    def row(i):
        at_lane = 128 * (i % 4) if i < 6 else 0
        if i < 6:
            pieces = [win[w, 1 + i // 4 : 2 + i // 4, at_lane : at_lane + 96] for w in range(8)]
        else:
            pieces = []
            for w in (2 * (i - 6), 2 * (i - 6) + 1):
                for k in range(6, 10):
                    at_lane = 128 * (k % 4)
                    pieces.append(win[w, 1 + k // 4 : 2 + k // 4, at_lane : at_lane + 96])
        return jnp.concatenate(pieces, axis=1)

    full_ctx = jnp.concatenate([ctx_in[q].reshape(256, 192) for q in range(4)], axis=1)
    flatten(wout_g, wout_v, slice(0, 768))
    own = jnp.concatenate([tok[zl * 4 + h], tok[(2 + zl) * 4 + h]], axis=0).astype(f32)
    normed_one, inv_one = add_norm(own + nn(full_ctx, wout_v[...]) + row(0))
    hidden = normed_one * row(1) + row(2)
    hidden_low = hidden.astype(bf)
    run_beside(111)
    for k in range(4):
        cols = slice(768 * k, 768 * k + 768)
        if k % 2 == 0:
            arrive(1 + k // 2)
        flatten(wup_g, wup_v, cols)
        raised = nn(hidden_low, wup_v[:, cols]) + row(6 + k)
        normal = 0.5 + 0.5 * lax.erf(raised * (0.5**0.5))
        active[:, cols] = (raised * normal).astype(bf)
        slope[:, cols] = normal + raised * jnp.exp(-0.5 * raised * raised) * (0.5 / math.pi) ** 0.5
    run_beside(112)
    for n in (3, 4):
        arrive(n)
    branch = nn(active[...], wdown_g[...].reshape(3072, 768)) + row(3)
    normed_two, inv_two = add_norm(hidden + branch)
    lo[...] = (normed_two * row(4) + row(5)).astype(bf).reshape(2, 128, 768)
    for k in range(2):

        @pl.when(pi == k)
        def _():
            pltpu.make_async_copy(lo.at[k], lo_out.at[pi], lo_rs.at[pi]).start()

        @pl.when(pi != k)
        def _():
            remote(lo.at[k], lo_out.at[pi], lo_ss, lo_rs.at[pi], to_z).start()

    grad = cot_in[...].reshape(256, 768).astype(f32)
    gvec[4:5, :] = column_sum(grad * normed_two)
    gvec[5:6, :] = column_sum(grad)
    grad_second = norm_pull(grad * row(4), normed_two, inv_two)
    grad_branch = grad_second.astype(bf)
    gvec[3:4, :] = column_sum(grad_branch.astype(f32))

    def halves(n, full, back, rows, part):
        def at(xs, ys, core):
            start = (xs * 16 + (ys * 2 + core) * 4) * (rows // 4)
            return pl.ds(pl.multiple_of(start, rows // 4 * 4), rows)

        for xs in range(2):
            for ys in range(2):
                remote(
                    full.at[at(xs, ys, 1 - c), part],
                    back.at[xs, ys, :, part],
                    c_ss.at[n, xs, ys],
                    c_rs.at[n, xs, ys],
                    to_c,
                ).start()

    def settle(full, back, rows, out, sems, base, parts):
        for xs in range(2):
            for ys in range(2):
                for n, part in parts:
                    wait_for(back.at[xs, ys, :, part], c_rs.at[n, xs, ys])

                def body(t, carry):
                    rel = pl.multiple_of(t * 16, 16)
                    start = (xs * 16 + (ys * 2 + c) * 4) * (rows // 4)
                    mine = full[pl.ds(pl.multiple_of(start + rel, 16), 16), :].astype(f32)
                    there = pl.ds(rel, 16)
                    back[xs, ys, there, :] = (
                        mine + back[xs, ys, there, :].astype(f32)
                    ).astype(bf)
                    return carry

                lax.fori_loop(0, rows // 16, body, 0)
                if out is not None:
                    k = base + xs * 2 + ys
                    pltpu.make_async_copy(back.at[xs, ys], out.at[xs, ys], sems.at[k]).start()

    def spread_down():
        settle(gd, rd, 384, None, o_sem, 0, [(0, pl.ds(0, 768))])
        for k in range(2):
            remote(
                rd.at[k, 1 - y, pl.ds(0, 192)], r2a.at[k], s2_ss.at[k], s2_rs.at[k], to_y
            ).start()
            remote(
                rd.at[1 - x, k, pl.ds(192, 192)], r2b.at[k], s2_ss.at[2 + k], s2_rs.at[2 + k], to_x
            ).start()

    def collect_down():
        for k in range(2):
            wait_for(r2a.at[k], s2_rs.at[k])
            wait_for(r2b.at[k], s2_rs.at[2 + k])

        def body(t, carry):
            k, rel = lax.div(t, 12), pl.multiple_of(lax.rem(t, 12) * 16, 16)
            a, b = pl.ds(rel, 16), pl.ds(pl.multiple_of(rel + 192, 16), 16)
            rd[k, y, a, :] = (rd[k, y, a, :].astype(f32) + r2a[k, a, :].astype(f32)).astype(bf)
            rd[x, k, b, :] = (rd[x, k, b, :].astype(f32) + r2b[k, a, :].astype(f32)).astype(bf)
            return carry

        lax.fori_loop(0, 24, body, 0)
        for k in range(2):
            wait_for(r2a.at[k], s2_ss.at[k])
            wait_for(r2b.at[k], s2_ss.at[2 + k])
        for k in range(4):
            xs, ys = k // 2, k % 2
            pltpu.make_async_copy(rd.at[xs, ys], gdown_h.at[xs, ys], o_sem.at[k]).start()

    for k in range(4):
        rows = slice(768 * k, 768 * k + 768)
        gd[rows, :] = tn(active[:, rows], grad_branch).astype(bf)
    halves(0, gd, rd, 384, pl.ds(0, 768))
    for k in range(4):
        cols = slice(768 * k, 768 * k + 768)
        pulled = (nt(grad_branch, wdown_g[8 * k : 8 * k + 8].reshape(768, 768)) * slope[:, cols]).astype(bf)
        active[:, cols] = pulled
        gvec[6 + k : 7 + k, :] = column_sum(pulled.astype(f32))
        gu[:, cols] = tn(hidden_low, pulled).astype(bf)
        halves(1 + k, gu, ru, 96, pl.ds(768 * k, 768))
        if k == 1:
            spread_down()
    grad_hidden = grad_second + nt(active[...], wup_v[...])
    gvec[1:2, :] = column_sum(grad_hidden * normed_one)
    gvec[2:3, :] = column_sum(grad_hidden)
    grad_first = norm_pull(grad_hidden * row(1), normed_one, inv_one)
    dr1[...] = grad_first.reshape(2, 128, 768)
    grad_attended = grad_first.astype(bf)
    gvec[0:1, :] = column_sum(grad_attended.astype(f32))
    gvec[10:16, :] = jnp.zeros((6, 768), f32)
    go[...] = tn(full_ctx, grad_attended).astype(bf)
    halves(5, go, ro, 96, pl.ds(0, 768))
    back = nt(grad_attended, wout_v[...]).astype(bf)
    for q in range(4):
        dctx[q] = back[:, 192 * q : 192 * q + 192].reshape(2, 128, 192)

    for t in range(2):
        j = (2 * t + zl) * 2 + y
        for k, (dev, target) in enumerate(
            ((to_n, 2 * (1 - zl) + y), (to_y, 2 * zl + 1 - y), (to_d, 2 * (1 - zl) + 1 - y))
        ):
            remote(dctx.at[target, t], dc_all.at[j], dc_ss.at[t, k], dc_rs.at[j], dev).start()
        pltpu.make_async_copy(dctx.at[g, t], dc_all.at[j], dc_rs.at[j]).start()

    settle(gu, ru, 96, gup_h, o_sem, 4, [(1 + k, pl.ds(768 * k, 768)) for k in range(4)])
    settle(go, ro, 96, gout_h, o_sem, 8, [(5, pl.ds(0, 768))])
    collect_down()
    for k in range(2):
        wait_for(lo_out.at[k], lo_rs.at[k])
        for n in range(3):
            wait_for(dctx.at[0, 0], dc_ss.at[k, n])
    wait_for(lo.at[0], lo_ss)
    for k in range(8):
        wait_for(dc_all.at[k], dc_rs.at[k])
    for n in range(6):
        for xs in range(2):
            for ys in range(2):
                gone = gd.at[pl.ds(0, 384)] if n == 0 else gu.at[pl.ds(0, 96), pl.ds(0, 768)]
                wait_for(gone, c_ss.at[n, xs, ys])
    for first, out in ((0, gdown_h), (4, gup_h), (8, gout_h)):
        for k in range(4):
            wait_for(out.at[k // 2, k % 2], o_sem.at[first + k])

    wait_for(cot.at[0], cot_ss)
    for i in range(2):
        for q in range(SUB):
            wait_for(tok.at[0, cuts[q]], tz_ss.at[i, q])
    for k in range(2, 4):

        @pl.when(inner)
        def _():
            for q in range(SUB):
                wait_for(tok.at[0, cuts[q]], tx_ss.at[k, q])

    for k in range(4):
        for q in range(SUB):
            wait_for(tok.at[0, cuts[q]], ty_ss.at[k, q])
    for k in range(8):
        wait_for(tok.at[0], tc_ss.at[k])
    for k in range(3):
        wait_for(wq.at[0], wq_ss.at[k])
    for k in range(3, 10):
        wait_for(land.at[0, 0, 0], wq_ss.at[k])
    for n in range(count):
        for k in range(2):
            wait_for(shard(n), wz_ss.at[n, k])

        @pl.when(inner)
        def _():
            wait_for(two(n), wz_ss.at[n, 2])

    for n, k in sent:
        gone = some(n, k - 3) if k in (3, 4) else at(n, quad(0, 0))
        wait_for(gone, wp_ss.at[n, k])
    for j in range(8):
        zz, yy = j // 2, j % 2
        stay = jnp.logical_and(zl == zz % 2, y == yy)

        @pl.when(jnp.logical_not(stay))
        def _():
            wait_for(ctx.at[j], ctx_ss.at[j])

    for k, (src, dst) in enumerate(kept):
        wait_for(dst, out_sem.at[k])


def forward_call(tokens, cot, segments, wqkv, wout, wup, wdown, rows24, up_bias, qv_bias):
    bf, f32 = jnp.bfloat16, jnp.float32
    sds = jax.ShapeDtypeStruct
    dma = pltpu.SemaphoreType.DMA
    outs = [
        sds((2, 128, 768), f32),
        sds((16, 768), f32),
        sds((2, 128, 768), bf),
        sds((8, 128, 192), bf),
        sds((2, 2, 96, 768), bf),
        sds((2, 2, 96, 3072), bf),
        sds((2, 2, 384, 768), bf),
        sds((16, 128, 768), bf),
        sds((3, 1024, 64), bf),
        sds((3, 2048, 64), bf),
        sds((3, 2048, 64), bf),
        sds((3, 1024, 64), f32),
        sds((3, 8, 1024), f32),
        sds((768, 576), bf),
        sds((8, 2048), f32),
        sds((2048, 128), f32),
    ]
    scratch = [
        pltpu.VMEM((16, 128, 768), bf),
        pltpu.VMEM((2, 2, 2, 4, 32, 576), bf),
        pltpu.VMEM((768, 576), bf),
        pltpu.VMEM((3, 1024, 64), bf),
        pltpu.VMEM((3, 2048, 64), bf),
        pltpu.VMEM((3, 2048, 64), bf),
        pltpu.VMEM((3, 1024, 64), f32),
        pltpu.VMEM((3, 8, 1024), f32),
        pltpu.VMEM((8, 2048), f32),
        pltpu.VMEM((2048, 128), f32),
        pltpu.VMEM((8, 128, 192), bf),
        pltpu.VMEM((32, 24, 768), bf),
        pltpu.VMEM((32, 24, 3072), bf),
        pltpu.VMEM((32, 96, 768), bf),
        pltpu.VMEM((8, 8, 576), f32),
        pltpu.VMEM((4, 2, 128, 192), bf),
        pltpu.VMEM((2, 128, 768), bf),
        pltpu.VMEM((768, 768), bf),
        pltpu.VMEM((768, 3072), bf),
        pltpu.VMEM((256, 3072), bf),
        pltpu.VMEM((256, 3072), f32),
        pltpu.VMEM((768, 768), bf),
        pltpu.VMEM((768, 3072), bf),
        pltpu.VMEM((3072, 768), bf),
        pltpu.VMEM((2, 2, 96, 768), bf),
        pltpu.VMEM((2, 2, 96, 3072), bf),
        pltpu.VMEM((2, 2, 384, 768), bf),
        dma((16, SUB)),
        dma((2, SUB)),
        dma((4, SUB)),
        dma((4, SUB)),
        dma((8,)),
        dma(()),
        dma((2,)),
        dma((10,)),
        dma((2, 2, 2, 4)),
        dma((len(PIECES), 3)),
        dma((len(PIECES), 5)),
        dma((len(PIECES), 8)),
        dma((len(PIECES), 2, 4, 2)),
        dma((8,)),
        dma((4, 2)),
        dma((9,)),
        dma((6, 2, 2)),
        dma((6, 2, 2)),
        dma((12,)),
        pltpu.VMEM((4, 32, 576), bf),
        pltpu.VMEM((2, 128, 768), bf),
        pltpu.VMEM((4, 2, 128, 192), bf),
        pltpu.VMEM((2, 192, 768), bf),
        pltpu.VMEM((2, 192, 768), bf),
        dma(()),
        dma((2,)),
        dma((2, 3)),
        dma((8,)),
        dma((4,)),
        dma((4,)),
    ]
    here, far = pl.BlockSpec(memory_space=pltpu.VMEM), pl.BlockSpec(memory_space=ANY)
    return pl.pallas_call(
        forward_kernel,
        out_shape=outs,
        in_specs=[far, far, here, here, far, far, far, here, here, here],
        out_specs=[here] * 2 + [far] * (len(outs) - 2),
        scratch_shapes=scratch,
        compiler_params=pltpu.CompilerParams(
            collective_id=0, has_side_effects=True, vmem_limit_bytes=VMEM_LIMIT
        ),
        name="forward",
    )(tokens, cot, segments, wqkv, wout, wup, wdown, rows24, up_bias, qv_bias)


RCUT = 2
EARLY_JOBS = 2
JOBS = (
    ("down", (48, 768), 0, 0),
    ("down", (48, 768), 48, 0),
    ("up", (24, 1536), 0, 0),
    ("up", (24, 1536), 0, 1536),
    ("out", (24, 768), 0, 0),
)


def add_block(dst, src):
    dst[...] = (dst[...].astype(jnp.float32) + src[...].astype(jnp.float32)).astype(jnp.bfloat16)


def backward_kernel(
    dc_h,
    dr1,
    gout,
    gup,
    gdown,
    gvec,
    tok_h,
    q_h,
    k_h,
    v_h,
    o_h,
    lse_h,
    wq_h,
    idrow_h,
    idcol_h,
    gt_out,
    gout_o,
    gup_o,
    gdown_o,
    gq_o,
    small_o,
    *rest,
):
    count = len(JOBS)
    accs, rest = rest[:count], rest[count:]
    r2as, rest = rest[:count], rest[count:]
    r2bs, rest = rest[:count], rest[count:]
    r1as, rest = rest[:count], rest[count:]
    r1bs, rest = rest[:count], rest[count:]
    rzs, rest = rest[:count], rest[count:]
    (
        tok,
        qs,
        ks,
        vs,
        os_,
        lses,
        wqs,
        idrow,
        idcol,
        dc,
        dks,
        dvs,
        dqs,
        douts,
        kv_send,
        kv_recv,
        dmix,
        dx,
        rx,
        dr,
        gt_send,
        gt_in,
        gq,
        gqc,
        gqx,
        gqz,
        gqin,
        gva,
        gvr,
        qb,
        qbr,
        qb_o,
        in_sem,
        own_ss,
        s2_ss,
        s2_rs,
        s1_ss,
        s1_rs,
        z_ss,
        z_rs,
        kv_ss,
        kv_rs,
        dx_ss,
        dx_rs,
        gt_ss,
        gt_rs,
        gq_ss,
        gq_rs,
        gv_ss,
        gv_rs,
        qb_ss,
        qb_rs,
    ) = rest
    x, y, c, h, z = place()
    zl, pi = lax.rem(z, 2), lax.div(z, 2)
    pz, zc = z + 1 - 2 * zl, lax.rem(z + 2, 4)
    g = 2 * zl + y
    hy = lax.rem(h + 2, 4)
    hc = h + 1 - 2 * c
    to_x, to_y, to_c = (1 - x, h, z), (x, hy, z), (x, hc, z)
    to_n, to_d, to_z = (x, h, pz), (x, hy, pz), (x, h, zc)
    sources = {"out": gout, "up": gup, "down": gdown}
    greet(peers_of(x, h, c, z))

    def loaded():
        return (
            (tok_h, tok),
            (q_h, qs),
            (k_h, ks),
            (v_h, vs),
            (o_h, os_),
            (lse_h, lses),
            (wq_h, wqs),
            (idrow_h, idrow),
            (idcol_h, idcol),
            (dr1, dr),
            (gvec, gva),
            (dc_h, dc),
        )

    for k, (src, dst) in enumerate(loaded()):
        pltpu.make_async_copy(src, dst, in_sem.at[k]).start()
    def part_of(n):
        name, shape, row, col = JOBS[n]
        return sources[name], (pl.ds(row, shape[0]), pl.ds(col, shape[1]))

    def cross(n, source, part):
        remote(
            source.at[(1 - x, y, pl.ds(0, RCUT)) + part],
            r1as[n],
            s1_ss.at[n, 0],
            s1_rs.at[n, 0],
            to_x,
        ).start()
        remote(
            source.at[(x, 1 - y, pl.ds(RCUT, 4 - RCUT)) + part],
            r1bs[n],
            s1_ss.at[n, 1],
            s1_rs.at[n, 1],
            to_y,
        ).start()

    def stage1(n):
        src, part = part_of(n)
        acc = accs[n]
        if n < EARLY_JOBS:
            cross(n, src, part)
            pltpu.make_async_copy(
                src.at[(x, y, pl.ds(0, 4)) + part], acc.at[x, y], own_ss.at[n, 0]
            ).start()
            return
        for k in range(2):
            remote(
                src.at[(k, 1 - y, pl.ds(0, RCUT)) + part],
                r2as[n].at[k],
                s2_ss.at[n, k],
                s2_rs.at[n, k],
                to_y,
            ).start()
            remote(
                src.at[(1 - x, k, pl.ds(RCUT, 4 - RCUT)) + part],
                r2bs[n].at[k],
                s2_ss.at[n, 2 + k],
                s2_rs.at[n, 2 + k],
                to_x,
            ).start()
        for k in range(2):
            pltpu.make_async_copy(
                src.at[(k, y, pl.ds(0, RCUT)) + part], acc.at[k, y, pl.ds(0, RCUT)], own_ss.at[n, k]
            ).start()
            pltpu.make_async_copy(
                src.at[(x, k, pl.ds(RCUT, 4 - RCUT)) + part],
                acc.at[x, k, pl.ds(RCUT, 4 - RCUT)],
                own_ss.at[n, 2 + k],
            ).start()

    for n in range(count):
        stage1(n)
    def stage2(n):
        acc = accs[n]
        if n < EARLY_JOBS:
            wait_for(acc.at[x, y], own_ss.at[n, 0])
            return
        for k in range(2):
            wait_for(r2as[n].at[k], s2_rs.at[n, k])
            wait_for(r2bs[n].at[k], s2_rs.at[n, 2 + k])
            wait_for(r2as[n].at[k], own_ss.at[n, k])
            wait_for(r2bs[n].at[k], own_ss.at[n, 2 + k])
        for k in range(2):
            for q in range(RCUT):
                add_block(acc.at[k, y, q], r2as[n].at[k, q])
            for q in range(4 - RCUT):
                add_block(acc.at[x, k, RCUT + q], r2bs[n].at[k, q])
        cross(n, acc, ())

    def stage3(n):
        acc = accs[n]
        wait_for(r1as[n], s1_rs.at[n, 0])
        wait_for(r1bs[n], s1_rs.at[n, 1])
        for q in range(RCUT):
            add_block(acc.at[x, y, q], r1as[n].at[q])
        for q in range(4 - RCUT):
            add_block(acc.at[x, y, RCUT + q], r1bs[n].at[q])
        for k in range(1, 4):
            zz = lax.rem(z + k, 4)
            remote(
                acc.at[x, y, zz], rzs[n].at[z], z_ss.at[n, k - 1], z_rs.at[n, z], (x, h, zz)
            ).start()

    def stage4(n):
        acc = accs[n]
        name, shape, row, col = JOBS[n]
        total = acc[x, y, z].astype(jnp.float32)
        for k in range(1, 4):
            zz = lax.rem(z + k, 4)
            wait_for(rzs[n].at[zz], z_rs.at[n, zz])
            total = total + rzs[n][zz].astype(jnp.float32)
        out = {"out": gout_o, "up": gup_o, "down": gdown_o}[name]
        out[row : row + shape[0], col : col + shape[1]] = total

    for k, (src, dst) in enumerate(loaded()):
        wait_for(dst, in_sem.at[k])

    def attend(zz):
        rows = slice(zz * 256, zz * 256 + 256)
        first = pl.ds(pl.multiple_of((zz * 4 + c) * 128, 128), 128)
        second = pl.ds(pl.multiple_of((zz * 4 + 2 + c) * 128, 128), 128)
        idq = jnp.concatenate([idrow[0:1, first], idrow[0:1, second]], axis=1)
        mask = idcol[:, 0:1] == idq
        both = jnp.concatenate([dc[2 * zz], dc[2 * zz + 1]], axis=0)
        for hh in range(3):
            douts[hh] = both[:, 64 * hh : 64 * hh + 64]

        def one_head(hh, carry):
            dout = douts[hh]
            q = qs[hh, rows, :]
            delta = jnp.sum(dout.astype(jnp.float32) * os_[hh, rows, :], axis=-1, keepdims=True)
            delta = jnp.transpose(jnp.broadcast_to(delta, (256, 128)))[0:1, :]
            scores = jnp.where(mask, nt(ks[hh], q), MASKED)
            probs = jnp.exp(scores - lses[hh, 0:1, rows])
            dprobs = nt(vs[hh], dout)
            ds = (probs * (dprobs - delta)).astype(jnp.bfloat16)
            dk = nn(ds, q)
            dv = nn(probs.astype(jnp.bfloat16), dout)
            if zz == 0:
                dks[hh] = dk
                dvs[hh] = dv
            else:
                dks[hh] += dk
                dvs[hh] += dv
            dqs[hh, rows, :] = (tn(ds, ks[hh]) * SCALE).astype(jnp.bfloat16)
            return carry

        lax.fori_loop(0, 3, one_head, 0)

    def add_gv(k):
        wait_for(gva, gv_rs.at[k])
        wait_for(gva, gv_ss.at[k])
        gva[...] = gva[...] + gvr[k]

    def gv_stage(n):
        if n < 3:
            if n > 0:
                add_gv(n - 1)
            remote(gva, gvr.at[n], gv_ss.at[n], gv_rs.at[n], (to_c, to_x, to_y)[n]).start()
        elif n == 3:
            add_gv(2)
            for k in range(1, 4):
                remote(
                    gva,
                    gvr.at[3 + z],
                    gv_ss.at[2 + k],
                    gv_rs.at[3 + z],
                    (x, h, lax.rem(z + k, 4)),
                ).start()
        else:
            gv = gva[...]
            for k in range(1, 4):
                zz = lax.rem(z + k, 4)
                wait_for(gvr.at[3 + zz], gv_rs.at[3 + zz])
                gv = gv + gvr[3 + zz]
            gvr[3 + z] = gv

    gv_stage(0)
    beside = {
        0: ((stage2, 0), (stage3, 0), (stage2, 1), (stage3, 1)),
        1: ((stage2, 2),),
        2: ((stage2, 3), (stage3, 2)),
    }
    for t in range(4):
        attend(t)
        gv_stage(t + 1)
        for stage, n in beside.get(t, ()):
            stage(n)

    for j in range(8):
        p = (j // 2) * 4 + (j % 2) * 2 + 1 - c
        rows = pl.ds(pl.multiple_of(p * 128, 128), 128)
        kv_send[j] = jnp.concatenate(
            [dks[hh, rows, :] for hh in range(3)] + [dvs[hh, rows, :] for hh in range(3)], axis=1
        ).astype(jnp.bfloat16)
    remote(kv_send, kv_recv, kv_ss, kv_rs, to_c).start()
    stage2(4)
    stage3(3)
    wait_for(kv_recv, kv_rs)

    qsum = jnp.zeros((1, 192), jnp.float32)
    vsum = jnp.zeros((1, 192), jnp.float32)
    for j in range(8):
        p = (j // 2) * 4 + (j % 2) * 2 + c
        rows = pl.ds(pl.multiple_of(p * 128, 128), 128)
        wide = jnp.concatenate(
            [dks[hh, rows, :] for hh in range(3)] + [dvs[hh, rows, :] for hh in range(3)], axis=1
        )
        wide = (wide + kv_recv[j].astype(jnp.float32)).astype(jnp.bfloat16)
        part = jnp.concatenate([dqs[hh, 128 * j : 128 * j + 128, :] for hh in range(3)], axis=1)
        dmix[128 * j : 128 * j + 128, :] = jnp.concatenate([part, wide], axis=1)
        qsum = qsum + jnp.sum(part.astype(jnp.float32), axis=0, keepdims=True)
        vsum = vsum + jnp.sum(wide[:, 192:].astype(jnp.float32), axis=0, keepdims=True)
    none = jnp.zeros((1, 192), jnp.float32)
    qb[...] = jnp.broadcast_to(
        jnp.concatenate([qsum, none, vsum, none[:, :64]], axis=1), (8, 640)
    )
    remote(qb, qbr.at[0], qb_ss.at[0], qb_rs.at[0], to_c).start()

    for j in range(8):
        zz, yy = j // 2, j % 2
        dx[j] = nt(dmix[128 * j : 128 * j + 128, :], wqs[...]).astype(jnp.bfloat16)
        slot = zz // 2
        stay = jnp.logical_and(zl == zz % 2, y == yy)

        @pl.when(jnp.logical_not(stay))
        def _():
            remote(
                dx.at[j],
                rx.at[g, slot],
                dx_ss.at[j],
                dx_rs.at[g, slot],
                (x, yy * 2 + c, 2 * pi + zz % 2),
            ).start()

        @pl.when(stay)
        def _():
            pltpu.make_async_copy(dx.at[j], rx.at[g, slot], dx_rs.at[g, slot]).start()

    total = jnp.zeros((768, 576), jnp.float32)
    for zz in range(4):
        left = jnp.concatenate([tok[zz * 4 + c], tok[zz * 4 + 2 + c]], axis=0)
        total = total + tn(left, dmix[256 * zz : 256 * zz + 256, :])
    for xs in range(2):
        for hs in range(4):
            for zz in range(4):
                base = (xs * 16 + hs * 4 + zz) * 24
                gq[hs % 2, xs, zz // 2, 2 * (zz % 2) + hs // 2] = total[base : base + 24].astype(jnp.bfloat16)
    remote(gq.at[1 - c], gqc, gq_ss.at[0], gq_rs.at[0], to_c).start()
    stage3(4)
    stage4(0)

    def add_qb(k):
        wait_for(qb, qb_rs.at[k])
        wait_for(qb, qb_ss.at[k])
        qb[...] = qb[...] + qbr[k]

    wait_for(gqc, gq_rs.at[0])

    def addq(t, carry):
        i, q = lax.div(t, 4), lax.rem(t, 4)
        xs, pp = lax.div(i, 2), lax.rem(i, 2)
        add_block(gq.at[c, xs, pp, q], gqc.at[xs, pp, q])
        return carry

    lax.fori_loop(0, 16, addq, 0)
    remote(gq.at[c, 1 - x], gqx, gq_ss.at[1], gq_rs.at[1], to_x).start()
    add_qb(0)
    remote(qb, qbr.at[1], qb_ss.at[1], qb_rs.at[1], to_x).start()
    stage4(1)
    wait_for(gqx, gq_rs.at[1])

    def addx(t, carry):
        pp, q = lax.div(t, 4), lax.rem(t, 4)
        add_block(gq.at[c, x, pp, q], gqx.at[pp, q])
        return carry

    lax.fori_loop(0, 8, addx, 0)
    remote(gq.at[c, x, 1 - pi], gqz, gq_ss.at[2], gq_rs.at[2], to_z).start()
    add_qb(1)
    remote(qb, qbr.at[2], qb_ss.at[2], qb_rs.at[2], to_z).start()
    stage4(2)

    for s in range(2):
        acc = dr[s]
        for q in range(4):
            wait_for(rx.at[q, s], dx_rs.at[q, s])
            acc = acc + rx[q, s].astype(jnp.float32)
        gt_send[s] = acc.astype(jnp.bfloat16)
        zz = 2 * s + zl
        row = pi
        stay = pi == s

        @pl.when(stay)
        def _():
            pltpu.make_async_copy(gt_send.at[s], gt_in.at[row], gt_rs.at[row]).start()

        @pl.when(jnp.logical_not(stay))
        def _():
            remote(gt_send.at[s], gt_in.at[row], gt_ss.at[s], gt_rs.at[row], to_z).start()

    wait_for(gqz, gq_rs.at[2])
    for q in range(4):
        add_block(gq.at[c, x, pi, q], gqz.at[q])
    add_qb(2)
    gqzs = gq.at[c, x, pi]
    for k, (dev, target) in enumerate(
        ((to_n, 2 * (1 - zl) + y), (to_y, 2 * zl + 1 - y), (to_d, 2 * (1 - zl) + 1 - y))
    ):
        remote(gqzs.at[target], gqin.at[g], gq_ss.at[3 + k], gq_rs.at[3 + g], dev).start()
        remote(qb, qb_o.at[g], qb_ss.at[3 + k], qb_rs.at[3 + g], dev).start()
    pltpu.make_async_copy(gqzs.at[g], gqin.at[g], gq_rs.at[3 + g]).start()
    pltpu.make_async_copy(qb, qb_o.at[g], qb_rs.at[3 + g]).start()
    stage4(3)
    for q in range(4):
        wait_for(gqin.at[q], gq_rs.at[3 + q])
        wait_for(qb_o.at[q], qb_rs.at[3 + q])
        gq_o[q] = gqin[q].astype(jnp.float32)
    me = x * 16 + h * 4 + z
    vectors = gvr[3 + z]
    own_rows = pltpu.roll(vectors[0:8, :], lax.rem(768 - 24 * me, 768), 1)[:, 0:128]
    up_row = jnp.zeros((1, 768), jnp.float32)
    for i in range(4):
        up_row = up_row + jnp.where(lax.div(me, 8) == i, vectors[6 + i : 7 + i, :], 0.0)
    up_rows = jnp.broadcast_to(up_row, (8, 768))
    up_rows = pltpu.roll(up_rows, lax.rem(768 - 96 * lax.rem(me, 8), 768), 1)[:, 0:128]
    qv_rows = pltpu.roll(qb_o[h], lax.rem(640 - 48 * z - 384 * x, 640), 1)[:, 0:128]
    line = lax.broadcasted_iota(jnp.int32, (8, 128), 0)
    small_o[...] = jnp.where(line < 6, own_rows, jnp.where(line == 6, up_rows, qv_rows))
    stage4(4)
    for i in range(2):
        wait_for(gt_in.at[i], gt_rs.at[i])
        gt_out[i] = gt_in[i].astype(jnp.float32)

    for s in range(2):

        @pl.when(pi != s)
        def _():
            wait_for(gt_send.at[s], gt_ss.at[s])

    for n in range(count):
        for k in range(2 if n >= EARLY_JOBS else 0):
            wait_for(r1as[n], s2_ss.at[n, k])
            wait_for(r1bs[n], s2_ss.at[n, 2 + k])
        wait_for(r1as[n], s1_ss.at[n, 0])
        wait_for(r1bs[n], s1_ss.at[n, 1])
        for k in range(3):
            wait_for(rzs[n].at[0], z_ss.at[n, k])
    wait_for(kv_send, kv_ss)
    for j in range(8):
        stay = jnp.logical_and(zl == (j // 2) % 2, y == j % 2)

        @pl.when(jnp.logical_not(stay))
        def _():
            wait_for(dx.at[j], dx_ss.at[j])

    wait_for(gqc, gq_ss.at[0])
    wait_for(gqx, gq_ss.at[1])
    wait_for(gqz, gq_ss.at[2])
    for k in range(3):
        wait_for(gqin.at[0], gq_ss.at[3 + k])
        wait_for(qb, qb_ss.at[3 + k])
        wait_for(gva, gv_ss.at[3 + k])


def backward_call(*args):
    bf, f32 = jnp.bfloat16, jnp.float32
    sds = jax.ShapeDtypeStruct
    dma = pltpu.SemaphoreType.DMA
    vm = pltpu.VMEM
    outs = [
        sds((2, 128, 768), f32),
        sds((24, 768), f32),
        sds((24, 3072), f32),
        sds((96, 768), f32),
        sds((4, 24, 576), f32),
        sds((8, 128), f32),
    ]
    shapes = [job[1] for job in JOBS]
    count = len(JOBS)
    scratch = (
        [vm((2, 2, 4) + s, bf) for s in shapes]
        + [vm((2, RCUT) + s, bf) for s in shapes]
        + [vm((2, 4 - RCUT) + s, bf) for s in shapes]
        + [vm((RCUT,) + s, bf) for s in shapes]
        + [vm((4 - RCUT,) + s, bf) for s in shapes]
        + [vm((4,) + s, bf) for s in shapes]
        + [
            vm((16, 128, 768), bf),
            vm((3, 1024, 64), bf),
            vm((3, 2048, 64), bf),
            vm((3, 2048, 64), bf),
            vm((3, 1024, 64), f32),
            vm((3, 8, 1024), f32),
            vm((768, 576), bf),
            vm((8, 2048), f32),
            vm((2048, 128), f32),
            vm((8, 128, 192), bf),
            vm((3, 2048, 64), f32),
            vm((3, 2048, 64), f32),
            vm((3, 1024, 64), bf),
            vm((3, 256, 64), bf),
            vm((8, 128, 384), bf),
            vm((8, 128, 384), bf),
            vm((1024, 576), bf),
            vm((8, 128, 768), bf),
            vm((4, 2, 128, 768), bf),
            vm((2, 128, 768), f32),
            vm((2, 128, 768), bf),
            vm((2, 128, 768), bf),
            vm((2, 2, 2, 4, 24, 576), bf),
            vm((2, 2, 4, 24, 576), bf),
            vm((2, 4, 24, 576), bf),
            vm((4, 24, 576), bf),
            vm((4, 24, 576), bf),
            vm((16, 768), f32),
            vm((7, 16, 768), f32),
            vm((8, 640), f32),
            vm((3, 8, 640), f32),
            vm((4, 8, 640), f32),
            dma((12,)),
            dma((count, 4)),
            dma((count, 4)),
            dma((count, 4)),
            dma((count, 2)),
            dma((count, 2)),
            dma((count, 3)),
            dma((count, 4)),
            dma(()),
            dma(()),
            dma((8,)),
            dma((4, 2)),
            dma((2,)),
            dma((2,)),
            dma((6,)),
            dma((7,)),
            dma((6,)),
            dma((7,)),
            dma((6,)),
            dma((7,)),
        ]
    )
    here = pl.BlockSpec(memory_space=pltpu.VMEM)
    far = pl.BlockSpec(memory_space=ANY)
    return pl.pallas_call(
        backward_kernel,
        out_shape=outs,
        in_specs=[far] * 15,
        out_specs=[here] * 6,
        scratch_shapes=scratch,
        compiler_params=pltpu.CompilerParams(
            collective_id=1, has_side_effects=True, vmem_limit_bytes=VMEM_LIMIT
        ),
        name="backward",
    )(*args)


def finish_kernel(lo, gt, gq, gout, gup, gdown, small, lo_o, gt_o, gqkv_o, gout_o, gup_o, gdown_o, *vectors):
    for src, dst in ((lo, lo_o), (gt, gt_o), (gout, gout_o), (gup, gup_o), (gdown, gdown_o)):
        dst[...] = src[...]
    for part in range(3):
        gqkv_o[:, 768 * part : 768 * part + 768] = jnp.concatenate(
            [gq[q, :, 192 * part : 192 * part + 192] for q in range(4)], axis=1
        )
    for k, dst in enumerate(vectors):
        dst[...] = small[k : k + 1, : dst.shape[1]]


def finish_call(lo, gt, gq, gout, gup, gdown, small):
    f32 = jnp.float32
    here = pl.BlockSpec(memory_space=pltpu.VMEM)
    like = lambda a: jax.ShapeDtypeStruct(a.shape, a.dtype)
    wide = jax.ShapeDtypeStruct((24, 2304), f32)
    outs = [like(lo), like(gt), wide, like(gout), like(gup), like(gdown)]
    outs += [jax.ShapeDtypeStruct((1, width), f32) for width in (24,) * 6 + (96, 48)]
    return pl.pallas_call(
        finish_kernel,
        out_shape=outs,
        in_specs=[here] * 7,
        out_specs=[here] * len(outs),
        compiler_params=pltpu.CompilerParams(vmem_limit_bytes=VMEM_LIMIT),
        name="finish",
    )(lo, gt, gq, gout, gup, gdown, small)


def slab_body(
    tokens,
    segments,
    qkv_weight,
    qv_bias,
    out_weight,
    out_bias,
    attn_gain,
    attn_shift,
    up_weight,
    up_bias,
    down_weight,
    down_bias,
    ffn_gain,
    ffn_shift,
    cotangent,
):
    rows24 = jnp.stack([out_bias, attn_gain, attn_shift, down_bias, ffn_gain, ffn_shift])
    (
        grad_first,
        gvec,
        lo_out,
        dc_all,
        grad_out,
        grad_up,
        grad_down,
        tok_all,
        q_all,
        k_all,
        v_all,
        o_all,
        lse_all,
        wq_all,
        idrow_all,
        idcol_all,
    ) = forward_call(
        tokens,
        cotangent,
        segments,
        qkv_weight,
        out_weight,
        up_weight,
        down_weight,
        rows24,
        up_bias.reshape(1, 96),
        qv_bias.reshape(1, 48),
    )
    gt_out, gout_o, gup_o, gdown_o, gq_o, small = backward_call(
        dc_all,
        grad_first,
        grad_out.reshape(2, 2, 4, 24, 768),
        grad_up.reshape(2, 2, 4, 24, 3072),
        grad_down.reshape(2, 2, 4, 96, 768),
        gvec,
        tok_all,
        q_all,
        k_all,
        v_all,
        o_all,
        lse_all,
        wq_all,
        idrow_all,
        idcol_all,
    )
    lo_out, gt_out, gqkv, gout_o, gup_o, gdown_o, *vectors = finish_call(
        lo_out, gt_out, gq_o, gout_o, gup_o, gdown_o, small
    )
    rows = [vector.reshape(vector.shape[1]) for vector in vectors]
    return (
        lo_out,
        gt_out,
        gqkv,
        rows[7],
        gout_o,
        rows[0],
        rows[1],
        rows[2],
        gup_o,
        rows[6],
        gdown_o,
        rows[3],
        rows[4],
        rows[5],
    )


def solution(mesh):
    sizes = tuple(mesh.shape[name] for name in ("dp", "head", "blk"))
    body = slab_body if sizes == (2, 4, 4) else general_body
    placed = (
        P("dp", ("blk", "head"), None),
        P("dp", ("blk", "head")),
        P(("dp", "head", "blk"), None),
        P(("dp", "head", "blk")),
        P(("dp", "head", "blk"), None),
        P(("dp", "head", "blk")),
        P(("dp", "head", "blk")),
        P(("dp", "head", "blk")),
        P(("dp", "head", "blk"), None),
        P(("dp", "head", "blk")),
        P(("dp", "head", "blk"), None),
        P(("dp", "head", "blk")),
        P(("dp", "head", "blk")),
        P(("dp", "head", "blk")),
        P("dp", ("blk", "head"), None),
    )
    return jax.shard_map(
        body,
        mesh=mesh,
        in_specs=placed,
        out_specs=(
            P("dp", ("blk", "head"), None),
            P("dp", ("blk", "head"), None),
            P(("dp", "head", "blk"), None),
            P(("dp", "head", "blk")),
            P(("dp", "head", "blk"), None),
            P(("dp", "head", "blk")),
            P(("dp", "head", "blk")),
            P(("dp", "head", "blk")),
            P(("dp", "head", "blk"), None),
            P(("dp", "head", "blk")),
            P(("dp", "head", "blk"), None),
            P(("dp", "head", "blk")),
            P(("dp", "head", "blk")),
            P(("dp", "head", "blk")),
        ),
        check_vma=False,
    )
```

```python
import math

import jax
import jax.numpy as jnp
from jax import lax
from jax.experimental import pallas as pl
from jax.experimental.pallas import tpu as pltpu
from jax.sharding import PartitionSpec as P

HEADS = 12
HDIM = 64
NSEG = 256


EPS = 1e-12
MASKED = -1e30
SCALE = 0.125


def norm_forward(values_in, gain, shift):
    mean_val = jnp.mean(values_in, axis=-1, keepdims=True)
    centred = values_in - mean_val
    inv_std = lax.rsqrt(jnp.mean(centred * centred, axis=-1, keepdims=True) + EPS)
    normed = centred * inv_std
    return (normed * gain + shift, normed, inv_std)


def norm_backward(grad_in, normed, inv_std, gain):
    scaled = grad_in * gain
    inner_term = (
        scaled
        - jnp.mean(scaled, axis=-1, keepdims=True)
        - normed * jnp.mean(scaled * normed, axis=-1, keepdims=True)
    )
    return (inner_term * inv_std, jnp.sum(grad_in * normed, axis=0), jnp.sum(grad_in, axis=0))


def exact_gelu(values_in):
    return jax.nn.gelu(values_in, approximate=False)


def stretch_scores(queries, key_part, query_seg, key_seg, query_place, key_place):
    scores = (
        jnp.einsum("sqhd,skhd->shqk", queries, key_part, preferred_element_type=jnp.float32) * SCALE
    )
    same_doc = query_seg[:, None, :, None] == key_seg[:, None, None, :]
    own_place = query_place[:, None] == key_place[None, :]
    usable = (query_seg[:, None, :, None] != NSEG - 1) | own_place[None, None]
    return (scores, same_doc & usable)


def slice_keys(key_piece, value_piece, seg_piece, offset, step_rows):
    key_part = lax.dynamic_slice_in_dim(key_piece, offset, step_rows, 1)
    value_part = lax.dynamic_slice_in_dim(value_piece, offset, step_rows, 1)
    seg_part = lax.dynamic_slice_in_dim(seg_piece, offset, step_rows, 1)
    return (key_part, value_part, seg_part)


def part_grads(
    queries,
    grad_ctx,
    log_total,
    row_delta,
    query_seg,
    query_place,
    key_part,
    value_part,
    key_seg,
    key_place,
):
    scores, allowed = stretch_scores(queries, key_part, query_seg, key_seg, query_place, key_place)
    probs = jnp.where(allowed, jnp.exp(scores - log_total[..., None]), 0.0)
    grad_probs = jnp.einsum(
        "sqhd,skhd->shqk", grad_ctx, value_part, preferred_element_type=jnp.float32
    )
    grad_scores = (probs * (grad_probs - row_delta[..., None])).astype(jnp.bfloat16)
    grad_query = (
        jnp.einsum("shqk,skhd->sqhd", grad_scores, key_part, preferred_element_type=jnp.float32)
        * SCALE
    )
    grad_key = (
        jnp.einsum("shqk,sqhd->skhd", grad_scores, queries, preferred_element_type=jnp.float32)
        * SCALE
    )
    grad_value = jnp.einsum(
        "shqk,sqhd->skhd", probs.astype(jnp.bfloat16), grad_ctx, preferred_element_type=jnp.float32
    )
    return (grad_query, grad_key, grad_value)


def general_body(
    tokens,
    segments,
    qkv_weight,
    qv_bias,
    out_weight,
    out_bias,
    attn_gain,
    attn_shift,
    up_weight,
    up_bias,
    down_weight,
    down_bias,
    ffn_gain,
    ffn_shift,
    cotangent,
):
    seq_count, local_rows, model_width = tokens.shape
    group_count = lax.axis_size("head")
    group_width = model_width // group_count
    heads_here = HEADS // group_count
    block_rows = local_rows * group_count
    key_rows = block_rows * lax.axis_size("blk")
    token_count = seq_count * local_rows
    gathered = (
        lax.all_gather(qkv_weight, ("dp", "head", "blk"), axis=0, tiled=True),
        lax.all_gather(qv_bias, ("dp", "head", "blk"), axis=0, tiled=True),
        lax.all_gather(out_weight, ("dp", "head", "blk"), axis=0, tiled=True),
        lax.all_gather(out_bias, ("dp", "head", "blk"), axis=0, tiled=True),
        lax.all_gather(attn_gain, ("dp", "head", "blk"), axis=0, tiled=True),
        lax.all_gather(attn_shift, ("dp", "head", "blk"), axis=0, tiled=True),
        lax.all_gather(up_weight, ("dp", "head", "blk"), axis=0, tiled=True),
        lax.all_gather(up_bias, ("dp", "head", "blk"), axis=0, tiled=True),
        lax.all_gather(down_weight, ("dp", "head", "blk"), axis=0, tiled=True),
        lax.all_gather(down_bias, ("dp", "head", "blk"), axis=0, tiled=True),
        lax.all_gather(ffn_gain, ("dp", "head", "blk"), axis=0, tiled=True),
        lax.all_gather(ffn_shift, ("dp", "head", "blk"), axis=0, tiled=True),
    )
    (
        whole_qkv,
        whole_qv,
        whole_out,
        whole_out_bias,
        whole_attn_gain,
        whole_attn_shift,
        whole_up,
        whole_up_bias,
        whole_down,
        whole_down_bias,
        whole_ffn_gain,
        whole_ffn_shift,
    ) = gathered
    attn_scale = whole_attn_gain.astype(jnp.float32)
    ffn_scale = whole_ffn_gain.astype(jnp.float32)
    flat_tokens = tokens.reshape(token_count, model_width)
    mixed = jnp.dot(flat_tokens, whole_qkv, preferred_element_type=jnp.float32)
    bias_row = jnp.concatenate(
        [whole_qv[:model_width], jnp.zeros((model_width,), jnp.bfloat16), whole_qv[model_width:]]
    ).astype(jnp.float32)
    mixed_low = (mixed + bias_row).astype(jnp.bfloat16)
    grouped = (
        mixed_low.reshape(seq_count, local_rows, 3, group_count, group_width)
        .transpose(0, 1, 3, 2, 4)
        .reshape(seq_count, local_rows, group_count, 3 * group_width)
    )
    seg_copies = jnp.broadcast_to(
        segments.astype(jnp.bfloat16)[:, :, None, None], (seq_count, local_rows, group_count, 1)
    )
    arrived, seg_arrived = (
        lax.all_to_all(grouped, "head", split_axis=2, concat_axis=1, tiled=True),
        lax.all_to_all(seg_copies, "head", split_axis=2, concat_axis=1, tiled=True),
    )
    arrived = arrived.reshape(seq_count, block_rows, 3, heads_here, HDIM)
    queries = arrived[:, :, 0]
    keys_here = arrived[:, :, 1]
    values_here = arrived[:, :, 2]
    query_seg = seg_arrived.reshape(seq_count, block_rows)
    query_place = lax.axis_index("blk") * block_rows + jnp.arange(block_rows)
    row_shape = (seq_count, heads_here, block_rows)
    start_state = (
        jnp.full(row_shape, MASKED, jnp.float32),
        jnp.zeros(row_shape, jnp.float32),
        jnp.zeros(row_shape + (HDIM,), jnp.float32),
    )
    key_piece = lax.all_gather(keys_here, "blk", axis=1, tiled=True)
    value_piece = lax.all_gather(values_here, "blk", axis=1, tiled=True)
    seg_piece = lax.all_gather(query_seg, "blk", axis=1, tiled=True)
    piece_rows = key_piece.shape[1]
    step_rows = math.gcd(piece_rows, 512)

    def attend_one_step(state_in, step_index):
        offset = step_index * step_rows
        key_part, value_part, key_seg = slice_keys(
            key_piece, value_piece, seg_piece, offset, step_rows
        )
        key_place = offset + jnp.arange(step_rows)
        best, total, accum = state_in
        scores, allowed = stretch_scores(
            queries, key_part, query_seg, key_seg, query_place, key_place
        )
        new_best = jnp.maximum(best, jnp.max(jnp.where(allowed, scores, MASKED), axis=-1))
        weights = jnp.where(allowed, jnp.exp(scores - new_best[..., None]), 0.0)
        factor = jnp.exp(best - new_best)
        total = total * factor + jnp.sum(weights, axis=-1)
        accum = accum * factor[..., None] + jnp.einsum(
            "shqk,skhd->shqd",
            weights.astype(jnp.bfloat16),
            value_part,
            preferred_element_type=jnp.float32,
        )
        return ((new_best, total, accum), None)

    result, unused = lax.scan(attend_one_step, start_state, jnp.arange(piece_rows // step_rows))
    best, total, accum = result
    context = accum / total[..., None]
    log_total = best + jnp.log(total)
    context_low = (
        context.astype(jnp.bfloat16)
        .transpose(0, 2, 1, 3)
        .reshape(seq_count, block_rows, 1, group_width)
    )
    returned_ctx = lax.all_to_all(context_low, "head", split_axis=1, concat_axis=2, tiled=True)
    ctx_tokens = returned_ctx.reshape(token_count, model_width)
    attended = jnp.dot(
        ctx_tokens, whole_out, preferred_element_type=jnp.float32
    ) + whole_out_bias.astype(jnp.float32)
    first_sum = flat_tokens.astype(jnp.float32) + attended
    hidden, normed_one, inv_one = norm_forward(
        first_sum, attn_scale, whole_attn_shift.astype(jnp.float32)
    )
    hidden_low = hidden.astype(jnp.bfloat16)
    inner = jnp.dot(
        hidden_low, whole_up, preferred_element_type=jnp.float32
    ) + whole_up_bias.astype(jnp.float32)
    active, gelu_pull = jax.vjp(exact_gelu, inner)
    active_low = active.astype(jnp.bfloat16)
    branch = jnp.dot(
        active_low, whole_down, preferred_element_type=jnp.float32
    ) + whole_down_bias.astype(jnp.float32)
    final, normed_two, inv_two = norm_forward(
        hidden + branch, ffn_scale, whole_ffn_shift.astype(jnp.float32)
    )
    layer_out = final.astype(jnp.bfloat16).reshape(seq_count, local_rows, model_width)
    grad_final = cotangent.reshape(token_count, model_width).astype(jnp.float32)
    grad_second, grad_ffn_gain, grad_ffn_shift = norm_backward(
        grad_final, normed_two, inv_two, ffn_scale
    )
    grad_branch = grad_second.astype(jnp.bfloat16)
    grad_down = jnp.dot(active_low.T, grad_branch, preferred_element_type=jnp.float32)
    grad_down_bias = jnp.sum(grad_branch.astype(jnp.float32), axis=0)
    grad_active = jnp.dot(grad_branch, whole_down.T, preferred_element_type=jnp.float32)
    grad_inner = gelu_pull(grad_active)[0].astype(jnp.bfloat16)
    grad_up = jnp.dot(hidden_low.T, grad_inner, preferred_element_type=jnp.float32)
    grad_up_bias = jnp.sum(grad_inner.astype(jnp.float32), axis=0)
    grad_hidden = grad_second + jnp.dot(grad_inner, whole_up.T, preferred_element_type=jnp.float32)
    grad_first, grad_attn_gain, grad_attn_shift = norm_backward(
        grad_hidden, normed_one, inv_one, attn_scale
    )
    grad_attended = grad_first.astype(jnp.bfloat16)
    grad_out = jnp.dot(ctx_tokens.T, grad_attended, preferred_element_type=jnp.float32)
    grad_out_bias = jnp.sum(grad_attended.astype(jnp.float32), axis=0)
    grad_context = jnp.dot(grad_attended, whole_out.T, preferred_element_type=jnp.float32).astype(
        jnp.bfloat16
    )
    grad_sent = lax.all_to_all(
        grad_context.reshape(seq_count, local_rows, group_count, group_width),
        "head",
        split_axis=2,
        concat_axis=1,
        tiled=True,
    )
    grad_ctx = grad_sent.reshape(seq_count, block_rows, heads_here, HDIM)
    row_delta = jnp.einsum("sqhd,shqd->shq", grad_ctx.astype(jnp.float32), context)
    query_zero = jnp.zeros((seq_count, block_rows, heads_here, HDIM), jnp.float32)
    zero_keys = jnp.zeros((seq_count, key_rows, heads_here, HDIM), jnp.float32)
    gather_key_piece = lax.all_gather(keys_here, "blk", axis=1, tiled=True)
    gather_value_piece = lax.all_gather(values_here, "blk", axis=1, tiled=True)
    gather_seg_piece = lax.all_gather(query_seg, "blk", axis=1, tiled=True)
    piece_rows = gather_key_piece.shape[1]
    gather_step_rows = math.gcd(piece_rows, 512)

    def gather_one_step(state_in, step_index):
        offset = step_index * gather_step_rows
        key_part, value_part, key_seg = slice_keys(
            gather_key_piece, gather_value_piece, gather_seg_piece, offset, gather_step_rows
        )
        key_place = offset + jnp.arange(gather_step_rows)
        grad_q, grad_k, grad_v = state_in
        part_q, part_k, part_v = part_grads(
            queries,
            grad_ctx,
            log_total,
            row_delta,
            query_seg,
            query_place,
            key_part,
            value_part,
            key_seg,
            key_place,
        )
        grad_k = lax.dynamic_update_slice_in_dim(
            grad_k,
            lax.dynamic_slice_in_dim(grad_k, offset, gather_step_rows, 1) + part_k,
            offset,
            1,
        )
        grad_v = lax.dynamic_update_slice_in_dim(
            grad_v,
            lax.dynamic_slice_in_dim(grad_v, offset, gather_step_rows, 1) + part_v,
            offset,
            1,
        )
        return ((grad_q + part_q, grad_k, grad_v), None)

    result, unused = lax.scan(
        gather_one_step,
        (query_zero, zero_keys, zero_keys),
        jnp.arange(piece_rows // gather_step_rows),
    )
    grad_q, all_keys, all_values = result
    grad_k, grad_v = (
        lax.psum_scatter(
            all_keys.astype(jnp.bfloat16), "blk", scatter_dimension=1, tiled=True
        ).astype(jnp.float32),
        lax.psum_scatter(
            all_values.astype(jnp.bfloat16), "blk", scatter_dimension=1, tiled=True
        ).astype(jnp.float32),
    )
    grad_low = jnp.concatenate(
        [
            grad_q.astype(jnp.bfloat16).reshape(seq_count, block_rows, 1, group_width),
            grad_k.astype(jnp.bfloat16).reshape(seq_count, block_rows, 1, group_width),
            grad_v.astype(jnp.bfloat16).reshape(seq_count, block_rows, 1, group_width),
        ],
        axis=3,
    )
    back_tokens = lax.all_to_all(grad_low, "head", split_axis=1, concat_axis=2, tiled=True)
    grad_mixed = (
        back_tokens.reshape(seq_count, local_rows, group_count, 3, group_width)
        .transpose(0, 1, 3, 2, 4)
        .reshape(token_count, 3 * model_width)
    )
    grad_qkv = jnp.dot(flat_tokens.T, grad_mixed, preferred_element_type=jnp.float32)
    column_sums = jnp.sum(grad_mixed.astype(jnp.float32), axis=0)
    grad_qv = jnp.concatenate([column_sums[:model_width], column_sums[2 * model_width :]])
    grad_tokens = grad_first + jnp.dot(grad_mixed, whole_qkv.T, preferred_element_type=jnp.float32)
    summed = (
        lax.psum_scatter(grad_qkv, ("dp", "head", "blk"), scatter_dimension=0, tiled=True),
        lax.psum_scatter(grad_qv, ("dp", "head", "blk"), scatter_dimension=0, tiled=True),
        lax.psum_scatter(grad_out, ("dp", "head", "blk"), scatter_dimension=0, tiled=True),
        lax.psum_scatter(grad_out_bias, ("dp", "head", "blk"), scatter_dimension=0, tiled=True),
        lax.psum_scatter(grad_attn_gain, ("dp", "head", "blk"), scatter_dimension=0, tiled=True),
        lax.psum_scatter(grad_attn_shift, ("dp", "head", "blk"), scatter_dimension=0, tiled=True),
        lax.psum_scatter(grad_up, ("dp", "head", "blk"), scatter_dimension=0, tiled=True),
        lax.psum_scatter(grad_up_bias, ("dp", "head", "blk"), scatter_dimension=0, tiled=True),
        lax.psum_scatter(grad_down, ("dp", "head", "blk"), scatter_dimension=0, tiled=True),
        lax.psum_scatter(grad_down_bias, ("dp", "head", "blk"), scatter_dimension=0, tiled=True),
        lax.psum_scatter(grad_ffn_gain, ("dp", "head", "blk"), scatter_dimension=0, tiled=True),
        lax.psum_scatter(grad_ffn_shift, ("dp", "head", "blk"), scatter_dimension=0, tiled=True),
    )
    return (
        layer_out,
        grad_tokens.reshape(seq_count, local_rows, model_width),
        summed[0],
        summed[1],
        summed[2],
        summed[3],
        summed[4],
        summed[5],
        summed[6],
        summed[7],
        summed[8],
        summed[9],
        summed[10],
        summed[11],
    )


MESH = pl.DeviceIdType.MESH
ANY = pl.ANY
VMEM_LIMIT = 60 * 1024 * 1024


def remote(src, dst, send_sem, recv_sem, device):
    return pltpu.make_async_remote_copy(
        src_ref=src,
        dst_ref=dst,
        send_sem=send_sem,
        recv_sem=recv_sem,
        device_id=device,
        device_id_type=MESH,
    )


def wait_for(ref, sem):
    pltpu.make_async_copy(ref, ref, sem).wait()


def place():
    x, h, z = lax.axis_index("dp"), lax.axis_index("head"), lax.axis_index("blk")
    return x, lax.div(h, 2), lax.rem(h, 2), h, z


def greet(peers):
    barrier = pltpu.get_barrier_semaphore()
    for peer in peers:
        pl.semaphore_signal(barrier, inc=1, device_id=peer, device_id_type=MESH)
    pl.semaphore_wait(barrier, len(peers))


def peers_of(x, h, c, z):
    around = [(x, h, lax.rem(z + k, 4)) for k in (1, 2, 3)]
    other = lax.rem(h + 2, 4)
    beside = z + 1 - 2 * lax.rem(z, 2)
    return around + [(1 - x, h, z), (x, other, z), (x, other, beside), (x, h + 1 - 2 * c, z)]


def nt(left, right):
    return lax.dot_general(left, right, (((1,), (1,)), ((), ())), preferred_element_type=jnp.float32)


def tn(left, right):
    return lax.dot_general(left, right, (((0,), (0,)), ((), ())), preferred_element_type=jnp.float32)


def nn(left, right):
    return jnp.dot(left, right, preferred_element_type=jnp.float32)


def add_norm(values_in):
    mean_val = jnp.mean(values_in, axis=-1, keepdims=True)
    centred = values_in - mean_val
    inv_std = lax.rsqrt(jnp.mean(centred * centred, axis=-1, keepdims=True) + EPS)
    return centred * inv_std, inv_std


def norm_pull(scaled, normed, inv_std):
    return inv_std * (
        scaled
        - jnp.mean(scaled, axis=-1, keepdims=True)
        - normed * jnp.mean(scaled * normed, axis=-1, keepdims=True)
    )


def column_sum(values_in):
    return jnp.sum(values_in, axis=0, keepdims=True)


CUT = 2
EARLY = 0
AHEAD = 1
BESIDE_TOKENS = {
    99: ((0, 0),),
    100: ((1, 0),),
    101: ((1, 1),),
    102: ((1, 2),),
    103: ((1, 3),),
    105: ((1, 4),),
    111: ((1, 5),),
    112: ((1, 6),),
}
LATE = 1
LATE_STEP = 7
WQ_STEPS = (4, 5, 8)
SUB = 2
ROWS_SUB = 64
PIECES = (
    ("out", (24, 768), 0, 0),
    ("up", (24, 1536), 0, 0),
    ("up", (24, 1536), 0, 1536),
    ("down", (48, 768), 0, 0),
    ("down", (48, 768), 48, 0),
)


def forward_kernel(
    tokens,
    cot,
    segments,
    wqkv,
    wout,
    wup,
    wdown,
    rows24,
    up_bias,
    qv_bias,
    dr1,
    gvec,
    lo_out,
    dc_all,
    gout_h,
    gup_h,
    gdown_h,
    tok_all,
    q_all,
    k_all,
    v_all,
    o_all,
    lse_all,
    wq_all,
    idrow_all,
    idcol_all,
    tok,
    land,
    wqs,
    qs,
    ks,
    vs,
    os_,
    lses,
    idrow,
    idcol,
    ctx,
    wout_g,
    wup_g,
    wdown_g,
    win,
    ctx_in,
    cot_in,
    wout_v,
    wup_v,
    active,
    slope,
    go,
    gu,
    gd,
    ro,
    ru,
    rd,
    tok_rs,
    tz_ss,
    tx_ss,
    ty_ss,
    tc_ss,
    cot_ss,
    cot_rs,
    wq_ss,
    wq_rs,
    wz_ss,
    wz_rs,
    wp_ss,
    wp_rs,
    ctx_ss,
    ctx_rs,
    out_sem,
    c_ss,
    c_rs,
    o_sem,
    wq,
    lo,
    dctx,
    r2a,
    r2b,
    lo_ss,
    lo_rs,
    dc_ss,
    dc_rs,
    s2_ss,
    s2_rs,
):
    f32, bf = jnp.float32, jnp.bfloat16
    x, y, c, h, z = place()
    zl, pi = lax.rem(z, 2), lax.div(z, 2)
    g = 2 * zl + y
    me = x * 16 + h * 4 + z
    hy = lax.rem(h + 2, 4)
    hc = h + 1 - 2 * c
    to_x, to_y, to_c = (1 - x, h, z), (x, hy, z), (x, hc, z)
    pz, zc = z + 1 - 2 * zl, lax.rem(z + 2, 4)
    to_n, to_d, to_z = (x, h, pz), (x, hy, pz), (x, h, zc)
    mid = jnp.where(z < 2, 2, 1)
    inner = jnp.logical_or(z == 1, z == 2)
    outer = jnp.logical_not(inner)
    def moved(values, width, steps, index):
        out = None
        for k, start in enumerate(steps):
            ends = []
            if start:
                ends.append(jnp.zeros((values.shape[0], start), f32))
            ends.append(values)
            if width - start - values.shape[1]:
                ends.append(jnp.zeros((values.shape[0], width - start - values.shape[1]), f32))
            row = jnp.concatenate(ends, axis=1)
            out = row if out is None else jnp.where(index == k, row, out)
        return out

    starts = [48 * k for k in range(4)] + [384 + 48 * k for k in range(4)]
    bias_row = moved(qv_bias[...].astype(f32), 576, starts, 4 * x + z)
    six = moved(rows24[...].astype(f32), 128, [24 * k for k in range(4)], z)
    up_row = jnp.concatenate([up_bias[...].astype(f32), jnp.zeros((1, 32), f32)], axis=1)
    ten = [six[k : k + 1] for k in range(6)] + [jnp.where(z == k, up_row, 0.0) for k in range(4)]
    gap = jnp.zeros((1, 64), f32)
    none = jnp.zeros((1, 128), f32)
    slots = [
        jnp.concatenate(ten[0:4] + [gap], axis=1),
        jnp.concatenate(ten[4:8] + [gap], axis=1),
        jnp.concatenate(ten[8:10] + [none, none, gap], axis=1),
    ]
    seg_rows = segments[...].astype(f32)
    seg_rows = [jnp.concatenate([seg_rows[k : k + 1], jnp.zeros((1, 448), f32)], axis=1) for k in range(2)]
    last_rows = jnp.concatenate(slots + seg_rows + [jnp.zeros((2, 576), f32)], axis=0)
    whole = wqkv[...].astype(f32)
    for q in range(4):
        cols = [whole[:, 768 * p + 192 * q : 768 * p + 192 * q + 192] for p in range(3)]
        first_row = jnp.where(h == q, bias_row, 0.0)
        rows = [jnp.concatenate(cols, axis=1), first_row, last_rows]
        wq[q] = jnp.concatenate(rows, axis=0).astype(bf)
    greet(peers_of(x, h, c, z))

    mine = z * 4 + h
    weights = {"out": (wout, wout_g), "up": (wup, wup_g), "down": (wdown, wdown_g)}
    count = len(PIECES)
    base = x * 16 + h * 4
    bx, by = (1 - x) * 16 + h * 4, x * 16 + hy * 4

    def side(start, ab):
        return pl.ds(start, CUT) if ab == 0 else pl.ds(start + CUT, 4 - CUT)

    sa, sb = side(bx, 0), side(by, 1)

    def quad(xs, hs):
        return pl.ds(xs * 16 + hs * 4, 4)

    sent = []

    def shard(n):
        name, shape, row, col = PIECES[n]
        return weights[name][0].at[pl.ds(row, shape[0]), pl.ds(col, shape[1])]

    def at(n, where):
        name, shape, row, col = PIECES[n]
        return weights[name][1].at[where, pl.ds(row, shape[0]), pl.ds(col, shape[1])]

    def two(n):
        return at(n, pl.ds(0, 2))

    def some(n, ab):
        return at(n, side(0, ab))

    def pass_on(n, where, k, sem, dev):
        remote(at(n, where), at(n, where), wp_ss.at[n, k], wp_rs.at[(n,) + sem], dev).start()
        sent.append((n, k))

    def along_z(n):
        pltpu.make_async_copy(shard(n), at(n, me), wz_rs.at[n, z]).start()
        for k, zz in enumerate((pz, mid)):
            remote(shard(n), at(n, me), wz_ss.at[n, k], wz_rs.at[n, z], (x, h, zz)).start()

    def relay(n):
        @pl.when(inner)
        def _():
            there = pl.ds(base + jnp.where(z < 2, 2, 0), 2)
            for k in range(2):
                wait_for(at(n, 0), wz_rs.at[n, jnp.where(z < 2, 2, 0) + k])
            remote(at(n, there), at(n, there), wz_ss.at[n, 2], wz_rs.at[n, 4], (x, h, pz)).start()

    def first_hop(n):
        for k in range(2):
            wait_for(at(n, 0), wz_rs.at[n, jnp.where(z < 2, 0, 2) + k])

        @pl.when(outer)
        def _():
            wait_for(two(n), wz_rs.at[n, 4])

        for k, dev in enumerate((to_x, to_y, to_c)):
            pass_on(n, quad(x, h), k, (x, h, 0), dev)

    def second_hop(n):
        wait_for(at(n, quad(0, 0)), wp_rs.at[n, 1 - x, h, 0])
        wait_for(at(n, quad(0, 0)), wp_rs.at[n, x, hy, 0])
        pass_on(n, sa, 3, (1 - x, h, 0), to_y)
        pass_on(n, sb, 4, (x, hy, 1), to_x)
        pass_on(n, quad(1 - x, h), 5, (1 - x, h, 0), to_c)
        pass_on(n, quad(x, hy), 6, (x, hy, 0), to_c)

    def third_hop(n):
        for ab in range(2):
            wait_for(some(n, ab), wp_rs.at[n, 1 - x, hy, ab])
        pass_on(n, quad(1 - x, hy), 7, (1 - x, hy, 0), to_c)

    def advance(t):
        if t < count:
            first_hop(t)
        if t + AHEAD < count:
            relay(t + AHEAD)
        if 0 <= t - 1 < count:
            second_hop(t - 1)
        if 0 <= t - 2 < count:
            third_hop(t - 2)

    for n in range(EARLY):
        along_z(n)

    cuts = [pl.ds(ROWS_SUB * q, ROWS_SUB) for q in range(SUB)]

    def send_row(i, to):
        for q in range(SUB):
            remote(
                tokens.at[i, cuts[q]], tok.at[mine, cuts[q]], tz_ss.at[i, q], tok_rs.at[mine, q], to
            ).start()

    for i in range(2):

        @pl.when(pi == i)
        def _():
            send_row(i, to_n)
            for q in range(SUB):
                pltpu.make_async_copy(
                    tokens.at[i, cuts[q]], tok.at[mine, cuts[q]], tok_rs.at[mine, q]
                ).start()

        @pl.when(pi != i)
        def _():
            send_row(i, (x, h, 1 + i))

    def run_beside(t):
        for kind, n in BESIDE_TOKENS.get(t, ()):
            relay(n) if kind == 0 else advance(n)

    pltpu.make_async_copy(wq.at[g], land.at[c, x, pi, g], wq_rs.at[c, x, pi, g]).start()
    for k, (dev, target) in enumerate(
        ((to_n, 2 * (1 - zl) + y), (to_y, 2 * zl + 1 - y), (to_d, 2 * (1 - zl) + 1 - y))
    ):
        remote(wq.at[target], land.at[c, x, pi, g], wq_ss.at[k], wq_rs.at[c, x, pi, g], dev).start()

    def give_slices(xs, pp, k, dev):
        block = land.at[c, xs, pp]
        remote(block, block, wq_ss.at[k], wq_rs.at[c, xs, pp, 0], dev).start()

    for q in range(4):
        wait_for(land.at[c, x, pi, q], wq_rs.at[c, x, pi, q])
    give_slices(x, pi, 3, to_z)
    give_slices(x, pi, 4, to_x)
    give_slices(x, pi, 5, to_c)
    for n in range(EARLY, LATE):
        along_z(n)
    turns = (z, pz, zc, lax.rem(pz + 2, 4))

    def hand_on(p, q, sends, keep_sem):
        wait_for(tok.at[p, cuts[q]], tok_rs.at[p, q])
        for sem, dev in sends:
            remote(tok.at[p, cuts[q]], tok.at[p, cuts[q]], sem.at[q], tok_rs.at[p, q], dev).start()
        if q == SUB - 1:
            remote(tok.at[p], tok.at[p], keep_sem, tok_rs.at[p, 0], to_c).start()

    def own_piece(k, q):
        p = turns[k] * 4 + h
        hand_on(p, q, [(ty_ss.at[k], to_y)], tc_ss.at[k])
        if k >= 2:

            @pl.when(inner)
            def _():
                cut = cuts[q]
                remote(
                    tok.at[p, cut], tok.at[p, cut], tx_ss.at[k, q], tok_rs.at[p, q], to_n
                ).start()

    def side_piece(k, q):
        hand_on(turns[k] * 4 + hy, q, [], tc_ss.at[4 + k])

    def slices_step(t):
        if t == WQ_STEPS[0]:
            wait_for(land.at[c, x, 1 - pi], wq_rs.at[c, x, 1 - pi, 0])
            give_slices(x, 1 - pi, 6, to_x)
            give_slices(x, 1 - pi, 7, to_c)
        for k in range(2):
            if t == WQ_STEPS[1 + k]:
                there = (pi, 1 - pi)[k]
                wait_for(land.at[c, 1 - x, there], wq_rs.at[c, 1 - x, there, 0])
                give_slices(1 - x, there, 8 + k, to_c)

    order = [(0, q) for q in range(SUB)] + [(k, q) for q in range(SUB) for k in range(1, 4)]
    lag = 3
    for t in range(len(order) + lag):
        if t < len(order):
            own_piece(*order[t])
        if t >= lag:
            side_piece(*order[t - lag])
        slices_step(t)
        if t == LATE_STEP:
            for n in range(LATE, count):
                along_z(n)
        run_beside(t)

    run_beside(99)
    for i in range(2):

        @pl.when(pi == i)
        def _():
            pltpu.make_async_copy(cot.at[i], cot_in.at[pi], cot_rs.at[pi]).start()

        @pl.when(pi != i)
        def _():
            remote(cot.at[i], cot_in.at[pi], cot_ss, cot_rs.at[pi], to_z).start()

    for k in range(4):
        zz = lax.rem(z + k, 4)
        for hh in (hc, lax.rem(hc + 2, 4)):
            p = zz * 4 + hh
            wait_for(tok.at[p], tok_rs.at[p, 0])
    for k in range(4):
        wait_for(land.at[1 - c, k // 2, k % 2], wq_rs.at[1 - c, k // 2, k % 2, 0])

    run_beside(100)
    bias8 = jnp.zeros((8, 576), jnp.float32)
    for xs in range(2):
        for hs in range(4):
            part = []
            window = jnp.zeros((8, 576), jnp.float32)
            for zz in range(4):
                block = land[hs % 2, xs, zz // 2, 2 * (zz % 2) + hs // 2].astype(jnp.float32)
                part.append(block[:24])
                window = window + block[24:]
            start = (xs * 16 + hs * 4) * 24
            bias8 = bias8 + window
            win[xs * 4 + hs] = window
            wqs[start : start + 96, :] = jnp.concatenate(part, axis=0).astype(jnp.bfloat16)
    bias = bias8[0:1, :]

    lane = lax.broadcasted_iota(jnp.int32, (1, 128), 1)
    for p in range(16):
        zz, hs = p // 4, p % 4
        block = land[hs % 2, x, zz // 2, 2 * (zz % 2) + hs // 2].astype(jnp.float32)
        seg = jnp.where(pi == 0, block[28:29, :128], block[29:30, :128])
        ident = jnp.where(seg == NSEG - 1.0, (1000.0 + 128 * p) + lane.astype(f32), seg)
        idrow[:, 128 * p : 128 * p + 128] = jnp.broadcast_to(ident, (8, 128))
        idcol[128 * p : 128 * p + 128, :] = jnp.transpose(jnp.broadcast_to(ident, (128, 128)))

    def project(j, carry):
        zz, yy = lax.div(j, 2), lax.rem(j, 2)
        p = zz * 4 + yy * 2 + c
        rows = pl.ds(pl.multiple_of(j * 128, 128), 128)
        mixed = nn(tok[p], wqs[:, 0:192]) + bias[:, 0:192]
        low = mixed.astype(jnp.bfloat16) * jnp.bfloat16(SCALE)
        for hh in range(3):
            qs[hh, rows, :] = low[:, 64 * hh : 64 * hh + 64]
        both = tok[pl.ds(2 * j, 2)].reshape(256, 768)
        wide = nn(both, wqs[:, 192:576]) + bias[:, 192:576]
        wide = wide.astype(jnp.bfloat16)
        key_rows = pl.ds(pl.multiple_of(j * 256, 256), 256)
        for hh in range(3):
            ks[hh, key_rows, :] = wide[:, 64 * hh : 64 * hh + 64]
            vs[hh, key_rows, :] = wide[:, 192 + 64 * hh : 256 + 64 * hh]
        return carry

    lax.fori_loop(0, 8, project, 0)
    run_beside(101)

    def attend(zz):
        rows = slice(zz * 256, zz * 256 + 256)
        upper = pl.ds(pl.multiple_of((zz * 4 + c) * 128, 128), 128)
        lower = pl.ds(pl.multiple_of((zz * 4 + 2 + c) * 128, 128), 128)
        idq = jnp.concatenate([idcol[upper, :], idcol[lower, :]], axis=0)
        mask = idq[:, 0:1] == idrow[0:1, :]
        def one_head(hh, carry):
            scores = nt(qs[hh, rows, :], ks[hh])
            scores = jnp.where(mask, scores, MASKED)
            top = jnp.max(scores, axis=-1, keepdims=True)
            weights_ = jnp.exp(scores - top)
            total = jnp.sum(weights_, axis=-1, keepdims=True)
            o = nn(weights_.astype(jnp.bfloat16), vs[hh]) / total
            os_[hh, rows, :] = o
            lse = jnp.broadcast_to(top + jnp.log(total), (256, 128))
            lses[hh, :, rows] = jnp.transpose(lse)[0:8, :]
            return carry

        lax.fori_loop(0, 3, one_head, 0)
        out = jnp.concatenate([os_[k, rows, :] for k in range(3)], axis=1).astype(jnp.bfloat16)
        slot = zz // 2
        for yy in range(2):
            j = zz * 2 + yy
            ctx[j] = out[128 * yy : 128 * yy + 128]
            stay = jnp.logical_and(zl == zz % 2, y == yy)

            @pl.when(stay)
            def _():
                pltpu.make_async_copy(ctx.at[j], ctx_in.at[g, slot], ctx_rs.at[g, slot]).start()

            @pl.when(jnp.logical_not(stay))
            def _():
                remote(
                    ctx.at[j],
                    ctx_in.at[g, slot],
                    ctx_ss.at[j],
                    ctx_rs.at[g, slot],
                    (x, yy * 2 + c, 2 * pi + zz % 2),
                ).start()

    for t in range(4):
        attend(t)
        run_beside(102 + t)

    kept = (
        (tok, tok_all),
        (qs, q_all),
        (ks, k_all),
        (vs, v_all),
        (os_, o_all),
        (lses, lse_all),
        (wqs, wq_all),
        (idrow, idrow_all),
        (idcol, idcol_all),
    )
    for k, (src, dst) in enumerate(kept):
        pltpu.make_async_copy(src, dst, out_sem.at[k]).start()
    def arrive(n):
        for xs in range(2):
            for yy in range(2):
                wait_for(at(n, quad(0, 0)), wp_rs.at[n, xs, yy * 2 + 1 - c, 0])

    def flatten(src, dst, cols):
        for k in range(8):
            part = [src[4 * k + q, :, cols].astype(f32) for q in range(4)]
            dst[96 * k : 96 * k + 96, cols] = jnp.concatenate(part, axis=0).astype(bf)

    run_beside(110)
    for s in range(2):
        wait_for(cot_in.at[s], cot_rs.at[s])
        for q in range(4):
            wait_for(ctx_in.at[q, s], ctx_rs.at[q, s])
    arrive(0)
    def row(i):
        at_lane = 128 * (i % 4) if i < 6 else 0
        if i < 6:
            pieces = [win[w, 1 + i // 4 : 2 + i // 4, at_lane : at_lane + 96] for w in range(8)]
        else:
            pieces = []
            for w in (2 * (i - 6), 2 * (i - 6) + 1):
                for k in range(6, 10):
                    at_lane = 128 * (k % 4)
                    pieces.append(win[w, 1 + k // 4 : 2 + k // 4, at_lane : at_lane + 96])
        return jnp.concatenate(pieces, axis=1)

    full_ctx = jnp.concatenate([ctx_in[q].reshape(256, 192) for q in range(4)], axis=1)
    flatten(wout_g, wout_v, slice(0, 768))
    own = jnp.concatenate([tok[zl * 4 + h], tok[(2 + zl) * 4 + h]], axis=0).astype(f32)
    normed_one, inv_one = add_norm(own + nn(full_ctx, wout_v[...]) + row(0))
    hidden = normed_one * row(1) + row(2)
    hidden_low = hidden.astype(bf)
    run_beside(111)
    for k in range(4):
        cols = slice(768 * k, 768 * k + 768)
        if k % 2 == 0:
            arrive(1 + k // 2)
        flatten(wup_g, wup_v, cols)
        raised = nn(hidden_low, wup_v[:, cols]) + row(6 + k)
        normal = 0.5 + 0.5 * lax.erf(raised * (0.5**0.5))
        active[:, cols] = (raised * normal).astype(bf)
        slope[:, cols] = normal + raised * jnp.exp(-0.5 * raised * raised) * (0.5 / math.pi) ** 0.5
    run_beside(112)
    for n in (3, 4):
        arrive(n)
    branch = nn(active[...], wdown_g[...].reshape(3072, 768)) + row(3)
    normed_two, inv_two = add_norm(hidden + branch)
    lo[...] = (normed_two * row(4) + row(5)).astype(bf).reshape(2, 128, 768)
    for k in range(2):

        @pl.when(pi == k)
        def _():
            pltpu.make_async_copy(lo.at[k], lo_out.at[pi], lo_rs.at[pi]).start()

        @pl.when(pi != k)
        def _():
            remote(lo.at[k], lo_out.at[pi], lo_ss, lo_rs.at[pi], to_z).start()

    grad = cot_in[...].reshape(256, 768).astype(f32)
    gvec[4:5, :] = column_sum(grad * normed_two)
    gvec[5:6, :] = column_sum(grad)
    grad_second = norm_pull(grad * row(4), normed_two, inv_two)
    grad_branch = grad_second.astype(bf)
    gvec[3:4, :] = column_sum(grad_branch.astype(f32))

    def halves(n, full, back, rows, part):
        def at(xs, ys, core):
            start = (xs * 16 + (ys * 2 + core) * 4) * (rows // 4)
            return pl.ds(pl.multiple_of(start, rows // 4 * 4), rows)

        for xs in range(2):
            for ys in range(2):
                remote(
                    full.at[at(xs, ys, 1 - c), part],
                    back.at[xs, ys, :, part],
                    c_ss.at[n, xs, ys],
                    c_rs.at[n, xs, ys],
                    to_c,
                ).start()

    def settle(full, back, rows, out, sems, base, parts):
        for xs in range(2):
            for ys in range(2):
                for n, part in parts:
                    wait_for(back.at[xs, ys, :, part], c_rs.at[n, xs, ys])

                def body(t, carry):
                    rel = pl.multiple_of(t * 16, 16)
                    start = (xs * 16 + (ys * 2 + c) * 4) * (rows // 4)
                    mine = full[pl.ds(pl.multiple_of(start + rel, 16), 16), :].astype(f32)
                    there = pl.ds(rel, 16)
                    back[xs, ys, there, :] = (
                        mine + back[xs, ys, there, :].astype(f32)
                    ).astype(bf)
                    return carry

                lax.fori_loop(0, rows // 16, body, 0)
                if out is not None:
                    k = base + xs * 2 + ys
                    pltpu.make_async_copy(back.at[xs, ys], out.at[xs, ys], sems.at[k]).start()

    def spread_down():
        settle(gd, rd, 384, None, o_sem, 0, [(0, pl.ds(0, 768))])
        for k in range(2):
            remote(
                rd.at[k, 1 - y, pl.ds(0, 192)], r2a.at[k], s2_ss.at[k], s2_rs.at[k], to_y
            ).start()
            remote(
                rd.at[1 - x, k, pl.ds(192, 192)], r2b.at[k], s2_ss.at[2 + k], s2_rs.at[2 + k], to_x
            ).start()

    def collect_down():
        for k in range(2):
            wait_for(r2a.at[k], s2_rs.at[k])
            wait_for(r2b.at[k], s2_rs.at[2 + k])

        def body(t, carry):
            k, rel = lax.div(t, 12), pl.multiple_of(lax.rem(t, 12) * 16, 16)
            a, b = pl.ds(rel, 16), pl.ds(pl.multiple_of(rel + 192, 16), 16)
            rd[k, y, a, :] = (rd[k, y, a, :].astype(f32) + r2a[k, a, :].astype(f32)).astype(bf)
            rd[x, k, b, :] = (rd[x, k, b, :].astype(f32) + r2b[k, a, :].astype(f32)).astype(bf)
            return carry

        lax.fori_loop(0, 24, body, 0)
        for k in range(2):
            wait_for(r2a.at[k], s2_ss.at[k])
            wait_for(r2b.at[k], s2_ss.at[2 + k])
        for k in range(4):
            xs, ys = k // 2, k % 2
            pltpu.make_async_copy(rd.at[xs, ys], gdown_h.at[xs, ys], o_sem.at[k]).start()

    for k in range(4):
        rows = slice(768 * k, 768 * k + 768)
        gd[rows, :] = tn(active[:, rows], grad_branch).astype(bf)
    halves(0, gd, rd, 384, pl.ds(0, 768))
    for k in range(4):
        cols = slice(768 * k, 768 * k + 768)
        pulled = (nt(grad_branch, wdown_g[8 * k : 8 * k + 8].reshape(768, 768)) * slope[:, cols]).astype(bf)
        active[:, cols] = pulled
        gvec[6 + k : 7 + k, :] = column_sum(pulled.astype(f32))
        gu[:, cols] = tn(hidden_low, pulled).astype(bf)
        halves(1 + k, gu, ru, 96, pl.ds(768 * k, 768))
        if k == 1:
            spread_down()
    grad_hidden = grad_second + nt(active[...], wup_v[...])
    gvec[1:2, :] = column_sum(grad_hidden * normed_one)
    gvec[2:3, :] = column_sum(grad_hidden)
    grad_first = norm_pull(grad_hidden * row(1), normed_one, inv_one)
    dr1[...] = grad_first.reshape(2, 128, 768)
    grad_attended = grad_first.astype(bf)
    gvec[0:1, :] = column_sum(grad_attended.astype(f32))
    gvec[10:16, :] = jnp.zeros((6, 768), f32)
    go[...] = tn(full_ctx, grad_attended).astype(bf)
    halves(5, go, ro, 96, pl.ds(0, 768))
    back = nt(grad_attended, wout_v[...]).astype(bf)
    for q in range(4):
        dctx[q] = back[:, 192 * q : 192 * q + 192].reshape(2, 128, 192)

    for t in range(2):
        j = (2 * t + zl) * 2 + y
        for k, (dev, target) in enumerate(
            ((to_n, 2 * (1 - zl) + y), (to_y, 2 * zl + 1 - y), (to_d, 2 * (1 - zl) + 1 - y))
        ):
            remote(dctx.at[target, t], dc_all.at[j], dc_ss.at[t, k], dc_rs.at[j], dev).start()
        pltpu.make_async_copy(dctx.at[g, t], dc_all.at[j], dc_rs.at[j]).start()

    settle(gu, ru, 96, gup_h, o_sem, 4, [(1 + k, pl.ds(768 * k, 768)) for k in range(4)])
    settle(go, ro, 96, gout_h, o_sem, 8, [(5, pl.ds(0, 768))])
    collect_down()
    for k in range(2):
        wait_for(lo_out.at[k], lo_rs.at[k])
        for n in range(3):
            wait_for(dctx.at[0, 0], dc_ss.at[k, n])
    wait_for(lo.at[0], lo_ss)
    for k in range(8):
        wait_for(dc_all.at[k], dc_rs.at[k])
    for n in range(6):
        for xs in range(2):
            for ys in range(2):
                gone = gd.at[pl.ds(0, 384)] if n == 0 else gu.at[pl.ds(0, 96), pl.ds(0, 768)]
                wait_for(gone, c_ss.at[n, xs, ys])
    for first, out in ((0, gdown_h), (4, gup_h), (8, gout_h)):
        for k in range(4):
            wait_for(out.at[k // 2, k % 2], o_sem.at[first + k])

    wait_for(cot.at[0], cot_ss)
    for i in range(2):
        for q in range(SUB):
            wait_for(tok.at[0, cuts[q]], tz_ss.at[i, q])
    for k in range(2, 4):

        @pl.when(inner)
        def _():
            for q in range(SUB):
                wait_for(tok.at[0, cuts[q]], tx_ss.at[k, q])

    for k in range(4):
        for q in range(SUB):
            wait_for(tok.at[0, cuts[q]], ty_ss.at[k, q])
    for k in range(8):
        wait_for(tok.at[0], tc_ss.at[k])
    for k in range(3):
        wait_for(wq.at[0], wq_ss.at[k])
    for k in range(3, 10):
        wait_for(land.at[0, 0, 0], wq_ss.at[k])
    for n in range(count):
        for k in range(2):
            wait_for(shard(n), wz_ss.at[n, k])

        @pl.when(inner)
        def _():
            wait_for(two(n), wz_ss.at[n, 2])

    for n, k in sent:
        gone = some(n, k - 3) if k in (3, 4) else at(n, quad(0, 0))
        wait_for(gone, wp_ss.at[n, k])
    for j in range(8):
        zz, yy = j // 2, j % 2
        stay = jnp.logical_and(zl == zz % 2, y == yy)

        @pl.when(jnp.logical_not(stay))
        def _():
            wait_for(ctx.at[j], ctx_ss.at[j])

    for k, (src, dst) in enumerate(kept):
        wait_for(dst, out_sem.at[k])


def forward_call(tokens, cot, segments, wqkv, wout, wup, wdown, rows24, up_bias, qv_bias):
    bf, f32 = jnp.bfloat16, jnp.float32
    sds = jax.ShapeDtypeStruct
    dma = pltpu.SemaphoreType.DMA
    outs = [
        sds((2, 128, 768), f32),
        sds((16, 768), f32),
        sds((2, 128, 768), bf),
        sds((8, 128, 192), bf),
        sds((2, 2, 96, 768), bf),
        sds((2, 2, 96, 3072), bf),
        sds((2, 2, 384, 768), bf),
        sds((16, 128, 768), bf),
        sds((3, 1024, 64), bf),
        sds((3, 2048, 64), bf),
        sds((3, 2048, 64), bf),
        sds((3, 1024, 64), f32),
        sds((3, 8, 1024), f32),
        sds((768, 576), bf),
        sds((8, 2048), f32),
        sds((2048, 128), f32),
    ]
    scratch = [
        pltpu.VMEM((16, 128, 768), bf),
        pltpu.VMEM((2, 2, 2, 4, 32, 576), bf),
        pltpu.VMEM((768, 576), bf),
        pltpu.VMEM((3, 1024, 64), bf),
        pltpu.VMEM((3, 2048, 64), bf),
        pltpu.VMEM((3, 2048, 64), bf),
        pltpu.VMEM((3, 1024, 64), f32),
        pltpu.VMEM((3, 8, 1024), f32),
        pltpu.VMEM((8, 2048), f32),
        pltpu.VMEM((2048, 128), f32),
        pltpu.VMEM((8, 128, 192), bf),
        pltpu.VMEM((32, 24, 768), bf),
        pltpu.VMEM((32, 24, 3072), bf),
        pltpu.VMEM((32, 96, 768), bf),
        pltpu.VMEM((8, 8, 576), f32),
        pltpu.VMEM((4, 2, 128, 192), bf),
        pltpu.VMEM((2, 128, 768), bf),
        pltpu.VMEM((768, 768), bf),
        pltpu.VMEM((768, 3072), bf),
        pltpu.VMEM((256, 3072), bf),
        pltpu.VMEM((256, 3072), f32),
        pltpu.VMEM((768, 768), bf),
        pltpu.VMEM((768, 3072), bf),
        pltpu.VMEM((3072, 768), bf),
        pltpu.VMEM((2, 2, 96, 768), bf),
        pltpu.VMEM((2, 2, 96, 3072), bf),
        pltpu.VMEM((2, 2, 384, 768), bf),
        dma((16, SUB)),
        dma((2, SUB)),
        dma((4, SUB)),
        dma((4, SUB)),
        dma((8,)),
        dma(()),
        dma((2,)),
        dma((10,)),
        dma((2, 2, 2, 4)),
        dma((len(PIECES), 3)),
        dma((len(PIECES), 5)),
        dma((len(PIECES), 8)),
        dma((len(PIECES), 2, 4, 2)),
        dma((8,)),
        dma((4, 2)),
        dma((9,)),
        dma((6, 2, 2)),
        dma((6, 2, 2)),
        dma((12,)),
        pltpu.VMEM((4, 32, 576), bf),
        pltpu.VMEM((2, 128, 768), bf),
        pltpu.VMEM((4, 2, 128, 192), bf),
        pltpu.VMEM((2, 192, 768), bf),
        pltpu.VMEM((2, 192, 768), bf),
        dma(()),
        dma((2,)),
        dma((2, 3)),
        dma((8,)),
        dma((4,)),
        dma((4,)),
    ]
    here, far = pl.BlockSpec(memory_space=pltpu.VMEM), pl.BlockSpec(memory_space=ANY)
    return pl.pallas_call(
        forward_kernel,
        out_shape=outs,
        in_specs=[far, far, here, here, far, far, far, here, here, here],
        out_specs=[here] * 2 + [far] * (len(outs) - 2),
        scratch_shapes=scratch,
        compiler_params=pltpu.CompilerParams(
            collective_id=0, has_side_effects=True, vmem_limit_bytes=VMEM_LIMIT
        ),
        name="forward",
    )(tokens, cot, segments, wqkv, wout, wup, wdown, rows24, up_bias, qv_bias)


RCUT = 3
EARLY_JOBS = 1
JOBS = (
    ("down", (96, 768), 0, 0),
    ("up", (24, 1536), 0, 0),
    ("up", (24, 1536), 0, 1536),
    ("out", (24, 768), 0, 0),
)


def cut_of(n):
    return 2 if n < EARLY_JOBS else RCUT


def add_block(dst, src):
    dst[...] = (dst[...].astype(jnp.float32) + src[...].astype(jnp.float32)).astype(jnp.bfloat16)


def backward_kernel(
    dc_h,
    dr1,
    gout,
    gup,
    gdown,
    gvec,
    tok_h,
    q_h,
    k_h,
    v_h,
    o_h,
    lse_h,
    wq_h,
    idrow_h,
    idcol_h,
    gt_out,
    gout_o,
    gup_o,
    gdown_o,
    gq_o,
    small_o,
    *rest,
):
    count = len(JOBS)
    accs, rest = rest[:count], rest[count:]
    r2as, rest = rest[:count], rest[count:]
    r2bs, rest = rest[:count], rest[count:]
    r1as, rest = rest[:count], rest[count:]
    r1bs, rest = rest[:count], rest[count:]
    rzs, rest = rest[:count], rest[count:]
    (
        tok,
        qs,
        ks,
        vs,
        os_,
        lses,
        wqs,
        idrow,
        idcol,
        dc,
        dks,
        dvs,
        dqs,
        douts,
        kv_send,
        kv_recv,
        dmix,
        dx,
        rx,
        dr,
        gt_send,
        gt_in,
        gq,
        gqc,
        gqx,
        gqz,
        gqin,
        gva,
        gvr,
        qb,
        qbr,
        qb_o,
        in_sem,
        own_ss,
        s2_ss,
        s2_rs,
        s1_ss,
        s1_rs,
        z_ss,
        z_rs,
        kv_ss,
        kv_rs,
        dx_ss,
        dx_rs,
        gt_ss,
        gt_rs,
        gq_ss,
        gq_rs,
        gv_ss,
        gv_rs,
        qb_ss,
        qb_rs,
    ) = rest
    x, y, c, h, z = place()
    zl, pi = lax.rem(z, 2), lax.div(z, 2)
    pz, zc = z + 1 - 2 * zl, lax.rem(z + 2, 4)
    g = 2 * zl + y
    hy = lax.rem(h + 2, 4)
    hc = h + 1 - 2 * c
    to_x, to_y, to_c = (1 - x, h, z), (x, hy, z), (x, hc, z)
    to_n, to_d, to_z = (x, h, pz), (x, hy, pz), (x, h, zc)
    sources = {"out": gout, "up": gup, "down": gdown}
    greet(peers_of(x, h, c, z))

    def loaded():
        return (
            (tok_h, tok),
            (q_h, qs),
            (k_h, ks),
            (v_h, vs),
            (o_h, os_),
            (lse_h, lses),
            (wq_h, wqs),
            (idrow_h, idrow),
            (idcol_h, idcol),
            (dr1, dr),
            (gvec, gva),
            (dc_h, dc),
        )

    for k, (src, dst) in enumerate(loaded()):
        pltpu.make_async_copy(src, dst, in_sem.at[k]).start()
    def part_of(n):
        name, shape, row, col = JOBS[n]
        return sources[name], (pl.ds(row, shape[0]), pl.ds(col, shape[1]))

    def cross(n, source, part):
        remote(
            source.at[(1 - x, y, pl.ds(0, cut_of(n))) + part],
            r1as[n],
            s1_ss.at[n, 0],
            s1_rs.at[n, 0],
            to_x,
        ).start()
        remote(
            source.at[(x, 1 - y, pl.ds(cut_of(n), 4 - cut_of(n))) + part],
            r1bs[n],
            s1_ss.at[n, 1],
            s1_rs.at[n, 1],
            to_y,
        ).start()

    def stage1(n):
        src, part = part_of(n)
        acc = accs[n]
        if n < EARLY_JOBS:
            cross(n, src, part)
            pltpu.make_async_copy(
                src.at[(x, y, pl.ds(0, 4)) + part], acc.at[x, y], own_ss.at[n, 0]
            ).start()
            return
        for k in range(2):
            remote(
                src.at[(k, 1 - y, pl.ds(0, RCUT)) + part],
                r2as[n].at[k],
                s2_ss.at[n, k],
                s2_rs.at[n, k],
                to_y,
            ).start()
            remote(
                src.at[(1 - x, k, pl.ds(RCUT, 4 - RCUT)) + part],
                r2bs[n].at[k],
                s2_ss.at[n, 2 + k],
                s2_rs.at[n, 2 + k],
                to_x,
            ).start()
        for k in range(2):
            pltpu.make_async_copy(
                src.at[(k, y, pl.ds(0, RCUT)) + part], acc.at[k, y, pl.ds(0, RCUT)], own_ss.at[n, k]
            ).start()
            pltpu.make_async_copy(
                src.at[(x, k, pl.ds(RCUT, 4 - RCUT)) + part],
                acc.at[x, k, pl.ds(RCUT, 4 - RCUT)],
                own_ss.at[n, 2 + k],
            ).start()

    for n in range(count):
        stage1(n)
    def stage2(n):
        acc = accs[n]
        if n < EARLY_JOBS:
            wait_for(acc.at[x, y], own_ss.at[n, 0])
            return
        for k in range(2):
            wait_for(r2as[n].at[k], s2_rs.at[n, k])
            wait_for(r2bs[n].at[k], s2_rs.at[n, 2 + k])
            wait_for(r2as[n].at[k], own_ss.at[n, k])
            wait_for(r2bs[n].at[k], own_ss.at[n, 2 + k])
        for k in range(2):
            for q in range(RCUT):
                add_block(acc.at[k, y, q], r2as[n].at[k, q])
            for q in range(4 - RCUT):
                add_block(acc.at[x, k, RCUT + q], r2bs[n].at[k, q])
        cross(n, acc, ())

    def stage3(n):
        acc = accs[n]
        wait_for(r1as[n], s1_rs.at[n, 0])
        wait_for(r1bs[n], s1_rs.at[n, 1])
        for q in range(cut_of(n)):
            add_block(acc.at[x, y, q], r1as[n].at[q])
        for q in range(4 - cut_of(n)):
            add_block(acc.at[x, y, cut_of(n) + q], r1bs[n].at[q])
        for k in range(1, 4):
            zz = lax.rem(z + k, 4)
            remote(
                acc.at[x, y, zz], rzs[n].at[z], z_ss.at[n, k - 1], z_rs.at[n, z], (x, h, zz)
            ).start()

    def stage4(n):
        acc = accs[n]
        name, shape, row, col = JOBS[n]
        total = acc[x, y, z].astype(jnp.float32)
        for k in range(1, 4):
            zz = lax.rem(z + k, 4)
            wait_for(rzs[n].at[zz], z_rs.at[n, zz])
            total = total + rzs[n][zz].astype(jnp.float32)
        out = {"out": gout_o, "up": gup_o, "down": gdown_o}[name]
        out[row : row + shape[0], col : col + shape[1]] = total

    for k, (src, dst) in enumerate(loaded()):
        wait_for(dst, in_sem.at[k])

    def attend(zz):
        rows = slice(zz * 256, zz * 256 + 256)
        first = pl.ds(pl.multiple_of((zz * 4 + c) * 128, 128), 128)
        second = pl.ds(pl.multiple_of((zz * 4 + 2 + c) * 128, 128), 128)
        idq = jnp.concatenate([idrow[0:1, first], idrow[0:1, second]], axis=1)
        mask = idcol[:, 0:1] == idq
        both = jnp.concatenate([dc[2 * zz], dc[2 * zz + 1]], axis=0)
        for hh in range(3):
            douts[hh] = both[:, 64 * hh : 64 * hh + 64]

        def one_head(hh, carry):
            dout = douts[hh]
            q = qs[hh, rows, :]
            delta = jnp.sum(dout.astype(jnp.float32) * os_[hh, rows, :], axis=-1, keepdims=True)
            delta = jnp.transpose(jnp.broadcast_to(delta, (256, 128)))[0:1, :]
            scores = jnp.where(mask, nt(ks[hh], q), MASKED)
            probs = jnp.exp(scores - lses[hh, 0:1, rows])
            dprobs = nt(vs[hh], dout)
            ds = (probs * (dprobs - delta)).astype(jnp.bfloat16)
            dk = nn(ds, q)
            dv = nn(probs.astype(jnp.bfloat16), dout)
            if zz == 0:
                dks[hh] = dk
                dvs[hh] = dv
            else:
                dks[hh] += dk
                dvs[hh] += dv
            dqs[hh, rows, :] = (tn(ds, ks[hh]) * SCALE).astype(jnp.bfloat16)
            return carry

        lax.fori_loop(0, 3, one_head, 0)

    def add_gv(k):
        wait_for(gva, gv_rs.at[k])
        wait_for(gva, gv_ss.at[k])
        gva[...] = gva[...] + gvr[k]

    def gv_stage(n):
        if n < 3:
            if n > 0:
                add_gv(n - 1)
            remote(gva, gvr.at[n], gv_ss.at[n], gv_rs.at[n], (to_c, to_x, to_y)[n]).start()
        elif n == 3:
            add_gv(2)
            for k in range(1, 4):
                remote(
                    gva,
                    gvr.at[3 + z],
                    gv_ss.at[2 + k],
                    gv_rs.at[3 + z],
                    (x, h, lax.rem(z + k, 4)),
                ).start()
        else:
            gv = gva[...]
            for k in range(1, 4):
                zz = lax.rem(z + k, 4)
                wait_for(gvr.at[3 + zz], gv_rs.at[3 + zz])
                gv = gv + gvr[3 + zz]
            gvr[3 + z] = gv

    gv_stage(0)
    beside = {
        0: ((stage2, 0), (stage3, 0)),
        1: ((stage2, 1),),
        2: ((stage2, 2), (stage3, 1)),
    }
    for t in range(4):
        attend(t)
        gv_stage(t + 1)
        for stage, n in beside.get(t, ()):
            stage(n)

    for j in range(8):
        p = (j // 2) * 4 + (j % 2) * 2 + 1 - c
        rows = pl.ds(pl.multiple_of(p * 128, 128), 128)
        kv_send[j] = jnp.concatenate(
            [dks[hh, rows, :] for hh in range(3)] + [dvs[hh, rows, :] for hh in range(3)], axis=1
        ).astype(jnp.bfloat16)
    remote(kv_send, kv_recv, kv_ss, kv_rs, to_c).start()
    stage2(3)
    stage3(2)
    wait_for(kv_recv, kv_rs)

    qsum = jnp.zeros((1, 192), jnp.float32)
    vsum = jnp.zeros((1, 192), jnp.float32)
    for j in range(8):
        p = (j // 2) * 4 + (j % 2) * 2 + c
        rows = pl.ds(pl.multiple_of(p * 128, 128), 128)
        wide = jnp.concatenate(
            [dks[hh, rows, :] for hh in range(3)] + [dvs[hh, rows, :] for hh in range(3)], axis=1
        )
        wide = (wide + kv_recv[j].astype(jnp.float32)).astype(jnp.bfloat16)
        part = jnp.concatenate([dqs[hh, 128 * j : 128 * j + 128, :] for hh in range(3)], axis=1)
        dmix[128 * j : 128 * j + 128, :] = jnp.concatenate([part, wide], axis=1)
        qsum = qsum + jnp.sum(part.astype(jnp.float32), axis=0, keepdims=True)
        vsum = vsum + jnp.sum(wide[:, 192:].astype(jnp.float32), axis=0, keepdims=True)
    none = jnp.zeros((1, 192), jnp.float32)
    qb[...] = jnp.broadcast_to(
        jnp.concatenate([qsum, none, vsum, none[:, :64]], axis=1), (8, 640)
    )
    remote(qb, qbr.at[0], qb_ss.at[0], qb_rs.at[0], to_c).start()

    for j in range(8):
        zz, yy = j // 2, j % 2
        dx[j] = nt(dmix[128 * j : 128 * j + 128, :], wqs[...]).astype(jnp.bfloat16)
        slot = zz // 2
        stay = jnp.logical_and(zl == zz % 2, y == yy)

        @pl.when(jnp.logical_not(stay))
        def _():
            remote(
                dx.at[j],
                rx.at[g, slot],
                dx_ss.at[j],
                dx_rs.at[g, slot],
                (x, yy * 2 + c, 2 * pi + zz % 2),
            ).start()

        @pl.when(stay)
        def _():
            pltpu.make_async_copy(dx.at[j], rx.at[g, slot], dx_rs.at[g, slot]).start()

    total = jnp.zeros((768, 576), jnp.float32)
    for zz in range(4):
        left = jnp.concatenate([tok[zz * 4 + c], tok[zz * 4 + 2 + c]], axis=0)
        total = total + tn(left, dmix[256 * zz : 256 * zz + 256, :])
    for xs in range(2):
        for hs in range(4):
            for zz in range(4):
                base = (xs * 16 + hs * 4 + zz) * 24
                gq[hs % 2, xs, zz // 2, 2 * (zz % 2) + hs // 2] = total[base : base + 24].astype(jnp.bfloat16)
    remote(gq.at[1 - c], gqc, gq_ss.at[0], gq_rs.at[0], to_c).start()
    stage3(3)
    stage4(0)

    def add_qb(k):
        wait_for(qb, qb_rs.at[k])
        wait_for(qb, qb_ss.at[k])
        qb[...] = qb[...] + qbr[k]

    wait_for(gqc, gq_rs.at[0])

    def addq(t, carry):
        i, q = lax.div(t, 4), lax.rem(t, 4)
        xs, pp = lax.div(i, 2), lax.rem(i, 2)
        add_block(gq.at[c, xs, pp, q], gqc.at[xs, pp, q])
        return carry

    lax.fori_loop(0, 16, addq, 0)
    remote(gq.at[c, 1 - x], gqx, gq_ss.at[1], gq_rs.at[1], to_x).start()
    add_qb(0)
    remote(qb, qbr.at[1], qb_ss.at[1], qb_rs.at[1], to_x).start()
    wait_for(gqx, gq_rs.at[1])

    def addx(t, carry):
        pp, q = lax.div(t, 4), lax.rem(t, 4)
        add_block(gq.at[c, x, pp, q], gqx.at[pp, q])
        return carry

    lax.fori_loop(0, 8, addx, 0)
    remote(gq.at[c, x, 1 - pi], gqz, gq_ss.at[2], gq_rs.at[2], to_z).start()
    add_qb(1)
    remote(qb, qbr.at[2], qb_ss.at[2], qb_rs.at[2], to_z).start()
    stage4(1)

    for s in range(2):
        acc = dr[s]
        for q in range(4):
            wait_for(rx.at[q, s], dx_rs.at[q, s])
            acc = acc + rx[q, s].astype(jnp.float32)
        gt_send[s] = acc.astype(jnp.bfloat16)
        zz = 2 * s + zl
        row = pi
        stay = pi == s

        @pl.when(stay)
        def _():
            pltpu.make_async_copy(gt_send.at[s], gt_in.at[row], gt_rs.at[row]).start()

        @pl.when(jnp.logical_not(stay))
        def _():
            remote(gt_send.at[s], gt_in.at[row], gt_ss.at[s], gt_rs.at[row], to_z).start()

    wait_for(gqz, gq_rs.at[2])
    for q in range(4):
        add_block(gq.at[c, x, pi, q], gqz.at[q])
    add_qb(2)
    gqzs = gq.at[c, x, pi]
    for k, (dev, target) in enumerate(
        ((to_n, 2 * (1 - zl) + y), (to_y, 2 * zl + 1 - y), (to_d, 2 * (1 - zl) + 1 - y))
    ):
        remote(gqzs.at[target], gqin.at[g], gq_ss.at[3 + k], gq_rs.at[3 + g], dev).start()
        remote(qb, qb_o.at[g], qb_ss.at[3 + k], qb_rs.at[3 + g], dev).start()
    pltpu.make_async_copy(gqzs.at[g], gqin.at[g], gq_rs.at[3 + g]).start()
    pltpu.make_async_copy(qb, qb_o.at[g], qb_rs.at[3 + g]).start()
    stage4(2)
    for q in range(4):
        wait_for(gqin.at[q], gq_rs.at[3 + q])
        wait_for(qb_o.at[q], qb_rs.at[3 + q])
        gq_o[q] = gqin[q].astype(jnp.float32)
    me = x * 16 + h * 4 + z
    vectors = gvr[3 + z]
    own_rows = pltpu.roll(vectors[0:8, :], lax.rem(768 - 24 * me, 768), 1)[:, 0:128]
    up_row = jnp.zeros((1, 768), jnp.float32)
    for i in range(4):
        up_row = up_row + jnp.where(lax.div(me, 8) == i, vectors[6 + i : 7 + i, :], 0.0)
    up_rows = jnp.broadcast_to(up_row, (8, 768))
    up_rows = pltpu.roll(up_rows, lax.rem(768 - 96 * lax.rem(me, 8), 768), 1)[:, 0:128]
    qv_rows = pltpu.roll(qb_o[h], lax.rem(640 - 48 * z - 384 * x, 640), 1)[:, 0:128]
    line = lax.broadcasted_iota(jnp.int32, (8, 128), 0)
    small_o[...] = jnp.where(line < 6, own_rows, jnp.where(line == 6, up_rows, qv_rows))
    stage4(3)
    for i in range(2):
        wait_for(gt_in.at[i], gt_rs.at[i])
        gt_out[i] = gt_in[i].astype(jnp.float32)

    for s in range(2):

        @pl.when(pi != s)
        def _():
            wait_for(gt_send.at[s], gt_ss.at[s])

    for n in range(count):
        for k in range(2 if n >= EARLY_JOBS else 0):
            wait_for(r1as[n], s2_ss.at[n, k])
            wait_for(r1bs[n], s2_ss.at[n, 2 + k])
        wait_for(r1as[n], s1_ss.at[n, 0])
        wait_for(r1bs[n], s1_ss.at[n, 1])
        for k in range(3):
            wait_for(rzs[n].at[0], z_ss.at[n, k])
    wait_for(kv_send, kv_ss)
    for j in range(8):
        stay = jnp.logical_and(zl == (j // 2) % 2, y == j % 2)

        @pl.when(jnp.logical_not(stay))
        def _():
            wait_for(dx.at[j], dx_ss.at[j])

    wait_for(gqc, gq_ss.at[0])
    wait_for(gqx, gq_ss.at[1])
    wait_for(gqz, gq_ss.at[2])
    for k in range(3):
        wait_for(gqin.at[0], gq_ss.at[3 + k])
        wait_for(qb, qb_ss.at[3 + k])
        wait_for(gva, gv_ss.at[3 + k])


def backward_call(*args):
    bf, f32 = jnp.bfloat16, jnp.float32
    sds = jax.ShapeDtypeStruct
    dma = pltpu.SemaphoreType.DMA
    vm = pltpu.VMEM
    outs = [
        sds((2, 128, 768), f32),
        sds((24, 768), f32),
        sds((24, 3072), f32),
        sds((96, 768), f32),
        sds((4, 24, 576), f32),
        sds((8, 128), f32),
    ]
    shapes = [job[1] for job in JOBS]
    count = len(JOBS)
    scratch = (
        [vm((2, 2, 4) + s, bf) for s in shapes]
        + [vm((2, RCUT) + s, bf) for s in shapes]
        + [vm((2, 4 - RCUT) + s, bf) for s in shapes]
        + [vm((cut_of(n),) + s, bf) for n, s in enumerate(shapes)]
        + [vm((4 - cut_of(n),) + s, bf) for n, s in enumerate(shapes)]
        + [vm((4,) + s, bf) for s in shapes]
        + [
            vm((16, 128, 768), bf),
            vm((3, 1024, 64), bf),
            vm((3, 2048, 64), bf),
            vm((3, 2048, 64), bf),
            vm((3, 1024, 64), f32),
            vm((3, 8, 1024), f32),
            vm((768, 576), bf),
            vm((8, 2048), f32),
            vm((2048, 128), f32),
            vm((8, 128, 192), bf),
            vm((3, 2048, 64), f32),
            vm((3, 2048, 64), f32),
            vm((3, 1024, 64), bf),
            vm((3, 256, 64), bf),
            vm((8, 128, 384), bf),
            vm((8, 128, 384), bf),
            vm((1024, 576), bf),
            vm((8, 128, 768), bf),
            vm((4, 2, 128, 768), bf),
            vm((2, 128, 768), f32),
            vm((2, 128, 768), bf),
            vm((2, 128, 768), bf),
            vm((2, 2, 2, 4, 24, 576), bf),
            vm((2, 2, 4, 24, 576), bf),
            vm((2, 4, 24, 576), bf),
            vm((4, 24, 576), bf),
            vm((4, 24, 576), bf),
            vm((16, 768), f32),
            vm((7, 16, 768), f32),
            vm((8, 640), f32),
            vm((3, 8, 640), f32),
            vm((4, 8, 640), f32),
            dma((12,)),
            dma((count, 4)),
            dma((count, 4)),
            dma((count, 4)),
            dma((count, 2)),
            dma((count, 2)),
            dma((count, 3)),
            dma((count, 4)),
            dma(()),
            dma(()),
            dma((8,)),
            dma((4, 2)),
            dma((2,)),
            dma((2,)),
            dma((6,)),
            dma((7,)),
            dma((6,)),
            dma((7,)),
            dma((6,)),
            dma((7,)),
        ]
    )
    here = pl.BlockSpec(memory_space=pltpu.VMEM)
    far = pl.BlockSpec(memory_space=ANY)
    return pl.pallas_call(
        backward_kernel,
        out_shape=outs,
        in_specs=[far] * 15,
        out_specs=[here] * 6,
        scratch_shapes=scratch,
        compiler_params=pltpu.CompilerParams(
            collective_id=1, has_side_effects=True, vmem_limit_bytes=VMEM_LIMIT
        ),
        name="backward",
    )(*args)


def finish_kernel(lo, gt, gq, gout, gup, gdown, small, lo_o, gt_o, gqkv_o, gout_o, gup_o, gdown_o, *vectors):
    for src, dst in ((lo, lo_o), (gt, gt_o), (gout, gout_o), (gup, gup_o), (gdown, gdown_o)):
        dst[...] = src[...]
    for part in range(3):
        gqkv_o[:, 768 * part : 768 * part + 768] = jnp.concatenate(
            [gq[q, :, 192 * part : 192 * part + 192] for q in range(4)], axis=1
        )
    for k, dst in enumerate(vectors):
        dst[...] = small[k : k + 1, : dst.shape[1]]


def finish_call(lo, gt, gq, gout, gup, gdown, small):
    f32 = jnp.float32
    here = pl.BlockSpec(memory_space=pltpu.VMEM)
    like = lambda a: jax.ShapeDtypeStruct(a.shape, a.dtype)
    wide = jax.ShapeDtypeStruct((24, 2304), f32)
    outs = [like(lo), like(gt), wide, like(gout), like(gup), like(gdown)]
    outs += [jax.ShapeDtypeStruct((1, width), f32) for width in (24,) * 6 + (96, 48)]
    return pl.pallas_call(
        finish_kernel,
        out_shape=outs,
        in_specs=[here] * 7,
        out_specs=[here] * len(outs),
        compiler_params=pltpu.CompilerParams(vmem_limit_bytes=VMEM_LIMIT),
        name="finish",
    )(lo, gt, gq, gout, gup, gdown, small)


def slab_body(
    tokens,
    segments,
    qkv_weight,
    qv_bias,
    out_weight,
    out_bias,
    attn_gain,
    attn_shift,
    up_weight,
    up_bias,
    down_weight,
    down_bias,
    ffn_gain,
    ffn_shift,
    cotangent,
):
    rows24 = jnp.stack([out_bias, attn_gain, attn_shift, down_bias, ffn_gain, ffn_shift])
    (
        grad_first,
        gvec,
        lo_out,
        dc_all,
        grad_out,
        grad_up,
        grad_down,
        tok_all,
        q_all,
        k_all,
        v_all,
        o_all,
        lse_all,
        wq_all,
        idrow_all,
        idcol_all,
    ) = forward_call(
        tokens,
        cotangent,
        segments,
        qkv_weight,
        out_weight,
        up_weight,
        down_weight,
        rows24,
        up_bias.reshape(1, 96),
        qv_bias.reshape(1, 48),
    )
    gt_out, gout_o, gup_o, gdown_o, gq_o, small = backward_call(
        dc_all,
        grad_first,
        grad_out.reshape(2, 2, 4, 24, 768),
        grad_up.reshape(2, 2, 4, 24, 3072),
        grad_down.reshape(2, 2, 4, 96, 768),
        gvec,
        tok_all,
        q_all,
        k_all,
        v_all,
        o_all,
        lse_all,
        wq_all,
        idrow_all,
        idcol_all,
    )
    lo_out, gt_out, gqkv, gout_o, gup_o, gdown_o, *vectors = finish_call(
        lo_out, gt_out, gq_o, gout_o, gup_o, gdown_o, small
    )
    rows = [vector.reshape(vector.shape[1]) for vector in vectors]
    return (
        lo_out,
        gt_out,
        gqkv,
        rows[7],
        gout_o,
        rows[0],
        rows[1],
        rows[2],
        gup_o,
        rows[6],
        gdown_o,
        rows[3],
        rows[4],
        rows[5],
    )


def solution(mesh):
    sizes = tuple(mesh.shape[name] for name in ("dp", "head", "blk"))
    body = slab_body if sizes == (2, 4, 4) else general_body
    placed = (
        P("dp", ("blk", "head"), None),
        P("dp", ("blk", "head")),
        P(("dp", "head", "blk"), None),
        P(("dp", "head", "blk")),
        P(("dp", "head", "blk"), None),
        P(("dp", "head", "blk")),
        P(("dp", "head", "blk")),
        P(("dp", "head", "blk")),
        P(("dp", "head", "blk"), None),
        P(("dp", "head", "blk")),
        P(("dp", "head", "blk"), None),
        P(("dp", "head", "blk")),
        P(("dp", "head", "blk")),
        P(("dp", "head", "blk")),
        P("dp", ("blk", "head"), None),
    )
    return jax.shard_map(
        body,
        mesh=mesh,
        in_specs=placed,
        out_specs=(
            P("dp", ("blk", "head"), None),
            P("dp", ("blk", "head"), None),
            P(("dp", "head", "blk"), None),
            P(("dp", "head", "blk")),
            P(("dp", "head", "blk"), None),
            P(("dp", "head", "blk")),
            P(("dp", "head", "blk")),
            P(("dp", "head", "blk")),
            P(("dp", "head", "blk"), None),
            P(("dp", "head", "blk")),
            P(("dp", "head", "blk"), None),
            P(("dp", "head", "blk")),
            P(("dp", "head", "blk")),
            P(("dp", "head", "blk")),
        ),
        check_vma=False,
    )
```

```python
import math

import jax
import jax.numpy as jnp
from jax import lax
from jax.experimental import pallas as pl
from jax.experimental.pallas import tpu as pltpu
from jax.sharding import PartitionSpec as P

HEADS = 12
HDIM = 64
NSEG = 256


EPS = 1e-12
MASKED = -1e30
SCALE = 0.125


def norm_forward(values_in, gain, shift):
    mean_val = jnp.mean(values_in, axis=-1, keepdims=True)
    centred = values_in - mean_val
    inv_std = lax.rsqrt(jnp.mean(centred * centred, axis=-1, keepdims=True) + EPS)
    normed = centred * inv_std
    return (normed * gain + shift, normed, inv_std)


def norm_backward(grad_in, normed, inv_std, gain):
    scaled = grad_in * gain
    inner_term = (
        scaled
        - jnp.mean(scaled, axis=-1, keepdims=True)
        - normed * jnp.mean(scaled * normed, axis=-1, keepdims=True)
    )
    return (inner_term * inv_std, jnp.sum(grad_in * normed, axis=0), jnp.sum(grad_in, axis=0))


def exact_gelu(values_in):
    return jax.nn.gelu(values_in, approximate=False)


def stretch_scores(queries, key_part, query_seg, key_seg, query_place, key_place):
    scores = (
        jnp.einsum("sqhd,skhd->shqk", queries, key_part, preferred_element_type=jnp.float32) * SCALE
    )
    same_doc = query_seg[:, None, :, None] == key_seg[:, None, None, :]
    own_place = query_place[:, None] == key_place[None, :]
    usable = (query_seg[:, None, :, None] != NSEG - 1) | own_place[None, None]
    return (scores, same_doc & usable)


def slice_keys(key_piece, value_piece, seg_piece, offset, step_rows):
    key_part = lax.dynamic_slice_in_dim(key_piece, offset, step_rows, 1)
    value_part = lax.dynamic_slice_in_dim(value_piece, offset, step_rows, 1)
    seg_part = lax.dynamic_slice_in_dim(seg_piece, offset, step_rows, 1)
    return (key_part, value_part, seg_part)


def part_grads(
    queries,
    grad_ctx,
    log_total,
    row_delta,
    query_seg,
    query_place,
    key_part,
    value_part,
    key_seg,
    key_place,
):
    scores, allowed = stretch_scores(queries, key_part, query_seg, key_seg, query_place, key_place)
    probs = jnp.where(allowed, jnp.exp(scores - log_total[..., None]), 0.0)
    grad_probs = jnp.einsum(
        "sqhd,skhd->shqk", grad_ctx, value_part, preferred_element_type=jnp.float32
    )
    grad_scores = (probs * (grad_probs - row_delta[..., None])).astype(jnp.bfloat16)
    grad_query = (
        jnp.einsum("shqk,skhd->sqhd", grad_scores, key_part, preferred_element_type=jnp.float32)
        * SCALE
    )
    grad_key = (
        jnp.einsum("shqk,sqhd->skhd", grad_scores, queries, preferred_element_type=jnp.float32)
        * SCALE
    )
    grad_value = jnp.einsum(
        "shqk,sqhd->skhd", probs.astype(jnp.bfloat16), grad_ctx, preferred_element_type=jnp.float32
    )
    return (grad_query, grad_key, grad_value)


def general_body(
    tokens,
    segments,
    qkv_weight,
    qv_bias,
    out_weight,
    out_bias,
    attn_gain,
    attn_shift,
    up_weight,
    up_bias,
    down_weight,
    down_bias,
    ffn_gain,
    ffn_shift,
    cotangent,
):
    seq_count, local_rows, model_width = tokens.shape
    group_count = lax.axis_size("head")
    group_width = model_width // group_count
    heads_here = HEADS // group_count
    block_rows = local_rows * group_count
    key_rows = block_rows * lax.axis_size("blk")
    token_count = seq_count * local_rows
    gathered = (
        lax.all_gather(qkv_weight, ("dp", "head", "blk"), axis=0, tiled=True),
        lax.all_gather(qv_bias, ("dp", "head", "blk"), axis=0, tiled=True),
        lax.all_gather(out_weight, ("dp", "head", "blk"), axis=0, tiled=True),
        lax.all_gather(out_bias, ("dp", "head", "blk"), axis=0, tiled=True),
        lax.all_gather(attn_gain, ("dp", "head", "blk"), axis=0, tiled=True),
        lax.all_gather(attn_shift, ("dp", "head", "blk"), axis=0, tiled=True),
        lax.all_gather(up_weight, ("dp", "head", "blk"), axis=0, tiled=True),
        lax.all_gather(up_bias, ("dp", "head", "blk"), axis=0, tiled=True),
        lax.all_gather(down_weight, ("dp", "head", "blk"), axis=0, tiled=True),
        lax.all_gather(down_bias, ("dp", "head", "blk"), axis=0, tiled=True),
        lax.all_gather(ffn_gain, ("dp", "head", "blk"), axis=0, tiled=True),
        lax.all_gather(ffn_shift, ("dp", "head", "blk"), axis=0, tiled=True),
    )
    (
        whole_qkv,
        whole_qv,
        whole_out,
        whole_out_bias,
        whole_attn_gain,
        whole_attn_shift,
        whole_up,
        whole_up_bias,
        whole_down,
        whole_down_bias,
        whole_ffn_gain,
        whole_ffn_shift,
    ) = gathered
    attn_scale = whole_attn_gain.astype(jnp.float32)
    ffn_scale = whole_ffn_gain.astype(jnp.float32)
    flat_tokens = tokens.reshape(token_count, model_width)
    mixed = jnp.dot(flat_tokens, whole_qkv, preferred_element_type=jnp.float32)
    bias_row = jnp.concatenate(
        [whole_qv[:model_width], jnp.zeros((model_width,), jnp.bfloat16), whole_qv[model_width:]]
    ).astype(jnp.float32)
    mixed_low = (mixed + bias_row).astype(jnp.bfloat16)
    grouped = (
        mixed_low.reshape(seq_count, local_rows, 3, group_count, group_width)
        .transpose(0, 1, 3, 2, 4)
        .reshape(seq_count, local_rows, group_count, 3 * group_width)
    )
    seg_copies = jnp.broadcast_to(
        segments.astype(jnp.bfloat16)[:, :, None, None], (seq_count, local_rows, group_count, 1)
    )
    arrived, seg_arrived = (
        lax.all_to_all(grouped, "head", split_axis=2, concat_axis=1, tiled=True),
        lax.all_to_all(seg_copies, "head", split_axis=2, concat_axis=1, tiled=True),
    )
    arrived = arrived.reshape(seq_count, block_rows, 3, heads_here, HDIM)
    queries = arrived[:, :, 0]
    keys_here = arrived[:, :, 1]
    values_here = arrived[:, :, 2]
    query_seg = seg_arrived.reshape(seq_count, block_rows)
    query_place = lax.axis_index("blk") * block_rows + jnp.arange(block_rows)
    row_shape = (seq_count, heads_here, block_rows)
    start_state = (
        jnp.full(row_shape, MASKED, jnp.float32),
        jnp.zeros(row_shape, jnp.float32),
        jnp.zeros(row_shape + (HDIM,), jnp.float32),
    )
    key_piece = lax.all_gather(keys_here, "blk", axis=1, tiled=True)
    value_piece = lax.all_gather(values_here, "blk", axis=1, tiled=True)
    seg_piece = lax.all_gather(query_seg, "blk", axis=1, tiled=True)
    piece_rows = key_piece.shape[1]
    step_rows = math.gcd(piece_rows, 512)

    def attend_one_step(state_in, step_index):
        offset = step_index * step_rows
        key_part, value_part, key_seg = slice_keys(
            key_piece, value_piece, seg_piece, offset, step_rows
        )
        key_place = offset + jnp.arange(step_rows)
        best, total, accum = state_in
        scores, allowed = stretch_scores(
            queries, key_part, query_seg, key_seg, query_place, key_place
        )
        new_best = jnp.maximum(best, jnp.max(jnp.where(allowed, scores, MASKED), axis=-1))
        weights = jnp.where(allowed, jnp.exp(scores - new_best[..., None]), 0.0)
        factor = jnp.exp(best - new_best)
        total = total * factor + jnp.sum(weights, axis=-1)
        accum = accum * factor[..., None] + jnp.einsum(
            "shqk,skhd->shqd",
            weights.astype(jnp.bfloat16),
            value_part,
            preferred_element_type=jnp.float32,
        )
        return ((new_best, total, accum), None)

    result, unused = lax.scan(attend_one_step, start_state, jnp.arange(piece_rows // step_rows))
    best, total, accum = result
    context = accum / total[..., None]
    log_total = best + jnp.log(total)
    context_low = (
        context.astype(jnp.bfloat16)
        .transpose(0, 2, 1, 3)
        .reshape(seq_count, block_rows, 1, group_width)
    )
    returned_ctx = lax.all_to_all(context_low, "head", split_axis=1, concat_axis=2, tiled=True)
    ctx_tokens = returned_ctx.reshape(token_count, model_width)
    attended = jnp.dot(
        ctx_tokens, whole_out, preferred_element_type=jnp.float32
    ) + whole_out_bias.astype(jnp.float32)
    first_sum = flat_tokens.astype(jnp.float32) + attended
    hidden, normed_one, inv_one = norm_forward(
        first_sum, attn_scale, whole_attn_shift.astype(jnp.float32)
    )
    hidden_low = hidden.astype(jnp.bfloat16)
    inner = jnp.dot(
        hidden_low, whole_up, preferred_element_type=jnp.float32
    ) + whole_up_bias.astype(jnp.float32)
    active, gelu_pull = jax.vjp(exact_gelu, inner)
    active_low = active.astype(jnp.bfloat16)
    branch = jnp.dot(
        active_low, whole_down, preferred_element_type=jnp.float32
    ) + whole_down_bias.astype(jnp.float32)
    final, normed_two, inv_two = norm_forward(
        hidden + branch, ffn_scale, whole_ffn_shift.astype(jnp.float32)
    )
    layer_out = final.astype(jnp.bfloat16).reshape(seq_count, local_rows, model_width)
    grad_final = cotangent.reshape(token_count, model_width).astype(jnp.float32)
    grad_second, grad_ffn_gain, grad_ffn_shift = norm_backward(
        grad_final, normed_two, inv_two, ffn_scale
    )
    grad_branch = grad_second.astype(jnp.bfloat16)
    grad_down = jnp.dot(active_low.T, grad_branch, preferred_element_type=jnp.float32)
    grad_down_bias = jnp.sum(grad_branch.astype(jnp.float32), axis=0)
    grad_active = jnp.dot(grad_branch, whole_down.T, preferred_element_type=jnp.float32)
    grad_inner = gelu_pull(grad_active)[0].astype(jnp.bfloat16)
    grad_up = jnp.dot(hidden_low.T, grad_inner, preferred_element_type=jnp.float32)
    grad_up_bias = jnp.sum(grad_inner.astype(jnp.float32), axis=0)
    grad_hidden = grad_second + jnp.dot(grad_inner, whole_up.T, preferred_element_type=jnp.float32)
    grad_first, grad_attn_gain, grad_attn_shift = norm_backward(
        grad_hidden, normed_one, inv_one, attn_scale
    )
    grad_attended = grad_first.astype(jnp.bfloat16)
    grad_out = jnp.dot(ctx_tokens.T, grad_attended, preferred_element_type=jnp.float32)
    grad_out_bias = jnp.sum(grad_attended.astype(jnp.float32), axis=0)
    grad_context = jnp.dot(grad_attended, whole_out.T, preferred_element_type=jnp.float32).astype(
        jnp.bfloat16
    )
    grad_sent = lax.all_to_all(
        grad_context.reshape(seq_count, local_rows, group_count, group_width),
        "head",
        split_axis=2,
        concat_axis=1,
        tiled=True,
    )
    grad_ctx = grad_sent.reshape(seq_count, block_rows, heads_here, HDIM)
    row_delta = jnp.einsum("sqhd,shqd->shq", grad_ctx.astype(jnp.float32), context)
    query_zero = jnp.zeros((seq_count, block_rows, heads_here, HDIM), jnp.float32)
    zero_keys = jnp.zeros((seq_count, key_rows, heads_here, HDIM), jnp.float32)
    gather_key_piece = lax.all_gather(keys_here, "blk", axis=1, tiled=True)
    gather_value_piece = lax.all_gather(values_here, "blk", axis=1, tiled=True)
    gather_seg_piece = lax.all_gather(query_seg, "blk", axis=1, tiled=True)
    piece_rows = gather_key_piece.shape[1]
    gather_step_rows = math.gcd(piece_rows, 512)

    def gather_one_step(state_in, step_index):
        offset = step_index * gather_step_rows
        key_part, value_part, key_seg = slice_keys(
            gather_key_piece, gather_value_piece, gather_seg_piece, offset, gather_step_rows
        )
        key_place = offset + jnp.arange(gather_step_rows)
        grad_q, grad_k, grad_v = state_in
        part_q, part_k, part_v = part_grads(
            queries,
            grad_ctx,
            log_total,
            row_delta,
            query_seg,
            query_place,
            key_part,
            value_part,
            key_seg,
            key_place,
        )
        grad_k = lax.dynamic_update_slice_in_dim(
            grad_k,
            lax.dynamic_slice_in_dim(grad_k, offset, gather_step_rows, 1) + part_k,
            offset,
            1,
        )
        grad_v = lax.dynamic_update_slice_in_dim(
            grad_v,
            lax.dynamic_slice_in_dim(grad_v, offset, gather_step_rows, 1) + part_v,
            offset,
            1,
        )
        return ((grad_q + part_q, grad_k, grad_v), None)

    result, unused = lax.scan(
        gather_one_step,
        (query_zero, zero_keys, zero_keys),
        jnp.arange(piece_rows // gather_step_rows),
    )
    grad_q, all_keys, all_values = result
    grad_k, grad_v = (
        lax.psum_scatter(
            all_keys.astype(jnp.bfloat16), "blk", scatter_dimension=1, tiled=True
        ).astype(jnp.float32),
        lax.psum_scatter(
            all_values.astype(jnp.bfloat16), "blk", scatter_dimension=1, tiled=True
        ).astype(jnp.float32),
    )
    grad_low = jnp.concatenate(
        [
            grad_q.astype(jnp.bfloat16).reshape(seq_count, block_rows, 1, group_width),
            grad_k.astype(jnp.bfloat16).reshape(seq_count, block_rows, 1, group_width),
            grad_v.astype(jnp.bfloat16).reshape(seq_count, block_rows, 1, group_width),
        ],
        axis=3,
    )
    back_tokens = lax.all_to_all(grad_low, "head", split_axis=1, concat_axis=2, tiled=True)
    grad_mixed = (
        back_tokens.reshape(seq_count, local_rows, group_count, 3, group_width)
        .transpose(0, 1, 3, 2, 4)
        .reshape(token_count, 3 * model_width)
    )
    grad_qkv = jnp.dot(flat_tokens.T, grad_mixed, preferred_element_type=jnp.float32)
    column_sums = jnp.sum(grad_mixed.astype(jnp.float32), axis=0)
    grad_qv = jnp.concatenate([column_sums[:model_width], column_sums[2 * model_width :]])
    grad_tokens = grad_first + jnp.dot(grad_mixed, whole_qkv.T, preferred_element_type=jnp.float32)
    summed = (
        lax.psum_scatter(grad_qkv, ("dp", "head", "blk"), scatter_dimension=0, tiled=True),
        lax.psum_scatter(grad_qv, ("dp", "head", "blk"), scatter_dimension=0, tiled=True),
        lax.psum_scatter(grad_out, ("dp", "head", "blk"), scatter_dimension=0, tiled=True),
        lax.psum_scatter(grad_out_bias, ("dp", "head", "blk"), scatter_dimension=0, tiled=True),
        lax.psum_scatter(grad_attn_gain, ("dp", "head", "blk"), scatter_dimension=0, tiled=True),
        lax.psum_scatter(grad_attn_shift, ("dp", "head", "blk"), scatter_dimension=0, tiled=True),
        lax.psum_scatter(grad_up, ("dp", "head", "blk"), scatter_dimension=0, tiled=True),
        lax.psum_scatter(grad_up_bias, ("dp", "head", "blk"), scatter_dimension=0, tiled=True),
        lax.psum_scatter(grad_down, ("dp", "head", "blk"), scatter_dimension=0, tiled=True),
        lax.psum_scatter(grad_down_bias, ("dp", "head", "blk"), scatter_dimension=0, tiled=True),
        lax.psum_scatter(grad_ffn_gain, ("dp", "head", "blk"), scatter_dimension=0, tiled=True),
        lax.psum_scatter(grad_ffn_shift, ("dp", "head", "blk"), scatter_dimension=0, tiled=True),
    )
    return (
        layer_out,
        grad_tokens.reshape(seq_count, local_rows, model_width),
        summed[0],
        summed[1],
        summed[2],
        summed[3],
        summed[4],
        summed[5],
        summed[6],
        summed[7],
        summed[8],
        summed[9],
        summed[10],
        summed[11],
    )


MESH = pl.DeviceIdType.MESH
ANY = pl.ANY
VMEM_LIMIT = 60 * 1024 * 1024


def remote(src, dst, send_sem, recv_sem, device):
    return pltpu.make_async_remote_copy(
        src_ref=src,
        dst_ref=dst,
        send_sem=send_sem,
        recv_sem=recv_sem,
        device_id=device,
        device_id_type=MESH,
    )


def wait_for(ref, sem):
    pltpu.make_async_copy(ref, ref, sem).wait()


def place():
    x, h, z = lax.axis_index("dp"), lax.axis_index("head"), lax.axis_index("blk")
    return x, lax.div(h, 2), lax.rem(h, 2), h, z


def greet(peers):
    barrier = pltpu.get_barrier_semaphore()
    for peer in peers:
        pl.semaphore_signal(barrier, inc=1, device_id=peer, device_id_type=MESH)
    pl.semaphore_wait(barrier, len(peers))


def peers_of(x, h, c, z):
    around = [(x, h, lax.rem(z + k, 4)) for k in (1, 2, 3)]
    other = lax.rem(h + 2, 4)
    beside = z + 1 - 2 * lax.rem(z, 2)
    return around + [(1 - x, h, z), (x, other, z), (x, other, beside), (x, h + 1 - 2 * c, z)]


def nt(left, right):
    return lax.dot_general(left, right, (((1,), (1,)), ((), ())), preferred_element_type=jnp.float32)


def tn(left, right):
    return lax.dot_general(left, right, (((0,), (0,)), ((), ())), preferred_element_type=jnp.float32)


def nn(left, right):
    return jnp.dot(left, right, preferred_element_type=jnp.float32)


def add_norm(values_in):
    mean_val = jnp.mean(values_in, axis=-1, keepdims=True)
    centred = values_in - mean_val
    inv_std = lax.rsqrt(jnp.mean(centred * centred, axis=-1, keepdims=True) + EPS)
    return centred * inv_std, inv_std


def norm_pull(scaled, normed, inv_std):
    return inv_std * (
        scaled
        - jnp.mean(scaled, axis=-1, keepdims=True)
        - normed * jnp.mean(scaled * normed, axis=-1, keepdims=True)
    )


def column_sum(values_in):
    return jnp.sum(values_in, axis=0, keepdims=True)


CUT = 2
EARLY = 0
AHEAD = 1
BESIDE_TOKENS = {
    99: ((0, 0),),
    100: ((1, 0),),
    101: ((1, 1),),
    102: ((1, 2),),
    103: ((1, 3),),
    105: ((1, 4),),
    111: ((1, 5),),
    112: ((1, 6),),
}
LATE = 1
LATE_STEP = 7
WQ_STEPS = (4, 5, 8)
SUB = 2
ROWS_SUB = 64
PIECES = (
    ("out", (24, 768), 0, 0),
    ("up", (24, 1536), 0, 0),
    ("up", (24, 1536), 0, 1536),
    ("down", (48, 768), 0, 0),
    ("down", (48, 768), 48, 0),
)


def forward_kernel(
    tokens,
    cot,
    segments,
    wqkv,
    wout,
    wup,
    wdown,
    rows24,
    up_bias,
    qv_bias,
    dr1,
    gvec,
    lo_out,
    dc_all,
    gout_h,
    gup_h,
    gdown_h,
    tok_all,
    q_all,
    k_all,
    v_all,
    o_all,
    lse_all,
    wq_all,
    idrow_all,
    idcol_all,
    tok,
    land,
    wqs,
    qs,
    ks,
    vs,
    os_,
    lses,
    idrow,
    idcol,
    ctx,
    wout_g,
    wup_g,
    wdown_g,
    win,
    ctx_in,
    cot_in,
    wout_v,
    wup_v,
    active,
    slope,
    go,
    gu,
    gd,
    ro,
    ru,
    rd,
    tok_rs,
    tz_ss,
    tx_ss,
    ty_ss,
    tc_ss,
    cot_ss,
    cot_rs,
    wq_ss,
    wq_rs,
    wz_ss,
    wz_rs,
    wp_ss,
    wp_rs,
    ctx_ss,
    ctx_rs,
    out_sem,
    c_ss,
    c_rs,
    o_sem,
    wq,
    lo,
    dctx,
    r2a,
    r2b,
    lo_ss,
    lo_rs,
    dc_ss,
    dc_rs,
    s2_ss,
    s2_rs,
):
    f32, bf = jnp.float32, jnp.bfloat16
    x, y, c, h, z = place()
    zl, pi = lax.rem(z, 2), lax.div(z, 2)
    g = 2 * zl + y
    me = x * 16 + h * 4 + z
    hy = lax.rem(h + 2, 4)
    hc = h + 1 - 2 * c
    to_x, to_y, to_c = (1 - x, h, z), (x, hy, z), (x, hc, z)
    pz, zc = z + 1 - 2 * zl, lax.rem(z + 2, 4)
    to_n, to_d, to_z = (x, h, pz), (x, hy, pz), (x, h, zc)
    mid = jnp.where(z < 2, 2, 1)
    inner = jnp.logical_or(z == 1, z == 2)
    outer = jnp.logical_not(inner)
    def moved(values, width, steps, index):
        out = None
        for k, start in enumerate(steps):
            ends = []
            if start:
                ends.append(jnp.zeros((values.shape[0], start), f32))
            ends.append(values)
            if width - start - values.shape[1]:
                ends.append(jnp.zeros((values.shape[0], width - start - values.shape[1]), f32))
            row = jnp.concatenate(ends, axis=1)
            out = row if out is None else jnp.where(index == k, row, out)
        return out

    starts = [48 * k for k in range(4)] + [384 + 48 * k for k in range(4)]
    bias_row = moved(qv_bias[...].astype(f32), 576, starts, 4 * x + z)
    six = moved(rows24[...].astype(f32), 128, [24 * k for k in range(4)], z)
    up_row = jnp.concatenate([up_bias[...].astype(f32), jnp.zeros((1, 32), f32)], axis=1)
    ten = [six[k : k + 1] for k in range(6)] + [jnp.where(z == k, up_row, 0.0) for k in range(4)]
    gap = jnp.zeros((1, 64), f32)
    none = jnp.zeros((1, 128), f32)
    slots = [
        jnp.concatenate(ten[0:4] + [gap], axis=1),
        jnp.concatenate(ten[4:8] + [gap], axis=1),
        jnp.concatenate(ten[8:10] + [none, none, gap], axis=1),
    ]
    seg_rows = segments[...].astype(f32)
    seg_rows = [jnp.concatenate([seg_rows[k : k + 1], jnp.zeros((1, 448), f32)], axis=1) for k in range(2)]
    last_rows = jnp.concatenate(slots + seg_rows + [jnp.zeros((2, 576), f32)], axis=0)
    whole = wqkv[...].astype(f32)
    for q in range(4):
        cols = [whole[:, 768 * p + 192 * q : 768 * p + 192 * q + 192] for p in range(3)]
        first_row = jnp.where(h == q, bias_row, 0.0)
        rows = [jnp.concatenate(cols, axis=1), first_row, last_rows]
        wq[q] = jnp.concatenate(rows, axis=0).astype(bf)
    greet(peers_of(x, h, c, z))

    mine = z * 4 + h
    weights = {"out": (wout, wout_g), "up": (wup, wup_g), "down": (wdown, wdown_g)}
    count = len(PIECES)
    base = x * 16 + h * 4
    bx, by = (1 - x) * 16 + h * 4, x * 16 + hy * 4

    def side(start, ab):
        return pl.ds(start, CUT) if ab == 0 else pl.ds(start + CUT, 4 - CUT)

    sa, sb = side(bx, 0), side(by, 1)

    def quad(xs, hs):
        return pl.ds(xs * 16 + hs * 4, 4)

    sent = []

    def shard(n):
        name, shape, row, col = PIECES[n]
        return weights[name][0].at[pl.ds(row, shape[0]), pl.ds(col, shape[1])]

    def at(n, where):
        name, shape, row, col = PIECES[n]
        return weights[name][1].at[where, pl.ds(row, shape[0]), pl.ds(col, shape[1])]

    def two(n):
        return at(n, pl.ds(0, 2))

    def some(n, ab):
        return at(n, side(0, ab))

    def pass_on(n, where, k, sem, dev):
        remote(at(n, where), at(n, where), wp_ss.at[n, k], wp_rs.at[(n,) + sem], dev).start()
        sent.append((n, k))

    def along_z(n):
        pltpu.make_async_copy(shard(n), at(n, me), wz_rs.at[n, z]).start()
        for k, zz in enumerate((pz, mid)):
            remote(shard(n), at(n, me), wz_ss.at[n, k], wz_rs.at[n, z], (x, h, zz)).start()

    def relay(n):
        @pl.when(inner)
        def _():
            there = pl.ds(base + jnp.where(z < 2, 2, 0), 2)
            for k in range(2):
                wait_for(at(n, 0), wz_rs.at[n, jnp.where(z < 2, 2, 0) + k])
            remote(at(n, there), at(n, there), wz_ss.at[n, 2], wz_rs.at[n, 4], (x, h, pz)).start()

    def first_hop(n):
        for k in range(2):
            wait_for(at(n, 0), wz_rs.at[n, jnp.where(z < 2, 0, 2) + k])

        @pl.when(outer)
        def _():
            wait_for(two(n), wz_rs.at[n, 4])

        for k, dev in enumerate((to_x, to_y, to_c)):
            pass_on(n, quad(x, h), k, (x, h, 0), dev)

    def second_hop(n):
        wait_for(at(n, quad(0, 0)), wp_rs.at[n, 1 - x, h, 0])
        wait_for(at(n, quad(0, 0)), wp_rs.at[n, x, hy, 0])
        pass_on(n, sa, 3, (1 - x, h, 0), to_y)
        pass_on(n, sb, 4, (x, hy, 1), to_x)
        pass_on(n, quad(1 - x, h), 5, (1 - x, h, 0), to_c)
        pass_on(n, quad(x, hy), 6, (x, hy, 0), to_c)

    def third_hop(n):
        for ab in range(2):
            wait_for(some(n, ab), wp_rs.at[n, 1 - x, hy, ab])
        pass_on(n, quad(1 - x, hy), 7, (1 - x, hy, 0), to_c)

    def advance(t):
        if t < count:
            first_hop(t)
        if t + AHEAD < count:
            relay(t + AHEAD)
        if 0 <= t - 1 < count:
            second_hop(t - 1)
        if 0 <= t - 2 < count:
            third_hop(t - 2)

    for n in range(EARLY):
        along_z(n)

    cuts = [pl.ds(ROWS_SUB * q, ROWS_SUB) for q in range(SUB)]

    def send_row(i, to):
        for q in range(SUB):
            remote(
                tokens.at[i, cuts[q]], tok.at[mine, cuts[q]], tz_ss.at[i, q], tok_rs.at[mine, q], to
            ).start()

    for i in range(2):

        @pl.when(pi == i)
        def _():
            send_row(i, to_n)
            for q in range(SUB):
                pltpu.make_async_copy(
                    tokens.at[i, cuts[q]], tok.at[mine, cuts[q]], tok_rs.at[mine, q]
                ).start()

        @pl.when(pi != i)
        def _():
            send_row(i, (x, h, 1 + i))

    def run_beside(t):
        for kind, n in BESIDE_TOKENS.get(t, ()):
            relay(n) if kind == 0 else advance(n)

    pltpu.make_async_copy(wq.at[g], land.at[c, x, pi, g], wq_rs.at[c, x, pi, g]).start()
    for k, (dev, target) in enumerate(
        ((to_n, 2 * (1 - zl) + y), (to_y, 2 * zl + 1 - y), (to_d, 2 * (1 - zl) + 1 - y))
    ):
        remote(wq.at[target], land.at[c, x, pi, g], wq_ss.at[k], wq_rs.at[c, x, pi, g], dev).start()

    def give_slices(xs, pp, k, dev):
        block = land.at[c, xs, pp]
        remote(block, block, wq_ss.at[k], wq_rs.at[c, xs, pp, 0], dev).start()

    for q in range(4):
        wait_for(land.at[c, x, pi, q], wq_rs.at[c, x, pi, q])
    give_slices(x, pi, 3, to_z)
    give_slices(x, pi, 4, to_x)
    give_slices(x, pi, 5, to_c)
    for n in range(EARLY, LATE):
        along_z(n)
    turns = (z, pz, zc, lax.rem(pz + 2, 4))

    def hand_on(p, q, sends, keep_sem):
        wait_for(tok.at[p, cuts[q]], tok_rs.at[p, q])
        for sem, dev in sends:
            remote(tok.at[p, cuts[q]], tok.at[p, cuts[q]], sem.at[q], tok_rs.at[p, q], dev).start()
        if q == SUB - 1:
            remote(tok.at[p], tok.at[p], keep_sem, tok_rs.at[p, 0], to_c).start()

    def own_piece(k, q):
        p = turns[k] * 4 + h
        hand_on(p, q, [(ty_ss.at[k], to_y)], tc_ss.at[k])
        if k >= 2:

            @pl.when(inner)
            def _():
                cut = cuts[q]
                remote(
                    tok.at[p, cut], tok.at[p, cut], tx_ss.at[k, q], tok_rs.at[p, q], to_n
                ).start()

    def side_piece(k, q):
        hand_on(turns[k] * 4 + hy, q, [], tc_ss.at[4 + k])

    def slices_step(t):
        if t == WQ_STEPS[0]:
            wait_for(land.at[c, x, 1 - pi], wq_rs.at[c, x, 1 - pi, 0])
            give_slices(x, 1 - pi, 6, to_x)
            give_slices(x, 1 - pi, 7, to_c)
        for k in range(2):
            if t == WQ_STEPS[1 + k]:
                there = (pi, 1 - pi)[k]
                wait_for(land.at[c, 1 - x, there], wq_rs.at[c, 1 - x, there, 0])
                give_slices(1 - x, there, 8 + k, to_c)

    order = [(0, q) for q in range(SUB)] + [(k, q) for q in range(SUB) for k in range(1, 4)]
    lag = 3
    for t in range(len(order) + lag):
        if t < len(order):
            own_piece(*order[t])
        if t >= lag:
            side_piece(*order[t - lag])
        slices_step(t)
        if t == LATE_STEP:
            for n in range(LATE, count):
                along_z(n)
        run_beside(t)

    run_beside(99)
    for i in range(2):

        @pl.when(pi == i)
        def _():
            pltpu.make_async_copy(cot.at[i], cot_in.at[pi], cot_rs.at[pi]).start()

        @pl.when(pi != i)
        def _():
            remote(cot.at[i], cot_in.at[pi], cot_ss, cot_rs.at[pi], to_z).start()

    for k in range(4):
        zz = lax.rem(z + k, 4)
        for hh in (hc, lax.rem(hc + 2, 4)):
            p = zz * 4 + hh
            wait_for(tok.at[p], tok_rs.at[p, 0])
    for k in range(4):
        wait_for(land.at[1 - c, k // 2, k % 2], wq_rs.at[1 - c, k // 2, k % 2, 0])

    run_beside(100)
    bias8 = jnp.zeros((8, 576), jnp.float32)
    for xs in range(2):
        for hs in range(4):
            part = []
            window = jnp.zeros((8, 576), jnp.float32)
            for zz in range(4):
                block = land[hs % 2, xs, zz // 2, 2 * (zz % 2) + hs // 2].astype(jnp.float32)
                part.append(block[:24])
                window = window + block[24:]
            start = (xs * 16 + hs * 4) * 24
            bias8 = bias8 + window
            win[xs * 4 + hs] = window
            wqs[start : start + 96, :] = jnp.concatenate(part, axis=0).astype(jnp.bfloat16)
    bias = bias8[0:1, :]

    lane = lax.broadcasted_iota(jnp.int32, (1, 128), 1)
    for p in range(16):
        zz, hs = p // 4, p % 4
        block = land[hs % 2, x, zz // 2, 2 * (zz % 2) + hs // 2].astype(jnp.float32)
        seg = jnp.where(pi == 0, block[28:29, :128], block[29:30, :128])
        ident = jnp.where(seg == NSEG - 1.0, (1000.0 + 128 * p) + lane.astype(f32), seg)
        idrow[:, 128 * p : 128 * p + 128] = jnp.broadcast_to(ident, (8, 128))
        idcol[128 * p : 128 * p + 128, :] = jnp.transpose(jnp.broadcast_to(ident, (128, 128)))

    def project(j, carry):
        zz, yy = lax.div(j, 2), lax.rem(j, 2)
        p = zz * 4 + yy * 2 + c
        rows = pl.ds(pl.multiple_of(j * 128, 128), 128)
        mixed = nn(tok[p], wqs[:, 0:192]) + bias[:, 0:192]
        low = mixed.astype(jnp.bfloat16) * jnp.bfloat16(SCALE)
        for hh in range(3):
            qs[hh, rows, :] = low[:, 64 * hh : 64 * hh + 64]
        both = tok[pl.ds(2 * j, 2)].reshape(256, 768)
        wide = nn(both, wqs[:, 192:576]) + bias[:, 192:576]
        wide = wide.astype(jnp.bfloat16)
        key_rows = pl.ds(pl.multiple_of(j * 256, 256), 256)
        for hh in range(3):
            ks[hh, key_rows, :] = wide[:, 64 * hh : 64 * hh + 64]
            vs[hh, key_rows, :] = wide[:, 192 + 64 * hh : 256 + 64 * hh]
        return carry

    lax.fori_loop(0, 8, project, 0)
    run_beside(101)

    def attend(zz):
        rows = slice(zz * 256, zz * 256 + 256)
        upper = pl.ds(pl.multiple_of((zz * 4 + c) * 128, 128), 128)
        lower = pl.ds(pl.multiple_of((zz * 4 + 2 + c) * 128, 128), 128)
        idq = jnp.concatenate([idcol[upper, :], idcol[lower, :]], axis=0)
        mask = idq[:, 0:1] == idrow[0:1, :]
        def one_head(hh, carry):
            scores = nt(qs[hh, rows, :], ks[hh])
            scores = jnp.where(mask, scores, MASKED)
            top = jnp.max(scores, axis=-1, keepdims=True)
            weights_ = jnp.exp(scores - top)
            total = jnp.sum(weights_, axis=-1, keepdims=True)
            o = nn(weights_.astype(jnp.bfloat16), vs[hh]) / total
            os_[hh, rows, :] = o
            lse = jnp.broadcast_to(top + jnp.log(total), (256, 128))
            lses[hh, :, rows] = jnp.transpose(lse)[0:8, :]
            return carry

        lax.fori_loop(0, 3, one_head, 0)
        out = jnp.concatenate([os_[k, rows, :] for k in range(3)], axis=1).astype(jnp.bfloat16)
        slot = zz // 2
        for yy in range(2):
            j = zz * 2 + yy
            ctx[j] = out[128 * yy : 128 * yy + 128]
            stay = jnp.logical_and(zl == zz % 2, y == yy)

            @pl.when(stay)
            def _():
                pltpu.make_async_copy(ctx.at[j], ctx_in.at[g, slot], ctx_rs.at[g, slot]).start()

            @pl.when(jnp.logical_not(stay))
            def _():
                remote(
                    ctx.at[j],
                    ctx_in.at[g, slot],
                    ctx_ss.at[j],
                    ctx_rs.at[g, slot],
                    (x, yy * 2 + c, 2 * pi + zz % 2),
                ).start()

    for t in range(4):
        attend(t)
        run_beside(102 + t)

    kept = (
        (tok, tok_all),
        (qs, q_all),
        (ks, k_all),
        (vs, v_all),
        (os_, o_all),
        (lses, lse_all),
        (wqs, wq_all),
        (idrow, idrow_all),
        (idcol, idcol_all),
    )
    for k, (src, dst) in enumerate(kept):
        pltpu.make_async_copy(src, dst, out_sem.at[k]).start()
    def arrive(n):
        for xs in range(2):
            for yy in range(2):
                wait_for(at(n, quad(0, 0)), wp_rs.at[n, xs, yy * 2 + 1 - c, 0])

    def flatten(src, dst, cols):
        for k in range(8):
            part = [src[4 * k + q, :, cols].astype(f32) for q in range(4)]
            dst[96 * k : 96 * k + 96, cols] = jnp.concatenate(part, axis=0).astype(bf)

    run_beside(110)
    for s in range(2):
        wait_for(cot_in.at[s], cot_rs.at[s])
        for q in range(4):
            wait_for(ctx_in.at[q, s], ctx_rs.at[q, s])
    arrive(0)
    def row(i):
        at_lane = 128 * (i % 4) if i < 6 else 0
        if i < 6:
            pieces = [win[w, 1 + i // 4 : 2 + i // 4, at_lane : at_lane + 96] for w in range(8)]
        else:
            pieces = []
            for w in (2 * (i - 6), 2 * (i - 6) + 1):
                for k in range(6, 10):
                    at_lane = 128 * (k % 4)
                    pieces.append(win[w, 1 + k // 4 : 2 + k // 4, at_lane : at_lane + 96])
        return jnp.concatenate(pieces, axis=1)

    full_ctx = jnp.concatenate([ctx_in[q].reshape(256, 192) for q in range(4)], axis=1)
    flatten(wout_g, wout_v, slice(0, 768))
    own = jnp.concatenate([tok[zl * 4 + h], tok[(2 + zl) * 4 + h]], axis=0).astype(f32)
    normed_one, inv_one = add_norm(own + nn(full_ctx, wout_v[...]) + row(0))
    hidden = normed_one * row(1) + row(2)
    hidden_low = hidden.astype(bf)
    run_beside(111)
    for k in range(4):
        cols = slice(768 * k, 768 * k + 768)
        if k % 2 == 0:
            arrive(1 + k // 2)
        flatten(wup_g, wup_v, cols)
        raised = nn(hidden_low, wup_v[:, cols]) + row(6 + k)
        normal = 0.5 + 0.5 * lax.erf(raised * (0.5**0.5))
        active[:, cols] = (raised * normal).astype(bf)
        slope[:, cols] = normal + raised * jnp.exp(-0.5 * raised * raised) * (0.5 / math.pi) ** 0.5
    run_beside(112)
    for n in (3, 4):
        arrive(n)
    branch = nn(active[...], wdown_g[...].reshape(3072, 768)) + row(3)
    normed_two, inv_two = add_norm(hidden + branch)
    lo[...] = (normed_two * row(4) + row(5)).astype(bf).reshape(2, 128, 768)
    for k in range(2):

        @pl.when(pi == k)
        def _():
            pltpu.make_async_copy(lo.at[k], lo_out.at[pi], lo_rs.at[pi]).start()

        @pl.when(pi != k)
        def _():
            remote(lo.at[k], lo_out.at[pi], lo_ss, lo_rs.at[pi], to_z).start()

    grad = cot_in[...].reshape(256, 768).astype(f32)
    gvec[4:5, :] = column_sum(grad * normed_two)
    gvec[5:6, :] = column_sum(grad)
    grad_second = norm_pull(grad * row(4), normed_two, inv_two)
    grad_branch = grad_second.astype(bf)
    gvec[3:4, :] = column_sum(grad_branch.astype(f32))

    def halves(n, full, back, rows, part):
        def at(xs, ys, core):
            start = (xs * 16 + (ys * 2 + core) * 4) * (rows // 4)
            return pl.ds(pl.multiple_of(start, rows // 4 * 4), rows)

        for xs in range(2):
            for ys in range(2):
                remote(
                    full.at[at(xs, ys, 1 - c), part],
                    back.at[xs, ys, :, part],
                    c_ss.at[n, xs, ys],
                    c_rs.at[n, xs, ys],
                    to_c,
                ).start()

    def settle(full, back, rows, out, sems, base, parts):
        for xs in range(2):
            for ys in range(2):
                for n, part in parts:
                    wait_for(back.at[xs, ys, :, part], c_rs.at[n, xs, ys])

                def body(t, carry):
                    rel = pl.multiple_of(t * 16, 16)
                    start = (xs * 16 + (ys * 2 + c) * 4) * (rows // 4)
                    mine = full[pl.ds(pl.multiple_of(start + rel, 16), 16), :].astype(f32)
                    there = pl.ds(rel, 16)
                    back[xs, ys, there, :] = (
                        mine + back[xs, ys, there, :].astype(f32)
                    ).astype(bf)
                    return carry

                lax.fori_loop(0, rows // 16, body, 0)
                if out is not None:
                    k = base + xs * 2 + ys
                    pltpu.make_async_copy(back.at[xs, ys], out.at[xs, ys], sems.at[k]).start()

    def spread_down():
        settle(gd, rd, 384, None, o_sem, 0, [(0, pl.ds(0, 768))])
        for k in range(2):
            remote(
                rd.at[k, 1 - y, pl.ds(0, 192)], r2a.at[k], s2_ss.at[k], s2_rs.at[k], to_y
            ).start()
            remote(
                rd.at[1 - x, k, pl.ds(192, 192)], r2b.at[k], s2_ss.at[2 + k], s2_rs.at[2 + k], to_x
            ).start()

    def collect_down():
        for k in range(2):
            wait_for(r2a.at[k], s2_rs.at[k])
            wait_for(r2b.at[k], s2_rs.at[2 + k])

        def body(t, carry):
            k, rel = lax.div(t, 12), pl.multiple_of(lax.rem(t, 12) * 16, 16)
            a, b = pl.ds(rel, 16), pl.ds(pl.multiple_of(rel + 192, 16), 16)
            rd[k, y, a, :] = (rd[k, y, a, :].astype(f32) + r2a[k, a, :].astype(f32)).astype(bf)
            rd[x, k, b, :] = (rd[x, k, b, :].astype(f32) + r2b[k, a, :].astype(f32)).astype(bf)
            return carry

        lax.fori_loop(0, 24, body, 0)
        for k in range(2):
            wait_for(r2a.at[k], s2_ss.at[k])
            wait_for(r2b.at[k], s2_ss.at[2 + k])
        for k in range(4):
            xs, ys = k // 2, k % 2
            pltpu.make_async_copy(rd.at[xs, ys], gdown_h.at[xs, ys], o_sem.at[k]).start()

    for k in range(4):
        rows = slice(768 * k, 768 * k + 768)
        gd[rows, :] = tn(active[:, rows], grad_branch).astype(bf)
    halves(0, gd, rd, 384, pl.ds(0, 768))
    for k in range(4):
        cols = slice(768 * k, 768 * k + 768)
        pulled = (nt(grad_branch, wdown_g[8 * k : 8 * k + 8].reshape(768, 768)) * slope[:, cols]).astype(bf)
        active[:, cols] = pulled
        gvec[6 + k : 7 + k, :] = column_sum(pulled.astype(f32))
        gu[:, cols] = tn(hidden_low, pulled).astype(bf)
        halves(1 + k, gu, ru, 96, pl.ds(768 * k, 768))
        if k == 1:
            spread_down()
    grad_hidden = grad_second + nt(active[...], wup_v[...])
    gvec[1:2, :] = column_sum(grad_hidden * normed_one)
    gvec[2:3, :] = column_sum(grad_hidden)
    grad_first = norm_pull(grad_hidden * row(1), normed_one, inv_one)
    dr1[...] = grad_first.reshape(2, 128, 768)
    grad_attended = grad_first.astype(bf)
    gvec[0:1, :] = column_sum(grad_attended.astype(f32))
    gvec[10:16, :] = jnp.zeros((6, 768), f32)
    go[...] = tn(full_ctx, grad_attended).astype(bf)
    halves(5, go, ro, 96, pl.ds(0, 768))
    back = nt(grad_attended, wout_v[...]).astype(bf)
    for q in range(4):
        dctx[q] = back[:, 192 * q : 192 * q + 192].reshape(2, 128, 192)

    for t in range(2):
        j = (2 * t + zl) * 2 + y
        for k, (dev, target) in enumerate(
            ((to_n, 2 * (1 - zl) + y), (to_y, 2 * zl + 1 - y), (to_d, 2 * (1 - zl) + 1 - y))
        ):
            remote(dctx.at[target, t], dc_all.at[j], dc_ss.at[t, k], dc_rs.at[j], dev).start()
        pltpu.make_async_copy(dctx.at[g, t], dc_all.at[j], dc_rs.at[j]).start()

    settle(gu, ru, 96, gup_h, o_sem, 4, [(1 + k, pl.ds(768 * k, 768)) for k in range(4)])
    settle(go, ro, 96, gout_h, o_sem, 8, [(5, pl.ds(0, 768))])
    collect_down()
    for k in range(2):
        wait_for(lo_out.at[k], lo_rs.at[k])
        for n in range(3):
            wait_for(dctx.at[0, 0], dc_ss.at[k, n])
    wait_for(lo.at[0], lo_ss)
    for k in range(8):
        wait_for(dc_all.at[k], dc_rs.at[k])
    for n in range(6):
        for xs in range(2):
            for ys in range(2):
                gone = gd.at[pl.ds(0, 384)] if n == 0 else gu.at[pl.ds(0, 96), pl.ds(0, 768)]
                wait_for(gone, c_ss.at[n, xs, ys])
    for first, out in ((0, gdown_h), (4, gup_h), (8, gout_h)):
        for k in range(4):
            wait_for(out.at[k // 2, k % 2], o_sem.at[first + k])

    wait_for(cot.at[0], cot_ss)
    for i in range(2):
        for q in range(SUB):
            wait_for(tok.at[0, cuts[q]], tz_ss.at[i, q])
    for k in range(2, 4):

        @pl.when(inner)
        def _():
            for q in range(SUB):
                wait_for(tok.at[0, cuts[q]], tx_ss.at[k, q])

    for k in range(4):
        for q in range(SUB):
            wait_for(tok.at[0, cuts[q]], ty_ss.at[k, q])
    for k in range(8):
        wait_for(tok.at[0], tc_ss.at[k])
    for k in range(3):
        wait_for(wq.at[0], wq_ss.at[k])
    for k in range(3, 10):
        wait_for(land.at[0, 0, 0], wq_ss.at[k])
    for n in range(count):
        for k in range(2):
            wait_for(shard(n), wz_ss.at[n, k])

        @pl.when(inner)
        def _():
            wait_for(two(n), wz_ss.at[n, 2])

    for n, k in sent:
        gone = some(n, k - 3) if k in (3, 4) else at(n, quad(0, 0))
        wait_for(gone, wp_ss.at[n, k])
    for j in range(8):
        zz, yy = j // 2, j % 2
        stay = jnp.logical_and(zl == zz % 2, y == yy)

        @pl.when(jnp.logical_not(stay))
        def _():
            wait_for(ctx.at[j], ctx_ss.at[j])

    for k, (src, dst) in enumerate(kept):
        wait_for(dst, out_sem.at[k])


def forward_call(tokens, cot, segments, wqkv, wout, wup, wdown, rows24, up_bias, qv_bias):
    bf, f32 = jnp.bfloat16, jnp.float32
    sds = jax.ShapeDtypeStruct
    dma = pltpu.SemaphoreType.DMA
    outs = [
        sds((2, 128, 768), f32),
        sds((16, 768), f32),
        sds((2, 128, 768), bf),
        sds((8, 128, 192), bf),
        sds((2, 2, 96, 768), bf),
        sds((2, 2, 96, 3072), bf),
        sds((2, 2, 384, 768), bf),
        sds((16, 128, 768), bf),
        sds((3, 1024, 64), bf),
        sds((3, 2048, 64), bf),
        sds((3, 2048, 64), bf),
        sds((3, 1024, 64), f32),
        sds((3, 8, 1024), f32),
        sds((768, 576), bf),
        sds((8, 2048), f32),
        sds((2048, 128), f32),
    ]
    scratch = [
        pltpu.VMEM((16, 128, 768), bf),
        pltpu.VMEM((2, 2, 2, 4, 32, 576), bf),
        pltpu.VMEM((768, 576), bf),
        pltpu.VMEM((3, 1024, 64), bf),
        pltpu.VMEM((3, 2048, 64), bf),
        pltpu.VMEM((3, 2048, 64), bf),
        pltpu.VMEM((3, 1024, 64), f32),
        pltpu.VMEM((3, 8, 1024), f32),
        pltpu.VMEM((8, 2048), f32),
        pltpu.VMEM((2048, 128), f32),
        pltpu.VMEM((8, 128, 192), bf),
        pltpu.VMEM((32, 24, 768), bf),
        pltpu.VMEM((32, 24, 3072), bf),
        pltpu.VMEM((32, 96, 768), bf),
        pltpu.VMEM((8, 8, 576), f32),
        pltpu.VMEM((4, 2, 128, 192), bf),
        pltpu.VMEM((2, 128, 768), bf),
        pltpu.VMEM((768, 768), bf),
        pltpu.VMEM((768, 3072), bf),
        pltpu.VMEM((256, 3072), bf),
        pltpu.VMEM((256, 3072), f32),
        pltpu.VMEM((768, 768), bf),
        pltpu.VMEM((768, 3072), bf),
        pltpu.VMEM((3072, 768), bf),
        pltpu.VMEM((2, 2, 96, 768), bf),
        pltpu.VMEM((2, 2, 96, 3072), bf),
        pltpu.VMEM((2, 2, 384, 768), bf),
        dma((16, SUB)),
        dma((2, SUB)),
        dma((4, SUB)),
        dma((4, SUB)),
        dma((8,)),
        dma(()),
        dma((2,)),
        dma((10,)),
        dma((2, 2, 2, 4)),
        dma((len(PIECES), 3)),
        dma((len(PIECES), 5)),
        dma((len(PIECES), 8)),
        dma((len(PIECES), 2, 4, 2)),
        dma((8,)),
        dma((4, 2)),
        dma((9,)),
        dma((6, 2, 2)),
        dma((6, 2, 2)),
        dma((12,)),
        pltpu.VMEM((4, 32, 576), bf),
        pltpu.VMEM((2, 128, 768), bf),
        pltpu.VMEM((4, 2, 128, 192), bf),
        pltpu.VMEM((2, 192, 768), bf),
        pltpu.VMEM((2, 192, 768), bf),
        dma(()),
        dma((2,)),
        dma((2, 3)),
        dma((8,)),
        dma((4,)),
        dma((4,)),
    ]
    here, far = pl.BlockSpec(memory_space=pltpu.VMEM), pl.BlockSpec(memory_space=ANY)
    return pl.pallas_call(
        forward_kernel,
        out_shape=outs,
        in_specs=[far, far, here, here, far, far, far, here, here, here],
        out_specs=[here] * 2 + [far] * (len(outs) - 2),
        scratch_shapes=scratch,
        compiler_params=pltpu.CompilerParams(
            collective_id=0, has_side_effects=True, vmem_limit_bytes=VMEM_LIMIT
        ),
        name="forward",
    )(tokens, cot, segments, wqkv, wout, wup, wdown, rows24, up_bias, qv_bias)


RCUT = 3
EARLY_JOBS = 1
JOBS = (
    ("down", (96, 768), 0, 0),
    ("up", (24, 1536), 0, 0),
    ("up", (24, 1536), 0, 1536),
    ("out", (24, 768), 0, 0),
)


def cut_of(n):
    return 2 if n < EARLY_JOBS else RCUT


def add_block(dst, src):
    dst[...] = (dst[...].astype(jnp.float32) + src[...].astype(jnp.float32)).astype(jnp.bfloat16)


def backward_kernel(
    dc_h,
    dr1,
    gout,
    gup,
    gdown,
    gvec,
    tok_h,
    q_h,
    k_h,
    v_h,
    o_h,
    lse_h,
    wq_h,
    idrow_h,
    idcol_h,
    gt_out,
    gout_o,
    gup_o,
    gdown_o,
    gq_o,
    small_o,
    *rest,
):
    count = len(JOBS)
    accs, rest = rest[:count], rest[count:]
    r2as, rest = rest[:count], rest[count:]
    r2bs, rest = rest[:count], rest[count:]
    r1as, rest = rest[:count], rest[count:]
    r1bs, rest = rest[:count], rest[count:]
    rzs, rest = rest[:count], rest[count:]
    (
        tok,
        qs,
        ks,
        vs,
        os_,
        lses,
        wqs,
        idrow,
        idcol,
        dc,
        dks,
        dvs,
        dqs,
        douts,
        kv_send,
        kv_recv,
        dmix,
        dx,
        rx,
        dr,
        gt_send,
        gt_in,
        gq,
        gqc,
        gqx,
        gqz,
        gqin,
        gva,
        gvr,
        qb,
        qbr,
        qb_o,
        in_sem,
        own_ss,
        s2_ss,
        s2_rs,
        s1_ss,
        s1_rs,
        z_ss,
        z_rs,
        kv_ss,
        kv_rs,
        dx_ss,
        dx_rs,
        gt_ss,
        gt_rs,
        gq_ss,
        gq_rs,
        gv_ss,
        gv_rs,
        qb_ss,
        qb_rs,
    ) = rest
    x, y, c, h, z = place()
    zl, pi = lax.rem(z, 2), lax.div(z, 2)
    pz, zc = z + 1 - 2 * zl, lax.rem(z + 2, 4)
    g = 2 * zl + y
    hy = lax.rem(h + 2, 4)
    hc = h + 1 - 2 * c
    to_x, to_y, to_c = (1 - x, h, z), (x, hy, z), (x, hc, z)
    to_n, to_d, to_z = (x, h, pz), (x, hy, pz), (x, h, zc)
    sources = {"out": gout, "up": gup, "down": gdown}
    greet(peers_of(x, h, c, z))

    def loaded():
        return (
            (tok_h, tok),
            (q_h, qs),
            (k_h, ks),
            (v_h, vs),
            (o_h, os_),
            (lse_h, lses),
            (wq_h, wqs),
            (idrow_h, idrow),
            (idcol_h, idcol),
            (dr1, dr),
            (gvec, gva),
            (dc_h, dc),
        )

    for k, (src, dst) in enumerate(loaded()):
        pltpu.make_async_copy(src, dst, in_sem.at[k]).start()
    def part_of(n):
        name, shape, row, col = JOBS[n]
        return sources[name], (pl.ds(row, shape[0]), pl.ds(col, shape[1]))

    def cross(n, source, part):
        remote(
            source.at[(1 - x, y, pl.ds(0, cut_of(n))) + part],
            r1as[n],
            s1_ss.at[n, 0],
            s1_rs.at[n, 0],
            to_x,
        ).start()
        remote(
            source.at[(x, 1 - y, pl.ds(cut_of(n), 4 - cut_of(n))) + part],
            r1bs[n],
            s1_ss.at[n, 1],
            s1_rs.at[n, 1],
            to_y,
        ).start()

    def stage1(n):
        src, part = part_of(n)
        acc = accs[n]
        if n < EARLY_JOBS:
            cross(n, src, part)
            pltpu.make_async_copy(
                src.at[(x, y, pl.ds(0, 4)) + part], acc.at[x, y], own_ss.at[n, 0]
            ).start()
            return
        for k in range(2):
            remote(
                src.at[(k, 1 - y, pl.ds(0, RCUT)) + part],
                r2as[n].at[k],
                s2_ss.at[n, k],
                s2_rs.at[n, k],
                to_y,
            ).start()
            remote(
                src.at[(1 - x, k, pl.ds(RCUT, 4 - RCUT)) + part],
                r2bs[n].at[k],
                s2_ss.at[n, 2 + k],
                s2_rs.at[n, 2 + k],
                to_x,
            ).start()
        for k in range(2):
            pltpu.make_async_copy(
                src.at[(k, y, pl.ds(0, RCUT)) + part], acc.at[k, y, pl.ds(0, RCUT)], own_ss.at[n, k]
            ).start()
            pltpu.make_async_copy(
                src.at[(x, k, pl.ds(RCUT, 4 - RCUT)) + part],
                acc.at[x, k, pl.ds(RCUT, 4 - RCUT)],
                own_ss.at[n, 2 + k],
            ).start()

    for n in range(count):
        stage1(n)
    def stage2(n):
        acc = accs[n]
        if n < EARLY_JOBS:
            wait_for(acc.at[x, y], own_ss.at[n, 0])
            return
        for k in range(2):
            wait_for(r2as[n].at[k], s2_rs.at[n, k])
            wait_for(r2bs[n].at[k], s2_rs.at[n, 2 + k])
            wait_for(r2as[n].at[k], own_ss.at[n, k])
            wait_for(r2bs[n].at[k], own_ss.at[n, 2 + k])
        for k in range(2):
            for q in range(RCUT):
                add_block(acc.at[k, y, q], r2as[n].at[k, q])
            for q in range(4 - RCUT):
                add_block(acc.at[x, k, RCUT + q], r2bs[n].at[k, q])
        cross(n, acc, ())

    def stage3(n):
        acc = accs[n]
        wait_for(r1as[n], s1_rs.at[n, 0])
        wait_for(r1bs[n], s1_rs.at[n, 1])
        for q in range(cut_of(n)):
            add_block(acc.at[x, y, q], r1as[n].at[q])
        for q in range(4 - cut_of(n)):
            add_block(acc.at[x, y, cut_of(n) + q], r1bs[n].at[q])
        for k in range(1, 4):
            zz = lax.rem(z + k, 4)
            remote(
                acc.at[x, y, zz], rzs[n].at[z], z_ss.at[n, k - 1], z_rs.at[n, z], (x, h, zz)
            ).start()

    def stage4(n):
        acc = accs[n]
        name, shape, row, col = JOBS[n]
        total = acc[x, y, z].astype(jnp.float32)
        for k in range(1, 4):
            zz = lax.rem(z + k, 4)
            wait_for(rzs[n].at[zz], z_rs.at[n, zz])
            total = total + rzs[n][zz].astype(jnp.float32)
        out = {"out": gout_o, "up": gup_o, "down": gdown_o}[name]
        out[row : row + shape[0], col : col + shape[1]] = total

    for k, (src, dst) in enumerate(loaded()):
        wait_for(dst, in_sem.at[k])

    def attend(zz):
        rows = slice(zz * 256, zz * 256 + 256)
        first = pl.ds(pl.multiple_of((zz * 4 + c) * 128, 128), 128)
        second = pl.ds(pl.multiple_of((zz * 4 + 2 + c) * 128, 128), 128)
        idq = jnp.concatenate([idrow[0:1, first], idrow[0:1, second]], axis=1)
        mask = idcol[:, 0:1] == idq
        both = jnp.concatenate([dc[2 * zz], dc[2 * zz + 1]], axis=0)
        for hh in range(3):
            douts[hh] = both[:, 64 * hh : 64 * hh + 64]

        def one_head(hh, carry):
            dout = douts[hh]
            q = qs[hh, rows, :]
            delta = jnp.sum(dout.astype(jnp.float32) * os_[hh, rows, :], axis=-1, keepdims=True)
            delta = jnp.transpose(jnp.broadcast_to(delta, (256, 128)))[0:1, :]
            scores = jnp.where(mask, nt(ks[hh], q), MASKED)
            probs = jnp.exp(scores - lses[hh, 0:1, rows])
            dprobs = nt(vs[hh], dout)
            ds = (probs * (dprobs - delta)).astype(jnp.bfloat16)
            dk = nn(ds, q)
            dv = nn(probs.astype(jnp.bfloat16), dout)
            if zz == 0:
                dks[hh] = dk
                dvs[hh] = dv
            else:
                dks[hh] += dk
                dvs[hh] += dv
            dqs[hh, rows, :] = (tn(ds, ks[hh]) * SCALE).astype(jnp.bfloat16)
            return carry

        lax.fori_loop(0, 3, one_head, 0)

    def add_gv(k):
        wait_for(gva, gv_rs.at[k])
        wait_for(gva, gv_ss.at[k])
        gva[...] = gva[...] + gvr[k]

    def gv_stage(n):
        if n < 3:
            if n > 0:
                add_gv(n - 1)
            remote(gva, gvr.at[n], gv_ss.at[n], gv_rs.at[n], (to_c, to_x, to_y)[n]).start()
        elif n == 3:
            add_gv(2)
            for k in range(1, 4):
                remote(
                    gva,
                    gvr.at[3 + z],
                    gv_ss.at[2 + k],
                    gv_rs.at[3 + z],
                    (x, h, lax.rem(z + k, 4)),
                ).start()
        else:
            gv = gva[...]
            for k in range(1, 4):
                zz = lax.rem(z + k, 4)
                wait_for(gvr.at[3 + zz], gv_rs.at[3 + zz])
                gv = gv + gvr[3 + zz]
            gvr[3 + z] = gv

    gv_stage(0)
    stage2(0)
    stage3(0)
    beside = {
        0: ((stage2, 1),),
        1: ((stage2, 2), (stage3, 1)),
        2: ((stage2, 3), (stage3, 2)),
    }
    for t in range(4):
        attend(t)
        gv_stage(t + 1)
        for stage, n in beside.get(t, ()):
            stage(n)

    for j in range(8):
        p = (j // 2) * 4 + (j % 2) * 2 + 1 - c
        rows = pl.ds(pl.multiple_of(p * 128, 128), 128)
        kv_send[j] = jnp.concatenate(
            [dks[hh, rows, :] for hh in range(3)] + [dvs[hh, rows, :] for hh in range(3)], axis=1
        ).astype(jnp.bfloat16)
    remote(kv_send, kv_recv, kv_ss, kv_rs, to_c).start()
    stage3(3)
    wait_for(kv_recv, kv_rs)

    qsum = jnp.zeros((1, 192), jnp.float32)
    vsum = jnp.zeros((1, 192), jnp.float32)
    for j in range(8):
        p = (j // 2) * 4 + (j % 2) * 2 + c
        rows = pl.ds(pl.multiple_of(p * 128, 128), 128)
        wide = jnp.concatenate(
            [dks[hh, rows, :] for hh in range(3)] + [dvs[hh, rows, :] for hh in range(3)], axis=1
        )
        wide = (wide + kv_recv[j].astype(jnp.float32)).astype(jnp.bfloat16)
        part = jnp.concatenate([dqs[hh, 128 * j : 128 * j + 128, :] for hh in range(3)], axis=1)
        dmix[128 * j : 128 * j + 128, :] = jnp.concatenate([part, wide], axis=1)
        qsum = qsum + jnp.sum(part.astype(jnp.float32), axis=0, keepdims=True)
        vsum = vsum + jnp.sum(wide[:, 192:].astype(jnp.float32), axis=0, keepdims=True)
    none = jnp.zeros((1, 192), jnp.float32)
    qb[...] = jnp.broadcast_to(
        jnp.concatenate([qsum, none, vsum, none[:, :64]], axis=1), (8, 640)
    )
    remote(qb, qbr.at[0], qb_ss.at[0], qb_rs.at[0], to_c).start()

    for j in range(8):
        zz, yy = j // 2, j % 2
        dx[j] = nt(dmix[128 * j : 128 * j + 128, :], wqs[...]).astype(jnp.bfloat16)
        slot = zz // 2
        stay = jnp.logical_and(zl == zz % 2, y == yy)

        @pl.when(jnp.logical_not(stay))
        def _():
            remote(
                dx.at[j],
                rx.at[g, slot],
                dx_ss.at[j],
                dx_rs.at[g, slot],
                (x, yy * 2 + c, 2 * pi + zz % 2),
            ).start()

        @pl.when(stay)
        def _():
            pltpu.make_async_copy(dx.at[j], rx.at[g, slot], dx_rs.at[g, slot]).start()

    total = jnp.zeros((768, 576), jnp.float32)
    for zz in range(4):
        left = jnp.concatenate([tok[zz * 4 + c], tok[zz * 4 + 2 + c]], axis=0)
        total = total + tn(left, dmix[256 * zz : 256 * zz + 256, :])
    for xs in range(2):
        for hs in range(4):
            for zz in range(4):
                base = (xs * 16 + hs * 4 + zz) * 24
                gq[hs % 2, xs, zz // 2, 2 * (zz % 2) + hs // 2] = total[base : base + 24].astype(jnp.bfloat16)
    remote(gq.at[1 - c], gqc, gq_ss.at[0], gq_rs.at[0], to_c).start()
    stage4(0)

    def add_qb(k):
        wait_for(qb, qb_rs.at[k])
        wait_for(qb, qb_ss.at[k])
        qb[...] = qb[...] + qbr[k]

    wait_for(gqc, gq_rs.at[0])

    def addq(t, carry):
        i, q = lax.div(t, 4), lax.rem(t, 4)
        xs, pp = lax.div(i, 2), lax.rem(i, 2)
        add_block(gq.at[c, xs, pp, q], gqc.at[xs, pp, q])
        return carry

    lax.fori_loop(0, 16, addq, 0)
    remote(gq.at[c, 1 - x], gqx, gq_ss.at[1], gq_rs.at[1], to_x).start()
    add_qb(0)
    remote(qb, qbr.at[1], qb_ss.at[1], qb_rs.at[1], to_x).start()
    wait_for(gqx, gq_rs.at[1])

    def addx(t, carry):
        pp, q = lax.div(t, 4), lax.rem(t, 4)
        add_block(gq.at[c, x, pp, q], gqx.at[pp, q])
        return carry

    lax.fori_loop(0, 8, addx, 0)
    remote(gq.at[c, x, 1 - pi], gqz, gq_ss.at[2], gq_rs.at[2], to_z).start()
    add_qb(1)
    remote(qb, qbr.at[2], qb_ss.at[2], qb_rs.at[2], to_z).start()
    stage4(1)

    for s in range(2):
        acc = dr[s]
        for q in range(4):
            wait_for(rx.at[q, s], dx_rs.at[q, s])
            acc = acc + rx[q, s].astype(jnp.float32)
        gt_send[s] = acc.astype(jnp.bfloat16)
        zz = 2 * s + zl
        row = pi
        stay = pi == s

        @pl.when(stay)
        def _():
            pltpu.make_async_copy(gt_send.at[s], gt_in.at[row], gt_rs.at[row]).start()

        @pl.when(jnp.logical_not(stay))
        def _():
            remote(gt_send.at[s], gt_in.at[row], gt_ss.at[s], gt_rs.at[row], to_z).start()

    wait_for(gqz, gq_rs.at[2])
    for q in range(4):
        add_block(gq.at[c, x, pi, q], gqz.at[q])
    add_qb(2)
    gqzs = gq.at[c, x, pi]
    for k, (dev, target) in enumerate(
        ((to_n, 2 * (1 - zl) + y), (to_y, 2 * zl + 1 - y), (to_d, 2 * (1 - zl) + 1 - y))
    ):
        remote(gqzs.at[target], gqin.at[g], gq_ss.at[3 + k], gq_rs.at[3 + g], dev).start()
        remote(qb, qb_o.at[g], qb_ss.at[3 + k], qb_rs.at[3 + g], dev).start()
    pltpu.make_async_copy(gqzs.at[g], gqin.at[g], gq_rs.at[3 + g]).start()
    pltpu.make_async_copy(qb, qb_o.at[g], qb_rs.at[3 + g]).start()
    stage4(2)
    for q in range(4):
        wait_for(gqin.at[q], gq_rs.at[3 + q])
        wait_for(qb_o.at[q], qb_rs.at[3 + q])
        gq_o[q] = gqin[q].astype(jnp.float32)
    me = x * 16 + h * 4 + z
    vectors = gvr[3 + z]
    own_rows = pltpu.roll(vectors[0:8, :], lax.rem(768 - 24 * me, 768), 1)[:, 0:128]
    up_row = jnp.zeros((1, 768), jnp.float32)
    for i in range(4):
        up_row = up_row + jnp.where(lax.div(me, 8) == i, vectors[6 + i : 7 + i, :], 0.0)
    up_rows = jnp.broadcast_to(up_row, (8, 768))
    up_rows = pltpu.roll(up_rows, lax.rem(768 - 96 * lax.rem(me, 8), 768), 1)[:, 0:128]
    qv_rows = pltpu.roll(qb_o[h], lax.rem(640 - 48 * z - 384 * x, 640), 1)[:, 0:128]
    line = lax.broadcasted_iota(jnp.int32, (8, 128), 0)
    small_o[...] = jnp.where(line < 6, own_rows, jnp.where(line == 6, up_rows, qv_rows))
    stage4(3)
    for i in range(2):
        wait_for(gt_in.at[i], gt_rs.at[i])
        gt_out[i] = gt_in[i].astype(jnp.float32)

    for s in range(2):

        @pl.when(pi != s)
        def _():
            wait_for(gt_send.at[s], gt_ss.at[s])

    for n in range(count):
        for k in range(2 if n >= EARLY_JOBS else 0):
            wait_for(r1as[n], s2_ss.at[n, k])
            wait_for(r1bs[n], s2_ss.at[n, 2 + k])
        wait_for(r1as[n], s1_ss.at[n, 0])
        wait_for(r1bs[n], s1_ss.at[n, 1])
        for k in range(3):
            wait_for(rzs[n].at[0], z_ss.at[n, k])
    wait_for(kv_send, kv_ss)
    for j in range(8):
        stay = jnp.logical_and(zl == (j // 2) % 2, y == j % 2)

        @pl.when(jnp.logical_not(stay))
        def _():
            wait_for(dx.at[j], dx_ss.at[j])

    wait_for(gqc, gq_ss.at[0])
    wait_for(gqx, gq_ss.at[1])
    wait_for(gqz, gq_ss.at[2])
    for k in range(3):
        wait_for(gqin.at[0], gq_ss.at[3 + k])
        wait_for(qb, qb_ss.at[3 + k])
        wait_for(gva, gv_ss.at[3 + k])


def backward_call(*args):
    bf, f32 = jnp.bfloat16, jnp.float32
    sds = jax.ShapeDtypeStruct
    dma = pltpu.SemaphoreType.DMA
    vm = pltpu.VMEM
    outs = [
        sds((2, 128, 768), f32),
        sds((24, 768), f32),
        sds((24, 3072), f32),
        sds((96, 768), f32),
        sds((4, 24, 576), f32),
        sds((8, 128), f32),
    ]
    shapes = [job[1] for job in JOBS]
    count = len(JOBS)
    scratch = (
        [vm((2, 2, 4) + s, bf) for s in shapes]
        + [vm((2, RCUT) + s, bf) for s in shapes]
        + [vm((2, 4 - RCUT) + s, bf) for s in shapes]
        + [vm((cut_of(n),) + s, bf) for n, s in enumerate(shapes)]
        + [vm((4 - cut_of(n),) + s, bf) for n, s in enumerate(shapes)]
        + [vm((4,) + s, bf) for s in shapes]
        + [
            vm((16, 128, 768), bf),
            vm((3, 1024, 64), bf),
            vm((3, 2048, 64), bf),
            vm((3, 2048, 64), bf),
            vm((3, 1024, 64), f32),
            vm((3, 8, 1024), f32),
            vm((768, 576), bf),
            vm((8, 2048), f32),
            vm((2048, 128), f32),
            vm((8, 128, 192), bf),
            vm((3, 2048, 64), f32),
            vm((3, 2048, 64), f32),
            vm((3, 1024, 64), bf),
            vm((3, 256, 64), bf),
            vm((8, 128, 384), bf),
            vm((8, 128, 384), bf),
            vm((1024, 576), bf),
            vm((8, 128, 768), bf),
            vm((4, 2, 128, 768), bf),
            vm((2, 128, 768), f32),
            vm((2, 128, 768), bf),
            vm((2, 128, 768), bf),
            vm((2, 2, 2, 4, 24, 576), bf),
            vm((2, 2, 4, 24, 576), bf),
            vm((2, 4, 24, 576), bf),
            vm((4, 24, 576), bf),
            vm((4, 24, 576), bf),
            vm((16, 768), f32),
            vm((7, 16, 768), f32),
            vm((8, 640), f32),
            vm((3, 8, 640), f32),
            vm((4, 8, 640), f32),
            dma((12,)),
            dma((count, 4)),
            dma((count, 4)),
            dma((count, 4)),
            dma((count, 2)),
            dma((count, 2)),
            dma((count, 3)),
            dma((count, 4)),
            dma(()),
            dma(()),
            dma((8,)),
            dma((4, 2)),
            dma((2,)),
            dma((2,)),
            dma((6,)),
            dma((7,)),
            dma((6,)),
            dma((7,)),
            dma((6,)),
            dma((7,)),
        ]
    )
    here = pl.BlockSpec(memory_space=pltpu.VMEM)
    far = pl.BlockSpec(memory_space=ANY)
    return pl.pallas_call(
        backward_kernel,
        out_shape=outs,
        in_specs=[far] * 15,
        out_specs=[here] * 6,
        scratch_shapes=scratch,
        compiler_params=pltpu.CompilerParams(
            collective_id=1, has_side_effects=True, vmem_limit_bytes=VMEM_LIMIT
        ),
        name="backward",
    )(*args)


def finish_kernel(lo, gt, gq, gout, gup, gdown, small, lo_o, gt_o, gqkv_o, gout_o, gup_o, gdown_o, *vectors):
    for src, dst in ((lo, lo_o), (gt, gt_o), (gout, gout_o), (gup, gup_o), (gdown, gdown_o)):
        dst[...] = src[...]
    for part in range(3):
        gqkv_o[:, 768 * part : 768 * part + 768] = jnp.concatenate(
            [gq[q, :, 192 * part : 192 * part + 192] for q in range(4)], axis=1
        )
    for k, dst in enumerate(vectors):
        dst[...] = small[k : k + 1, : dst.shape[1]]


def finish_call(lo, gt, gq, gout, gup, gdown, small):
    f32 = jnp.float32
    here = pl.BlockSpec(memory_space=pltpu.VMEM)
    like = lambda a: jax.ShapeDtypeStruct(a.shape, a.dtype)
    wide = jax.ShapeDtypeStruct((24, 2304), f32)
    outs = [like(lo), like(gt), wide, like(gout), like(gup), like(gdown)]
    outs += [jax.ShapeDtypeStruct((1, width), f32) for width in (24,) * 6 + (96, 48)]
    return pl.pallas_call(
        finish_kernel,
        out_shape=outs,
        in_specs=[here] * 7,
        out_specs=[here] * len(outs),
        compiler_params=pltpu.CompilerParams(vmem_limit_bytes=VMEM_LIMIT),
        name="finish",
    )(lo, gt, gq, gout, gup, gdown, small)


def slab_body(
    tokens,
    segments,
    qkv_weight,
    qv_bias,
    out_weight,
    out_bias,
    attn_gain,
    attn_shift,
    up_weight,
    up_bias,
    down_weight,
    down_bias,
    ffn_gain,
    ffn_shift,
    cotangent,
):
    rows24 = jnp.stack([out_bias, attn_gain, attn_shift, down_bias, ffn_gain, ffn_shift])
    (
        grad_first,
        gvec,
        lo_out,
        dc_all,
        grad_out,
        grad_up,
        grad_down,
        tok_all,
        q_all,
        k_all,
        v_all,
        o_all,
        lse_all,
        wq_all,
        idrow_all,
        idcol_all,
    ) = forward_call(
        tokens,
        cotangent,
        segments,
        qkv_weight,
        out_weight,
        up_weight,
        down_weight,
        rows24,
        up_bias.reshape(1, 96),
        qv_bias.reshape(1, 48),
    )
    gt_out, gout_o, gup_o, gdown_o, gq_o, small = backward_call(
        dc_all,
        grad_first,
        grad_out.reshape(2, 2, 4, 24, 768),
        grad_up.reshape(2, 2, 4, 24, 3072),
        grad_down.reshape(2, 2, 4, 96, 768),
        gvec,
        tok_all,
        q_all,
        k_all,
        v_all,
        o_all,
        lse_all,
        wq_all,
        idrow_all,
        idcol_all,
    )
    lo_out, gt_out, gqkv, gout_o, gup_o, gdown_o, *vectors = finish_call(
        lo_out, gt_out, gq_o, gout_o, gup_o, gdown_o, small
    )
    rows = [vector.reshape(vector.shape[1]) for vector in vectors]
    return (
        lo_out,
        gt_out,
        gqkv,
        rows[7],
        gout_o,
        rows[0],
        rows[1],
        rows[2],
        gup_o,
        rows[6],
        gdown_o,
        rows[3],
        rows[4],
        rows[5],
    )


def solution(mesh):
    sizes = tuple(mesh.shape[name] for name in ("dp", "head", "blk"))
    body = slab_body if sizes == (2, 4, 4) else general_body
    placed = (
        P("dp", ("blk", "head"), None),
        P("dp", ("blk", "head")),
        P(("dp", "head", "blk"), None),
        P(("dp", "head", "blk")),
        P(("dp", "head", "blk"), None),
        P(("dp", "head", "blk")),
        P(("dp", "head", "blk")),
        P(("dp", "head", "blk")),
        P(("dp", "head", "blk"), None),
        P(("dp", "head", "blk")),
        P(("dp", "head", "blk"), None),
        P(("dp", "head", "blk")),
        P(("dp", "head", "blk")),
        P(("dp", "head", "blk")),
        P("dp", ("blk", "head"), None),
    )
    return jax.shard_map(
        body,
        mesh=mesh,
        in_specs=placed,
        out_specs=(
            P("dp", ("blk", "head"), None),
            P("dp", ("blk", "head"), None),
            P(("dp", "head", "blk"), None),
            P(("dp", "head", "blk")),
            P(("dp", "head", "blk"), None),
            P(("dp", "head", "blk")),
            P(("dp", "head", "blk")),
            P(("dp", "head", "blk")),
            P(("dp", "head", "blk"), None),
            P(("dp", "head", "blk")),
            P(("dp", "head", "blk"), None),
            P(("dp", "head", "blk")),
            P(("dp", "head", "blk")),
            P(("dp", "head", "blk")),
        ),
        check_vma=False,
    )
```
